512 devices in a mesh: pairs: 64 (over x, z), tensor: 8 (over y, core).
Axes of the slice: x: 4, y: 4, z: 16, core: 2. Of those that a mesh axis runs over, the one named last changes fastest.
Arguments:
- tokens: bfloat16 [8192, 4096], P('pairs', 'tensor'), may hold values from -6 to 6
- norm_gain: bfloat16 [4096], replicated, may hold values from 0.099609375 to 1.8984375
- wq: bfloat16 [4096, 4096], P('pairs', 'tensor'), may hold values from -0.09375 to 0.09375
- wk: bfloat16 [4096, 1024], P('pairs', 'tensor'), may hold values from -0.09375 to 0.09375
- wv: bfloat16 [4096, 1024], P('pairs', 'tensor'), may hold values from -0.09375 to 0.09375
- doc_cache: bfloat16 [128, 128, 2048], P('pairs', None, 'tensor'), may hold values from -140 to 140
- doc_lists: int32 [64, 16], replicated, may hold values from 0 to 127, as said below
- doc_place: int32 [128], replicated, may hold values from 0 to 127, as said below
- block_use: int32 [128, 16], P('pairs'), may hold values 0 or 1
Outputs:
- attended: bfloat16 [8192, 4096], P('pairs', 'tensor')
The draws below stay inside these ranges and needn't reach their ends.
Inputs may be any that keep to these rules, and one draw needn't show every extreme that they name: `doc_lists`: in each row the documents are distinct; a group takes exactly 2 documents from each owner (storage places k*2 to k*2 + 1) that it names, and none from the others. `doc_place`: A permutation of the documents.
All inputs are finite; a program needn't handle non-finite values. No bound on the sum of `block_use` on one device may be relied on, other than what follows from the above.
Results may differ from the reference program's by a relative error of at most 0.0085.
The reference program's roundings to bfloat16 on the way count: a program that leaves them out, or rounds other values in their place, can miss the bound.
Values may be sent and summed in bfloat16 or wider, within the bound.
No kernel may reach another device: no remote copies, remote signals or barrier semaphores. Data moves between devices by JAX's collectives and lax.ppermute only.
A program may use at most 64 MiB of HBM per device.

```python
import jax
import jax.numpy as jnp
from jax import lax

D = 4096
HEADS = 32
KV_HEADS = 8
HEAD_DIM = 128
PAIRS_DEV = 1
SEQ = 128
QBLK = 64
BLK = 128
PICKS_PAIR = 16
PICKS = 16
CAP = 2
DOC_DEV = 2
DOCS = 128
TOKENS = 8192
N_PAIRS = 64


def shared_tables(key):
    place = jax.random.permutation(jax.random.fold_in(key, 11), DOCS).astype(jnp.int32)
    at_place = jnp.argsort(place).astype(jnp.int32)
    owners_needed = PICKS // CAP
    base = jax.random.randint(jax.random.fold_in(key, 12), (N_PAIRS, N_PAIRS), 0, 4096)
    favored = (jax.random.randint(jax.random.fold_in(key, 13), (N_PAIRS,), 0, 4) == 0).astype(jnp.int32)
    score = (base + favored[None, :] * 4096) * N_PAIRS + jnp.arange(N_PAIRS, dtype=jnp.int32)[None, :]
    unused, owners = lax.top_k(score, owners_needed)
    places = owners.astype(jnp.int32)[:, :, None] * DOC_DEV + jnp.arange(CAP, dtype=jnp.int32)[None, None, :]
    places = places.reshape(N_PAIRS, PICKS)
    mixing = jax.random.randint(jax.random.fold_in(key, 14), (N_PAIRS, PICKS), 0, 65536)
    order = jnp.argsort(mixing * PICKS + jnp.arange(PICKS, dtype=jnp.int32)[None, :], axis=1).astype(jnp.int32)
    places = jnp.take_along_axis(places, order, axis=1)
    lists = at_place[places]
    return (lists.astype(jnp.int32), place)


def draw_doc_lists(key, part):
    lists, place = shared_tables(key)
    return lists


def draw_doc_place(key, part):
    lists, place = shared_tables(key)
    return place


def draw_doc_cache(key, part):
    key = jax.random.fold_in(key, 3)
    shape = (DOCS, BLK, KV_HEADS, 2, HEAD_DIM)
    values = jnp.clip(jax.random.normal(jax.random.fold_in(key, 7), shape, jnp.float32), -4.0, 4.0)
    return values.reshape(DOCS, BLK, KV_HEADS * 2 * HEAD_DIM).astype(jnp.bfloat16)


def set_ends(values, stream_key, low, largest):
    extent = values.shape
    spot = [jax.random.randint(jax.random.fold_in(stream_key, axis), (), 0, extent[axis]) for axis in range(len(extent))]
    values = values.at[tuple(spot)].set(low)
    longest = extent.index(max(extent))
    spot[longest] = (spot[longest] + 1) % extent[longest]
    return values.at[tuple(spot)].set(largest)


def steps_of(rng, extent, split, smallest, largest):
    def one(axis_at, blocks):
        heights = jax.random.uniform(jax.random.fold_in(jax.random.fold_in(rng, 6), axis_at), (blocks,), jnp.float32, smallest / len(split), largest / len(split))
        return jnp.repeat(jnp.exp(heights), extent[axis_at] // blocks).reshape((-1,) + (1,) * (len(extent) - axis_at - 1))

    level = one(*split[0])
    for cut in split[1:]:
        level = level * one(*cut)
    return level


def noise(rng, shape, width, reach, shards=(), kind=jnp.bfloat16):
    factor_of = steps_of(rng, shape, shards, -0.22, 0.18) if shards else 1.0
    drawn = jax.random.normal(rng, shape, jnp.float32) * width * factor_of
    return jnp.minimum(jnp.maximum(drawn, -reach), reach).astype(kind)


def setup_inputs(seed: int = 0) -> dict:
    streams_of = jax.random.split(jax.random.key(seed), 10)
    tokens = noise(streams_of[0], (TOKENS, D), 1.0, 6.0, ((0, 64), (1, 8)))
    norm_gain = jnp.clip(1.0 + 0.18 * jax.random.normal(streams_of[1], (D,), jnp.float32), 0.099609375, 1.8984375).astype(jnp.bfloat16)
    wq = noise(streams_of[2], (D, HEADS * HEAD_DIM), D ** -0.5, 0.09375, ((0, 64), (1, 8)))
    wk = noise(streams_of[3], (D, KV_HEADS * HEAD_DIM), D ** -0.5, 0.09375, ((0, 64), (1, 8)))
    wv = noise(streams_of[4], (D, KV_HEADS * HEAD_DIM), D ** -0.5, 0.09375, ((0, 64), (1, 8)))
    doc_cache = draw_doc_cache(jax.random.fold_in(streams_of[9], 71), 0)
    doc_lists = draw_doc_lists(jax.random.fold_in(streams_of[9], 71), 0)
    doc_place = draw_doc_place(jax.random.fold_in(streams_of[9], 71), 0)
    block_use = set_ends((jax.random.randint(streams_of[8], (TOKENS // QBLK, PICKS_PAIR), 0, 4) < 3).astype(jnp.int32), jax.random.fold_in(streams_of[8], 1), 0, 1)
    return dict(tokens=tokens, norm_gain=norm_gain, wq=wq, wk=wk, wv=wv, doc_cache=doc_cache, doc_lists=doc_lists, doc_place=doc_place, block_use=block_use)


def attend(query, key_own, value_own, key_doc, value_doc, use):
    head_size = query.shape[-1]
    scale = head_size ** (-0.5)
    qf = query.astype(jnp.float32)
    s_doc = jnp.einsum('psvgd,pkvd->pvgsk', qf, key_doc.astype(jnp.float32)) * scale
    s_own = jnp.einsum('psvgd,ptvd->pvgst', qf, key_own.astype(jnp.float32)) * scale
    keep_doc = jnp.repeat(jnp.repeat(use, QBLK, axis=1), BLK, axis=2) > 0
    causal = jnp.arange(SEQ)[:, None] >= jnp.arange(SEQ)[None, :]
    s_doc = jnp.where(keep_doc[:, None, None], s_doc, -1e+30)
    s_own = jnp.where(causal[None, None, None], s_own, -1e+30)
    scores = jnp.concatenate([s_doc, s_own], axis=-1)
    top = lax.optimization_barrier(jnp.max(scores, axis=-1, keepdims=True))
    expo = jnp.exp(scores - top)
    probs = (expo / lax.optimization_barrier(jnp.sum(expo, axis=-1, keepdims=True))).astype(jnp.bfloat16)
    values = jnp.concatenate([value_doc, value_own], axis=1)
    out = jnp.einsum('pvgsk,pkvd->psvgd', probs.astype(jnp.float32), values.astype(jnp.float32))
    return out.astype(jnp.bfloat16)

def reference(tokens, norm_gain, wq, wk, wv, doc_cache, doc_lists, doc_place, block_use):
    feats = tokens.astype(jnp.float32)
    power = lax.optimization_barrier(jnp.mean(feats * feats, axis=-1, keepdims=True))
    normed = (feats * lax.rsqrt(power + 1e-05) * norm_gain.astype(jnp.float32)).astype(jnp.bfloat16)
    query = jnp.dot(normed, wq, preferred_element_type=jnp.float32).astype(jnp.bfloat16)
    key_own = jnp.dot(normed, wk, preferred_element_type=jnp.float32).astype(jnp.bfloat16)
    value_own = jnp.dot(normed, wv, preferred_element_type=jnp.float32).astype(jnp.bfloat16)
    places_all = doc_place[doc_lists]
    group_size = KV_HEADS
    ratio = HEADS // KV_HEADS
    rows = PAIRS_DEV * SEQ
    qblocks = PAIRS_DEV * (SEQ // QBLK)

    def one_group(group):
        start = (group * rows).astype(jnp.int32)
        q_rows = lax.dynamic_slice_in_dim(query, start, rows, 0).reshape(PAIRS_DEV, SEQ, group_size, ratio, HEAD_DIM)
        k_rows = lax.dynamic_slice_in_dim(key_own, start, rows, 0).reshape(PAIRS_DEV, SEQ, group_size, HEAD_DIM)
        v_rows = lax.dynamic_slice_in_dim(value_own, start, rows, 0).reshape(PAIRS_DEV, SEQ, group_size, HEAD_DIM)
        places = lax.dynamic_index_in_dim(places_all, group, 0, keepdims=False)
        blocks = doc_cache[places].reshape(PAIRS_DEV, PICKS_PAIR * BLK, group_size, 2, HEAD_DIM)
        use = lax.dynamic_slice_in_dim(block_use, (group * qblocks).astype(jnp.int32), qblocks, 0)
        use = use.reshape(PAIRS_DEV, SEQ // QBLK, PICKS_PAIR)
        out = attend(q_rows, k_rows, v_rows, blocks[:, :, :, 0], blocks[:, :, :, 1], use)
        return out.reshape(rows, HEADS * HEAD_DIM)
    result = lax.map(one_group, jnp.arange(N_PAIRS, dtype=jnp.int32))
    return result.reshape(TOKENS, HEADS * HEAD_DIM)
```

```python
import jax
import jax.numpy as jnp
from jax import lax
from jax.experimental import pallas as pl
from jax.experimental.pallas import tpu as pltpu
from jax.sharding import Mesh
from jax.sharding import PartitionSpec as P

F32 = jnp.float32
BF16 = jnp.bfloat16
HEAD = 128
HALF = 64
SEQ = 128
RATIO = 4
NX = 4
NZ = 16
PICKS = 16
ROWS = NX * SEQ
COLS = RATIO * SEQ
SCALE = HEAD ** (-0.5)
LOW = -1e30
UNITS = 128

VMEM = pl.BlockSpec(memory_space=pltpu.VMEM)
SMEM = pl.BlockSpec(memory_space=pltpu.SMEM)
PARAMS = pltpu.CompilerParams(vmem_limit_bytes=40 * 1024 * 1024)


def call(kernel, outs, args, specs, out_specs=None, scratch=(), flops=0, moved=0):
    return pl.pallas_call(
        kernel,
        out_shape=outs,
        in_specs=specs,
        out_specs=VMEM if out_specs is None else out_specs,
        scratch_shapes=list(scratch),
        compiler_params=PARAMS,
        cost_estimate=pl.CostEstimate(flops=flops, bytes_accessed=moved, transcendentals=0),
    )(*args)


def side_by_side(left, right, left_at, right_at):
    left, right = left.astype(F32), right.astype(F32)
    lane = lax.broadcasted_iota(jnp.int32, left.shape, 1)
    left = pltpu.roll(left, HALF, 1) if left_at else left
    right = right if right_at else pltpu.roll(right, HALF, 1)
    return jnp.where(lane < HALF, left, right).astype(BF16)


def pack_kernel(wq, wk, wv, out):
    for part in range(NX):
        src = wk if part < 2 else wv
        at = HALF * (part % 2)
        packed = side_by_side(src[0:32, :], src[32:64, :], at, at)
        for copy in range(4):
            out[part, copy, 0:64, :] = wq[:, part * HEAD : (part + 1) * HEAD]
            out[part, copy, 64:96, :] = packed


def norm_kernel(where, mine, other, gain, out):
    core = where[3]
    for row in range(NX):
        rows = pl.ds(row * SEQ, SEQ)
        total = jnp.zeros((SEQ, HEAD), F32)
        for src in (mine, other):
            for y in range(4):
                for c in range(4):
                    feats = src[row, y, :, c * HEAD : (c + 1) * HEAD].astype(F32)
                    total = total + feats * feats
        power = jnp.sum(total, axis=-1, keepdims=True) * (1.0 / 4096.0)
        factor = lax.rsqrt(power + 1e-05)
        for src, flip in ((mine, 0), (other, 1)):
            side = core if flip == 0 else 1 - core
            for y in range(4):
                slot = 2 * y + side
                feats = src[row, y].astype(F32)
                out[slot, rows, :] = (feats * factor * gain[slot]).astype(BF16)


def route_kernel(where, lists, place, use, units, table):
    x, z = where[0], where[1]

    def clear(i, carry):
        table[i] = 0
        return carry

    lax.fori_loop(0, NX * NZ, clear, 0)

    def fill(i, carry):
        row, pick = i // PICKS, i % PICKS
        at = place[lists[row * NZ + z, pick]]
        owner, local = at // 2, at % 2
        bits = use[row * 2, pick] + 2 * use[row * 2 + 1, pick]
        entry = row * NZ + owner % NZ
        mine = jnp.where(owner // NZ == x, 1, 0)
        table[entry] = table[entry] + mine * bits * jnp.where(local == 1, 4, 1)
        return carry

    lax.fori_loop(0, NX * PICKS, fill, 0)

    def compact(i, count):
        bits = table[i]
        units[count + 1] = i * 16 + bits
        return count + jnp.where(bits > 0, 1, 0)

    units[0] = lax.fori_loop(0, NX * NZ, compact, 0)


def project_kernel(where, normed, near, ahead, far_a, far_b, behind, send, weights):
    lane_part = where[2]
    for step in range(4):
        row = lax.rem(lane_part + step, 4) * HALF
        for b in range(16):
            if step == 0:
                block = near[b]
            elif step == 1:
                block = ahead[b]
            elif step == 3:
                block = behind[b]
            else:
                block = far_a[b] if b < 8 else far_b[b - 8]
            base = pl.multiple_of(b * 256 + row, HALF)
            packed = block[64:96, :]
            weights[pl.ds(base, 64), 0:HEAD] = block[0:64, :]
            weights[pl.ds(base, 32), HEAD : 2 * HEAD] = packed
            weights[pl.ds(pl.multiple_of(base + 32, 32), 32), HEAD : 2 * HEAD] = pltpu.roll(
                packed.astype(F32), HALF, 1
            ).astype(BF16)
    total = jnp.zeros((ROWS, 2 * HEAD), F32)
    for slot in range(8):
        total = total + jnp.dot(
            normed[slot], weights[slot * 512 : (slot + 1) * 512, :], preferred_element_type=F32
        )
    query = total[:, 0:HEAD].astype(BF16)
    for dest in range(NX):
        own = total[dest * SEQ : (dest + 1) * SEQ, HEAD : 2 * HEAD]
        send[dest, 0:ROWS, :] = query
        send[dest, ROWS : ROWS + HALF, :] = side_by_side(own[0:HALF], own[HALF:SEQ], 0, 0)


def own_part(got, first):
    a, b = got[first, ROWS : ROWS + HALF, :], got[first + 1, ROWS : ROWS + HALF, :]
    return jnp.concatenate([side_by_side(a, b, 0, 0), side_by_side(a, b, HALF, HALF)], axis=0)


def queries(got, group):
    rows = pl.ds(pl.multiple_of(group * SEQ, SEQ), SEQ)
    return jnp.concatenate([got[head, rows, :] for head in range(RATIO)], axis=0)


def scores_of(keys, query):
    return (
        lax.dot_general(keys, query, (((1,), (1,)), ((), ())), preferred_element_type=F32) * SCALE
    )


def own_scores(got, group):
    scores = scores_of(own_part(got, 0), queries(got, group))
    key_at = lax.broadcasted_iota(jnp.int32, (SEQ, COLS), 0)
    row_at = lax.broadcasted_iota(jnp.int32, (SEQ, COLS), 1) % SEQ
    return jnp.where(row_at >= key_at, scores, LOW)


def unit_scores(code, got, docs):
    entry, bits = code // 16, code % 16
    group, owner = entry // NZ, entry % NZ
    keys = docs[pl.ds(owner * 2, 2), :, 0:HEAD].reshape(2 * SEQ, HEAD)
    scores = scores_of(keys, queries(got, group))
    second = (lax.broadcasted_iota(jnp.int32, (1, COLS), 1) % SEQ) // HALF
    kept = []
    for local in range(2):
        use_a, use_b = (bits // (4**local)) % 2, (bits // (2 * 4**local)) % 2
        keep = jnp.where(second == 0, use_a, use_b)
        kept.append(jnp.where(keep > 0, scores[local * SEQ : (local + 1) * SEQ], LOW))
    return group, owner, jnp.concatenate(kept, axis=0)


def stats_kernel(where, units, got, docs, send, stats):
    x = where[0]
    scores = own_scores(got, x)
    top = jnp.max(scores, axis=0, keepdims=True)
    stats[0:4, :] = jnp.full((4, COLS), LOW, F32)
    stats[4:8, :] = jnp.zeros((4, COLS), F32)
    stats[pl.ds(x, 1), :] = top
    stats[pl.ds(x + 4, 1), :] = jnp.sum(jnp.exp(scores - top), axis=0, keepdims=True)

    def unit(i, carry):
        group, owner, scores = unit_scores(units[i + 1], got, docs)
        before = stats[pl.ds(group, 1), :]
        top = jnp.maximum(before, jnp.max(scores, axis=0, keepdims=True))
        part = jnp.sum(jnp.exp(scores - top), axis=0, keepdims=True)
        stats[pl.ds(group, 1), :] = top
        stats[pl.ds(group + 4, 1), :] = stats[pl.ds(group + 4, 1), :] * jnp.exp(before - top) + part
        return carry

    lax.fori_loop(0, units[0], unit, 0)
    for dest in range(NX):
        send[dest] = stats[...]


def values_kernel(where, units, got, docs, all_stats, send, total):
    x = where[0]
    tops = [all_stats[src, 0:4, :] for src in range(NX)]
    top = jnp.maximum(jnp.maximum(tops[0], tops[1]), jnp.maximum(tops[2], tops[3]))
    sums = jnp.zeros((4, COLS), F32)
    for src in range(NX):
        sums = sums + all_stats[src, 4:8, :] * jnp.exp(tops[src] - top)
    total[0:4, :] = top
    total[4:8, :] = sums
    send[...] = jnp.zeros(send.shape, F32)

    def add(group, scores, values):
        expo = jnp.exp(scores - total[pl.ds(group, 1), :])
        probs = (expo / total[pl.ds(group + 4, 1), :]).astype(BF16)
        out = lax.dot_general(values, probs, (((0,), (0,)), ((), ())), preferred_element_type=F32)
        send[pl.ds(group, 1)] = send[pl.ds(group, 1)] + out[None]

    add(x, own_scores(got, x), own_part(got, 2))

    def unit(i, carry):
        group, owner, scores = unit_scores(units[i + 1], got, docs)
        values = docs[pl.ds(owner * 2, 2), :, HEAD : 2 * HEAD].reshape(2 * SEQ, HEAD)
        add(group, scores, values)
        return carry

    lax.fori_loop(0, units[0], unit, 0)


def finish_kernel(got, out):
    for head in range(RATIO):
        cols = slice(head * SEQ, (head + 1) * SEQ)
        total = (got[0, :, cols] + got[1, :, cols]) + (got[2, :, cols] + got[3, :, cols])
        out[:, cols] = total.T.astype(BF16)


def exchange(array, axes):
    return lax.all_to_all(array, axes, 0, 0, tiled=True)


def spread(array, axes, count):
    return exchange(jnp.broadcast_to(array[None], (count, *array.shape)), axes)


def shards(tokens, norm_gain, wq, wk, wv, doc_cache, doc_lists, doc_place, block_use):
    shape = jax.ShapeDtypeStruct
    z_axes = ("zh", "zl")
    docs = lax.all_gather(doc_cache, z_axes, axis=0, tiled=True)
    x, zh, zl = lax.axis_index("x"), lax.axis_index("zh"), lax.axis_index("zl")
    where = jnp.stack([x, zh * 4 + zl, zl, lax.axis_index("core")]).astype(jnp.int32)

    parts = call(pack_kernel, shape((4, 4, 96, HEAD), BF16), (wq, wk, wv), [VMEM] * 3)
    near = exchange(parts.reshape(16, 96, HEAD), ("x", "zh"))

    by_y = spread(tokens, "y", 4)
    mine = spread(by_y, "x", NX)
    other = lax.ppermute(mine, "core", [(0, 1), (1, 0)])
    gain = norm_gain.astype(F32).reshape(8, 1, 512)
    normed = call(
        norm_kernel,
        shape((8, ROWS, 512), BF16),
        (where, mine, other, gain),
        [SMEM, VMEM, VMEM, VMEM],
        flops=ROWS * 4096 * 8,
        moved=8 << 20,
    )
    use = spread(block_use, "x", NX).reshape(8, PICKS)
    units = call(
        route_kernel,
        shape((UNITS,), jnp.int32),
        (where, doc_lists, doc_place, use),
        [SMEM] * 4,
        out_specs=SMEM,
        scratch=[pltpu.SMEM((NX * NZ,), jnp.int32)],
    )

    def from_z(array, step):
        return lax.ppermute(array, z_axes, [((i + step) % NZ, i) for i in range(NZ)])

    ahead = from_z(near, 1)
    behind = from_z(near, -1)
    far_a = from_z(near[0:8], 2)
    far_b = from_z(near[8:16], -2)
    send = call(
        project_kernel,
        shape((NX, ROWS + HALF, HEAD), BF16),
        (where, normed, near, ahead, far_a, far_b, behind),
        [SMEM] + [VMEM] * 6,
        scratch=[pltpu.VMEM((4096, 2 * HEAD), BF16)],
        flops=2 * ROWS * 4096 * 256,
        moved=8 << 20,
    )
    got = exchange(send, "x")
    stats = call(
        stats_kernel,
        shape((NX, 8, COLS), F32),
        (where, units, got, docs),
        [SMEM, SMEM, VMEM, VMEM],
        scratch=[pltpu.VMEM((8, COLS), F32)],
    )
    all_stats = exchange(stats, "x")
    partial = call(
        values_kernel,
        shape((NX, HEAD, COLS), F32),
        (where, units, got, docs, all_stats),
        [SMEM, SMEM, VMEM, VMEM, VMEM],
        scratch=[pltpu.VMEM((8, COLS), F32)],
    )
    returned = exchange(partial, "x")
    return call(finish_kernel, shape((SEQ, COLS), BF16), (returned,), [VMEM])


def solution(mesh):
    fine = Mesh(mesh.devices.reshape(4, 4, 4, 4, 2), ("x", "zh", "zl", "y", "core"))
    pairs, tensor = ("x", "zh", "zl"), ("y", "core")
    placed = (
        P(pairs, tensor),
        P(),
        P(pairs, tensor),
        P(pairs, tensor),
        P(pairs, tensor),
        P(pairs, None, tensor),
        P(),
        P(),
        P(pairs, None),
    )
    return jax.shard_map(
        shards, mesh=fine, in_specs=placed, out_specs=P(pairs, tensor), check_vma=False
    )
```

```python
import jax
import jax.numpy as jnp
from jax import lax
from jax.experimental import pallas as pl
from jax.experimental.pallas import tpu as pltpu
from jax.sharding import Mesh
from jax.sharding import PartitionSpec as P

F32 = jnp.float32
BF16 = jnp.bfloat16
HEAD = 128
HALF = 64
SEQ = 128
RATIO = 4
NX = 4
NZ = 16
PICKS = 16
ROWS = NX * SEQ
COLS = RATIO * SEQ
SCALE = HEAD ** (-0.5)
LOW = -1e30
UNITS = 128

VMEM = pl.BlockSpec(memory_space=pltpu.VMEM)
SMEM = pl.BlockSpec(memory_space=pltpu.SMEM)
PARAMS = pltpu.CompilerParams(vmem_limit_bytes=24 * 1024 * 1024)


def call(kernel, outs, args, specs, out_specs=None, scratch=(), flops=0, moved=0):
    return pl.pallas_call(
        kernel,
        out_shape=outs,
        in_specs=specs,
        out_specs=VMEM if out_specs is None else out_specs,
        scratch_shapes=list(scratch),
        compiler_params=PARAMS,
        cost_estimate=pl.CostEstimate(flops=flops, bytes_accessed=moved, transcendentals=0),
    )(*args)


def side_by_side(left, right, left_at, right_at):
    left, right = left.astype(F32), right.astype(F32)
    lane = lax.broadcasted_iota(jnp.int32, left.shape, 1)
    left = pltpu.roll(left, HALF, 1) if left_at else left
    right = right if right_at else pltpu.roll(right, HALF, 1)
    return jnp.where(lane < HALF, left, right).astype(BF16)


def pack_kernel(wq, wk, wv, out):
    for part in range(NX):
        src = wk if part < 2 else wv
        at = HALF * (part % 2)
        packed = side_by_side(src[0:32, :], src[32:64, :], at, at)
        for copy in range(4):
            out[part, copy, 0:64, :] = wq[:, part * HEAD : (part + 1) * HEAD]
            out[part, copy, 64:96, :] = packed


def norm_kernel(where, mine, other, gain, out):
    core = where[3]
    for row in range(NX):
        rows = pl.ds(row * SEQ, SEQ)
        total = jnp.zeros((SEQ, HEAD), F32)
        for src in (mine, other):
            for y in range(4):
                for c in range(4):
                    feats = src[row, y, :, c * HEAD : (c + 1) * HEAD].astype(F32)
                    total = total + feats * feats
        power = jnp.sum(total, axis=-1, keepdims=True) * (1.0 / 4096.0)
        factor = lax.rsqrt(power + 1e-05)
        for src, flip in ((mine, 0), (other, 1)):
            side = core if flip == 0 else 1 - core
            for y in range(4):
                slot = 2 * lax.rem(where[4] + y, 4) + side
                feats = src[row, y].astype(F32)
                out[slot, rows, :] = (feats * factor * gain[slot]).astype(BF16)


def route_kernel(where, lists, place, use, units, table):
    x, z = where[0], where[1]

    def clear(i, carry):
        table[i] = 0
        return carry

    lax.fori_loop(0, NX * NZ, clear, 0)

    def fill(i, carry):
        row, pick = i // PICKS, i % PICKS
        at = place[lists[row * NZ + z, pick]]
        owner, local = at // 2, at % 2
        bits = use[row * 2, pick] + 2 * use[row * 2 + 1, pick]
        entry = row * NZ + owner % NZ
        mine = jnp.where(owner // NZ == x, 1, 0)
        table[entry] = table[entry] + mine * bits * jnp.where(local == 1, 4, 1)
        return carry

    lax.fori_loop(0, NX * PICKS, fill, 0)

    def compact(i, count):
        bits = table[i]
        units[count + 1] = i * 16 + bits
        return count + jnp.where(bits > 0, 1, 0)

    units[0] = lax.fori_loop(0, NX * NZ, compact, 0)


def project_kernel(where, normed, near, ahead, far_a, far_b, behind, send, weights):
    lane_part = where[2]
    for step in range(4):
        row = lax.rem(lane_part + step, 4) * HALF
        for b in range(16):
            if step == 0:
                block = near[b]
            elif step == 1:
                block = ahead[b]
            elif step == 3:
                block = behind[b]
            else:
                block = far_a[b] if b < 8 else far_b[b - 8]
            base = pl.multiple_of(b * 256 + row, HALF)
            packed = block[64:96, :]
            weights[pl.ds(base, 64), 0:HEAD] = block[0:64, :]
            weights[pl.ds(base, 32), HEAD : 2 * HEAD] = packed
            weights[pl.ds(pl.multiple_of(base + 32, 32), 32), HEAD : 2 * HEAD] = pltpu.roll(
                packed.astype(F32), HALF, 1
            ).astype(BF16)
    total = jnp.zeros((ROWS, 2 * HEAD), F32)
    for slot in range(8):
        total = total + jnp.dot(
            normed[slot], weights[slot * 512 : (slot + 1) * 512, :], preferred_element_type=F32
        )
    query = total[:, 0:HEAD].astype(BF16)
    for dest in range(NX):
        own = total[dest * SEQ : (dest + 1) * SEQ, HEAD : 2 * HEAD]
        send[dest, 0:ROWS, :] = query
        send[dest, ROWS : ROWS + HALF, :] = side_by_side(own[0:HALF], own[HALF:SEQ], 0, 0)


def own_part(got, first):
    a, b = got[first, ROWS : ROWS + HALF, :], got[first + 1, ROWS : ROWS + HALF, :]
    return jnp.concatenate([side_by_side(a, b, 0, 0), side_by_side(a, b, HALF, HALF)], axis=0)


def queries(got, group):
    rows = pl.ds(pl.multiple_of(group * SEQ, SEQ), SEQ)
    return jnp.concatenate([got[head, rows, :] for head in range(RATIO)], axis=0)


def scores_of(keys, query):
    return (
        lax.dot_general(keys, query, (((1,), (1,)), ((), ())), preferred_element_type=F32) * SCALE
    )


def own_scores(got, group):
    scores = scores_of(own_part(got, 0), queries(got, group))
    key_at = lax.broadcasted_iota(jnp.int32, (SEQ, COLS), 0)
    row_at = lax.broadcasted_iota(jnp.int32, (SEQ, COLS), 1) % SEQ
    return jnp.where(row_at >= key_at, scores, LOW)


def documents(docs, owner, parity, part):
    mine, up, down = docs
    at, cols = (owner // 2) * 2, slice(part * HEAD, (part + 1) * HEAD)
    from_mine = mine[pl.ds(at, 2), :, cols]
    from_up = up[pl.ds(jnp.minimum(at, 6), 2), :, cols]
    from_down = down[pl.ds(jnp.maximum(at - 8, 0), 2), :, cols]
    other = jnp.where(at < 8, from_up, from_down)
    return jnp.where(owner % 2 == parity, from_mine, other).reshape(2 * SEQ, HEAD)


def unit_scores(code, got, docs, parity):
    entry, bits = code // 16, code % 16
    group, owner = entry // NZ, entry % NZ
    keys = documents(docs, owner, parity, 0)
    scores = scores_of(keys, queries(got, group))
    second = (lax.broadcasted_iota(jnp.int32, (1, COLS), 1) % SEQ) // HALF
    kept = []
    for local in range(2):
        use_a, use_b = (bits // (4**local)) % 2, (bits // (2 * 4**local)) % 2
        keep = jnp.where(second == 0, use_a, use_b)
        kept.append(jnp.where(keep > 0, scores[local * SEQ : (local + 1) * SEQ], LOW))
    return group, owner, jnp.concatenate(kept, axis=0)


def stats_kernel(where, units, got, docs_mine, docs_up, docs_down, send, stats):
    x = where[0]
    docs = (docs_mine, docs_up, docs_down)
    scores = own_scores(got, x)
    top = jnp.max(scores, axis=0, keepdims=True)
    stats[0:4, :] = jnp.full((4, COLS), LOW, F32)
    stats[4:8, :] = jnp.zeros((4, COLS), F32)
    stats[pl.ds(x, 1), :] = top
    stats[pl.ds(x + 4, 1), :] = jnp.sum(jnp.exp(scores - top), axis=0, keepdims=True)

    def unit(i, carry):
        group, owner, scores = unit_scores(units[i + 1], got, docs, where[1] % 2)
        before = stats[pl.ds(group, 1), :]
        top = jnp.maximum(before, jnp.max(scores, axis=0, keepdims=True))
        part = jnp.sum(jnp.exp(scores - top), axis=0, keepdims=True)
        stats[pl.ds(group, 1), :] = top
        stats[pl.ds(group + 4, 1), :] = stats[pl.ds(group + 4, 1), :] * jnp.exp(before - top) + part
        return carry

    lax.fori_loop(0, units[0], unit, 0)
    for dest in range(NX):
        send[dest] = stats[...]


def values_kernel(where, units, got, docs_mine, docs_up, docs_down, all_stats, send, total):
    x = where[0]
    docs = (docs_mine, docs_up, docs_down)
    tops = [all_stats[src, 0:4, :] for src in range(NX)]
    top = jnp.maximum(jnp.maximum(tops[0], tops[1]), jnp.maximum(tops[2], tops[3]))
    sums = jnp.zeros((4, COLS), F32)
    for src in range(NX):
        sums = sums + all_stats[src, 4:8, :] * jnp.exp(tops[src] - top)
    total[0:4, :] = top
    total[4:8, :] = sums
    send[...] = jnp.zeros(send.shape, F32)

    def add(group, scores, values):
        expo = jnp.exp(scores - total[pl.ds(group, 1), :])
        probs = (expo / total[pl.ds(group + 4, 1), :]).astype(BF16)
        out = lax.dot_general(values, probs, (((0,), (0,)), ((), ())), preferred_element_type=F32)
        send[pl.ds(group, 1)] = send[pl.ds(group, 1)] + out[None]

    add(x, own_scores(got, x), own_part(got, 2))

    def unit(i, carry):
        group, owner, scores = unit_scores(units[i + 1], got, docs, where[1] % 2)
        values = documents(docs, owner, where[1] % 2, 1)
        add(group, scores, values)
        return carry

    lax.fori_loop(0, units[0], unit, 0)


def finish_kernel(got, out):
    for head in range(RATIO):
        cols = slice(head * SEQ, (head + 1) * SEQ)
        total = (got[0, :, cols] + got[1, :, cols]) + (got[2, :, cols] + got[3, :, cols])
        out[:, cols] = total.T.astype(BF16)


def exchange(array, axes):
    return lax.all_to_all(array, axes, 0, 0, tiled=True)


def spread(array, axes, count):
    return exchange(jnp.broadcast_to(array[None], (count, *array.shape)), axes)


def shards(tokens, norm_gain, wq, wk, wv, doc_cache, doc_lists, doc_place, block_use):
    shape = jax.ShapeDtypeStruct
    z_axes = ("zh", "zm", "zp")

    def from_z(array, step):
        return lax.ppermute(array, z_axes, [((i + step) % NZ, i) for i in range(NZ)])

    docs_mine = lax.all_gather(doc_cache, ("zh", "zm"), axis=0, tiled=True)
    x, zh = lax.axis_index("x"), lax.axis_index("zh")
    zl = lax.axis_index("zm") * 2 + lax.axis_index("zp")
    where = jnp.stack([x, zh * 4 + zl, zl, lax.axis_index("core"), lax.axis_index("y")]).astype(jnp.int32)

    parts = call(pack_kernel, shape((4, 4, 96, HEAD), BF16), (wq, wk, wv), [VMEM] * 3)
    near = exchange(parts.reshape(16, 96, HEAD), ("x", "zh"))
    tokens, _ = lax.optimization_barrier((tokens, parts))
    by_y = jnp.stack([tokens] + [lax.ppermute(tokens, "y", [((i + k) % 4, i) for i in range(4)]) for k in (1, 2, 3)])
    by_y, near = lax.optimization_barrier((by_y, near))
    mine = spread(by_y, "x", NX)
    ahead = from_z(near, 1)
    behind = from_z(near, -1)
    far_a = from_z(near[0:8], 2)
    far_b = from_z(near[8:16], -2)
    mine, ahead, behind, far_a, far_b, docs_mine = lax.optimization_barrier(
        (mine, ahead, behind, far_a, far_b, docs_mine)
    )
    docs_up = from_z(docs_mine[0:8], 1)
    docs_down = from_z(docs_mine[8:16], -1)
    docs = (docs_mine, docs_up, docs_down)
    other = lax.ppermute(mine, "core", [(0, 1), (1, 0)])
    gain = norm_gain.astype(F32).reshape(8, 1, 512)
    normed = call(
        norm_kernel,
        shape((8, ROWS, 512), BF16),
        (where, mine, other, gain),
        [SMEM, VMEM, VMEM, VMEM],
        flops=ROWS * 4096 * 8,
        moved=8 << 20,
    )
    use = spread(block_use, "x", NX).reshape(8, PICKS)
    units = call(
        route_kernel,
        shape((UNITS,), jnp.int32),
        (where, doc_lists, doc_place, use),
        [SMEM] * 4,
        out_specs=SMEM,
        scratch=[pltpu.SMEM((NX * NZ,), jnp.int32)],
    )

    send = call(
        project_kernel,
        shape((NX, ROWS + HALF, HEAD), BF16),
        (where, normed, near, ahead, far_a, far_b, behind),
        [SMEM] + [VMEM] * 6,
        scratch=[pltpu.VMEM((4096, 2 * HEAD), BF16)],
        flops=2 * ROWS * 4096 * 256,
        moved=8 << 20,
    )
    got = exchange(send, "x")
    stats = call(
        stats_kernel,
        shape((NX, 8, COLS), F32),
        (where, units, got, *docs),
        [SMEM, SMEM] + [VMEM] * 4,
        scratch=[pltpu.VMEM((8, COLS), F32)],
    )
    all_stats = exchange(stats, "x")
    partial = call(
        values_kernel,
        shape((NX, HEAD, COLS), F32),
        (where, units, got, *docs, all_stats),
        [SMEM, SMEM] + [VMEM] * 5,
        scratch=[pltpu.VMEM((8, COLS), F32)],
    )
    returned = exchange(partial, "x")
    return call(finish_kernel, shape((SEQ, COLS), BF16), (returned,), [VMEM])


def solution(mesh):
    fine = Mesh(mesh.devices.reshape(4, 4, 2, 2, 4, 2), ("x", "zh", "zm", "zp", "y", "core"))
    pairs, tensor = ("x", "zh", "zm", "zp"), ("y", "core")
    placed = (
        P(pairs, tensor),
        P(),
        P(pairs, tensor),
        P(pairs, tensor),
        P(pairs, tensor),
        P(pairs, None, tensor),
        P(),
        P(),
        P(pairs, None),
    )
    return jax.shard_map(
        shards, mesh=fine, in_specs=placed, out_specs=P(pairs, tensor), check_vma=False
    )
```

```python
import jax
import jax.numpy as jnp
from jax import lax
from jax.experimental import pallas as pl
from jax.experimental.pallas import tpu as pltpu
from jax.sharding import Mesh
from jax.sharding import PartitionSpec as P

F32 = jnp.float32
BF16 = jnp.bfloat16
HEAD = 128
HALF = 64
SEQ = 128
RATIO = 4
NX = 4
NZ = 16
PICKS = 16
ROWS = NX * SEQ
COLS = RATIO * SEQ
SCALE = HEAD ** (-0.5)
LOW = -1e30
UNITS = 128

VMEM = pl.BlockSpec(memory_space=pltpu.VMEM)
SMEM = pl.BlockSpec(memory_space=pltpu.SMEM)
PARAMS = pltpu.CompilerParams(vmem_limit_bytes=24 * 1024 * 1024)


def call(kernel, outs, args, specs, out_specs=None, scratch=(), flops=0, moved=0):
    return pl.pallas_call(
        kernel,
        out_shape=outs,
        in_specs=specs,
        out_specs=VMEM if out_specs is None else out_specs,
        scratch_shapes=list(scratch),
        compiler_params=PARAMS,
        cost_estimate=pl.CostEstimate(flops=flops, bytes_accessed=moved, transcendentals=0),
    )(*args)


def side_by_side(left, right, left_at, right_at):
    left, right = left.astype(F32), right.astype(F32)
    lane = lax.broadcasted_iota(jnp.int32, left.shape, 1)
    left = pltpu.roll(left, HALF, 1) if left_at else left
    right = right if right_at else pltpu.roll(right, HALF, 1)
    return jnp.where(lane < HALF, left, right).astype(BF16)


def pack_kernel(wq, wk, wv, out):
    for part in range(NX):
        src = wk if part < 2 else wv
        at = HALF * (part % 2)
        packed = side_by_side(src[0:32, :], src[32:64, :], at, at)
        for copy in range(4):
            out[part, copy, 0:64, :] = wq[:, part * HEAD : (part + 1) * HEAD]
            out[part, copy, 64:96, :] = packed


def norm_kernel(where, mine, other, gain, out):
    core = where[3]
    for row in range(NX):
        rows = pl.ds(pl.multiple_of(lax.rem(where[0] + row, NX) * SEQ, SEQ), SEQ)
        total = jnp.zeros((SEQ, HEAD), F32)
        for src in (mine, other):
            for y in range(4):
                for c in range(4):
                    feats = src[row, y, :, c * HEAD : (c + 1) * HEAD].astype(F32)
                    total = total + feats * feats
        power = jnp.sum(total, axis=-1, keepdims=True) * (1.0 / 4096.0)
        factor = lax.rsqrt(power + 1e-05)
        for src, flip in ((mine, 0), (other, 1)):
            side = core if flip == 0 else 1 - core
            for y in range(4):
                slot = 2 * y + side
                feats = src[row, y].astype(F32)
                out[slot, rows, :] = (feats * factor * gain[slot]).astype(BF16)


def route_kernel(where, lists, place, use, units, table):
    x, z = where[0], where[1]

    def clear(i, carry):
        table[i] = 0
        return carry

    lax.fori_loop(0, NX * NZ, clear, 0)

    def fill(i, carry):
        row, pick = i // PICKS, i % PICKS
        at = place[lists[row * NZ + z, pick]]
        owner, local = at // 2, at % 2
        bits = use[row * 2, pick] + 2 * use[row * 2 + 1, pick]
        entry = row * NZ + owner % NZ
        mine = jnp.where(owner // NZ == x, 1, 0)
        table[entry] = table[entry] + mine * bits * jnp.where(local == 1, 4, 1)
        return carry

    lax.fori_loop(0, NX * PICKS, fill, 0)

    def compact(i, count):
        bits = table[i]
        units[count + 1] = i * 16 + bits
        return count + jnp.where(bits > 0, 1, 0)

    units[0] = lax.fori_loop(0, NX * NZ, compact, 0)


def project_kernel(where, normed, near, ahead, far_a, far_b, behind, send, weights):
    lane_part = where[2]
    for step in range(4):
        row = lax.rem(lane_part + step, 4) * HALF
        for b in range(16):
            if step == 0:
                block = near[b]
            elif step == 1:
                block = ahead[b]
            elif step == 3:
                block = behind[b]
            else:
                block = far_a[b] if b < 8 else far_b[b - 8]
            base = pl.multiple_of(b * 256 + row, HALF)
            packed = block[64:96, :]
            weights[pl.ds(base, 64), 0:HEAD] = block[0:64, :]
            weights[pl.ds(base, 32), HEAD : 2 * HEAD] = packed
            weights[pl.ds(pl.multiple_of(base + 32, 32), 32), HEAD : 2 * HEAD] = pltpu.roll(
                packed.astype(F32), HALF, 1
            ).astype(BF16)
    total = jnp.zeros((ROWS, 2 * HEAD), F32)
    for slot in range(8):
        total = total + jnp.dot(
            normed[slot], weights[slot * 512 : (slot + 1) * 512, :], preferred_element_type=F32
        )
    query = total[:, 0:HEAD].astype(BF16)
    for dest in range(NX):
        own = total[dest * SEQ : (dest + 1) * SEQ, HEAD : 2 * HEAD]
        send[dest, 0:ROWS, :] = query
        send[dest, ROWS : ROWS + HALF, :] = side_by_side(own[0:HALF], own[HALF:SEQ], 0, 0)


def own_part(got, first):
    a, b = got[first, ROWS : ROWS + HALF, :], got[first + 1, ROWS : ROWS + HALF, :]
    return jnp.concatenate([side_by_side(a, b, 0, 0), side_by_side(a, b, HALF, HALF)], axis=0)


def queries(got, group):
    rows = pl.ds(pl.multiple_of(group * SEQ, SEQ), SEQ)
    return jnp.concatenate([got[head, rows, :] for head in range(RATIO)], axis=0)


def scores_of(keys, query):
    return (
        lax.dot_general(keys, query, (((1,), (1,)), ((), ())), preferred_element_type=F32) * SCALE
    )


def own_scores(got, group):
    scores = scores_of(own_part(got, 0), queries(got, group))
    key_at = lax.broadcasted_iota(jnp.int32, (SEQ, COLS), 0)
    row_at = lax.broadcasted_iota(jnp.int32, (SEQ, COLS), 1) % SEQ
    return jnp.where(row_at >= key_at, scores, LOW)


def unit_scores(code, got, docs):
    entry, bits = code // 16, code % 16
    group, owner = entry // NZ, entry % NZ
    keys = docs[pl.ds(owner * 2, 2), :, 0:HEAD].reshape(2 * SEQ, HEAD)
    scores = scores_of(keys, queries(got, group))
    second = (lax.broadcasted_iota(jnp.int32, (1, COLS), 1) % SEQ) // HALF
    kept = []
    for local in range(2):
        use_a, use_b = (bits // (4**local)) % 2, (bits // (2 * 4**local)) % 2
        keep = jnp.where(second == 0, use_a, use_b)
        kept.append(jnp.where(keep > 0, scores[local * SEQ : (local + 1) * SEQ], LOW))
    return group, owner, jnp.concatenate(kept, axis=0)


def stats_kernel(where, units, got, docs, send, stats):
    x = where[0]
    scores = own_scores(got, x)
    top = jnp.max(scores, axis=0, keepdims=True)
    stats[0:4, :] = jnp.full((4, COLS), LOW, F32)
    stats[4:8, :] = jnp.zeros((4, COLS), F32)
    stats[pl.ds(x, 1), :] = top
    stats[pl.ds(x + 4, 1), :] = jnp.sum(jnp.exp(scores - top), axis=0, keepdims=True)

    def unit(i, carry):
        group, owner, scores = unit_scores(units[i + 1], got, docs)
        before = stats[pl.ds(group, 1), :]
        top = jnp.maximum(before, jnp.max(scores, axis=0, keepdims=True))
        part = jnp.sum(jnp.exp(scores - top), axis=0, keepdims=True)
        stats[pl.ds(group, 1), :] = top
        stats[pl.ds(group + 4, 1), :] = stats[pl.ds(group + 4, 1), :] * jnp.exp(before - top) + part
        return carry

    lax.fori_loop(0, units[0], unit, 0)
    for dest in range(NX):
        send[dest] = stats[...]


def values_kernel(where, units, got, docs, all_stats, send, total):
    x = where[0]
    tops = [all_stats[src, 0:4, :] for src in range(NX)]
    top = jnp.maximum(jnp.maximum(tops[0], tops[1]), jnp.maximum(tops[2], tops[3]))
    sums = jnp.zeros((4, COLS), F32)
    for src in range(NX):
        sums = sums + all_stats[src, 4:8, :] * jnp.exp(tops[src] - top)
    total[0:4, :] = top
    total[4:8, :] = sums
    send[...] = jnp.zeros(send.shape, F32)

    def add(group, scores, values):
        expo = jnp.exp(scores - total[pl.ds(group, 1), :])
        probs = (expo / total[pl.ds(group + 4, 1), :]).astype(BF16)
        out = lax.dot_general(values, probs, (((0,), (0,)), ((), ())), preferred_element_type=F32)
        send[pl.ds(group, 1)] = send[pl.ds(group, 1)] + out[None]

    add(x, own_scores(got, x), own_part(got, 2))

    def unit(i, carry):
        group, owner, scores = unit_scores(units[i + 1], got, docs)
        values = docs[pl.ds(owner * 2, 2), :, HEAD : 2 * HEAD].reshape(2 * SEQ, HEAD)
        add(group, scores, values)
        return carry

    lax.fori_loop(0, units[0], unit, 0)


def finish_kernel(got, out):
    for head in range(RATIO):
        cols = slice(head * SEQ, (head + 1) * SEQ)
        total = (got[0, :, cols] + got[1, :, cols]) + (got[2, :, cols] + got[3, :, cols])
        out[:, cols] = total.T.astype(BF16)


def exchange(array, axes):
    return lax.all_to_all(array, axes, 0, 0, tiled=True)


def spread(array, axes, count):
    return exchange(jnp.broadcast_to(array[None], (count, *array.shape)), axes)


def shards(tokens, norm_gain, wq, wk, wv, doc_cache, doc_lists, doc_place, block_use):
    shape = jax.ShapeDtypeStruct
    z_axes = ("zh", "zl")
    docs = lax.all_gather(doc_cache, z_axes, axis=0, tiled=True)
    x, zh, zl = lax.axis_index("x"), lax.axis_index("zh"), lax.axis_index("zl")
    where = jnp.stack([x, zh * 4 + zl, zl, lax.axis_index("core")]).astype(jnp.int32)

    parts = call(pack_kernel, shape((4, 4, 96, HEAD), BF16), (wq, wk, wv), [VMEM] * 3)
    near = exchange(parts.reshape(16, 96, HEAD), ("x", "zh"))

    def from_z(array, step):
        return lax.ppermute(array, z_axes, [((i + step) % NZ, i) for i in range(NZ)])

    tokens, _ = lax.optimization_barrier((tokens, parts))
    by_y = lax.all_gather(tokens, "y")
    def from_x(array, step):
        return lax.ppermute(array, "x", [((i + step) % NX, i) for i in range(NX)])

    mine = jnp.concatenate(
        [by_y, from_x(by_y, 1), from_x(by_y[0:2], 2), from_x(by_y[2:4], -2), from_x(by_y, -1)]
    ).reshape(4, 4, SEQ, 512)
    ahead = from_z(near, 1)
    behind = from_z(near, -1)
    mine, ahead, behind = lax.optimization_barrier((mine, ahead, behind))
    other = lax.ppermute(mine, "core", [(0, 1), (1, 0)])
    gain = norm_gain.astype(F32).reshape(8, 1, 512)
    normed = call(
        norm_kernel,
        shape((8, ROWS, 512), BF16),
        (where, mine, other, gain),
        [SMEM, VMEM, VMEM, VMEM],
        flops=ROWS * 4096 * 8,
        moved=8 << 20,
    )
    use = spread(block_use, "x", NX).reshape(8, PICKS)
    units = call(
        route_kernel,
        shape((UNITS,), jnp.int32),
        (where, doc_lists, doc_place, use),
        [SMEM] * 4,
        out_specs=SMEM,
        scratch=[pltpu.SMEM((NX * NZ,), jnp.int32)],
    )

    far_a = from_z(ahead[0:8], 1)
    far_b = from_z(behind[8:16], -1)
    send = call(
        project_kernel,
        shape((NX, ROWS + HALF, HEAD), BF16),
        (where, normed, near, ahead, far_a, far_b, behind),
        [SMEM] + [VMEM] * 6,
        scratch=[pltpu.VMEM((4096, 2 * HEAD), BF16)],
        flops=2 * ROWS * 4096 * 256,
        moved=8 << 20,
    )
    got = exchange(send, "x")
    stats = call(
        stats_kernel,
        shape((NX, 8, COLS), F32),
        (where, units, got, docs),
        [SMEM, SMEM, VMEM, VMEM],
        scratch=[pltpu.VMEM((8, COLS), F32)],
    )
    all_stats = exchange(stats, "x")
    partial = call(
        values_kernel,
        shape((NX, HEAD, COLS), F32),
        (where, units, got, docs, all_stats),
        [SMEM, SMEM, VMEM, VMEM, VMEM],
        scratch=[pltpu.VMEM((8, COLS), F32)],
    )
    returned = exchange(partial, "x")
    return call(finish_kernel, shape((SEQ, COLS), BF16), (returned,), [VMEM])


def solution(mesh):
    fine = Mesh(mesh.devices.reshape(4, 4, 4, 4, 2), ("x", "zh", "zl", "y", "core"))
    pairs, tensor = ("x", "zh", "zl"), ("y", "core")
    placed = (
        P(pairs, tensor),
        P(),
        P(pairs, tensor),
        P(pairs, tensor),
        P(pairs, tensor),
        P(pairs, None, tensor),
        P(),
        P(),
        P(pairs, None),
    )
    return jax.shard_map(
        shards, mesh=fine, in_specs=placed, out_specs=P(pairs, tensor), check_vma=False
    )
```

```python
import jax
import jax.numpy as jnp
from jax import lax
from jax.experimental import pallas as pl
from jax.experimental.pallas import tpu as pltpu
from jax.sharding import Mesh
from jax.sharding import PartitionSpec as P

F32 = jnp.float32
BF16 = jnp.bfloat16
HEAD = 128
HALF = 64
SEQ = 128
RATIO = 4
NX = 4
NZ = 16
PICKS = 16
ROWS = NX * SEQ
COLS = RATIO * SEQ
SCALE = HEAD ** (-0.5)
LOW = -1e30
UNITS = 128

VMEM = pl.BlockSpec(memory_space=pltpu.VMEM)
SMEM = pl.BlockSpec(memory_space=pltpu.SMEM)
PARAMS = pltpu.CompilerParams(vmem_limit_bytes=24 * 1024 * 1024)


def call(kernel, outs, args, specs, out_specs=None, scratch=(), flops=0, moved=0):
    return pl.pallas_call(
        kernel,
        out_shape=outs,
        in_specs=specs,
        out_specs=VMEM if out_specs is None else out_specs,
        scratch_shapes=list(scratch),
        compiler_params=PARAMS,
        cost_estimate=pl.CostEstimate(flops=flops, bytes_accessed=moved, transcendentals=0),
    )(*args)


def side_by_side(left, right, left_at, right_at):
    left, right = left.astype(F32), right.astype(F32)
    lane = lax.broadcasted_iota(jnp.int32, left.shape, 1)
    left = pltpu.roll(left, HALF, 1) if left_at else left
    right = right if right_at else pltpu.roll(right, HALF, 1)
    return jnp.where(lane < HALF, left, right).astype(BF16)


def pack_kernel(wq, wk, wv, use, out):
    for part in range(NX):
        src = wk if part < 2 else wv
        at = HALF * (part % 2)
        out[part, 0:64, :] = wq[:, part * HEAD : (part + 1) * HEAD]
        out[part, 64:96, :] = side_by_side(src[0:32, :], src[32:64, :], at, at)
        out[part, 96:112, :] = use[...]


def norm_kernel(where, mine, other, gain, out):
    core = where[3]
    for x in range(NX):
        rows = pl.ds(x * SEQ, SEQ)
        total = jnp.zeros((SEQ, HEAD), F32)
        for src in (mine, other):
            for y in range(4):
                for c in range(4):
                    feats = src[x * 4 + y, :, c * HEAD : (c + 1) * HEAD].astype(F32)
                    total = total + feats * feats
        power = jnp.sum(total, axis=-1, keepdims=True) * (1.0 / 4096.0)
        factor = lax.rsqrt(power + 1e-05)
        for src, side in ((mine, core), (other, 1 - core)):
            for y in range(4):
                slot = 2 * y + side
                feats = src[x * 4 + y].astype(F32)
                out[slot, rows, :] = (feats * factor * gain[slot]).astype(BF16)


def route_kernel(where, lists, place, use, units, table):
    x, z = where[0], where[1]

    def clear(i, carry):
        table[i] = 0
        return carry

    lax.fori_loop(0, NX * NZ, clear, 0)

    def fill(i, carry):
        row, pick = i // PICKS, i % PICKS
        at = place[lists[row * NZ + z, pick]]
        owner, local = at // 2, at % 2
        bits = use[row * 2, pick] + 2 * use[row * 2 + 1, pick]
        entry = row * NZ + owner % NZ
        mine = jnp.where(owner // NZ == x, 1, 0)
        table[entry] = table[entry] + mine * bits * jnp.where(local == 1, 4, 1)
        return carry

    lax.fori_loop(0, NX * PICKS, fill, 0)

    def compact(i, count):
        bits = table[i]
        units[count + 1] = i * 16 + bits
        return count + jnp.where(bits > 0, 1, 0)

    units[0] = lax.fori_loop(0, NX * NZ, compact, 0)


def project_kernel(where, normed, near, ahead, far, behind, send, weights):
    z = where[1]
    for step, blocks in ((0, near), (1, ahead), (2, far), (NZ - 1, behind)):
        at = lax.rem(z + step, NZ)
        for b in range(16):
            block = blocks[b]
            depth = (b % 4) * 1024 + lax.rem(at + (b // 4) * 4, NZ) * HALF
            base = pl.multiple_of(depth, HALF)
            packed = block[64:96, :]
            weights[pl.ds(base, 64), 0:HEAD] = block[0:64, :]
            weights[pl.ds(base, 32), HEAD : 2 * HEAD] = packed
            weights[pl.ds(pl.multiple_of(base + 32, 32), 32), HEAD : 2 * HEAD] = pltpu.roll(
                packed.astype(F32), HALF, 1
            ).astype(BF16)
    total = jnp.zeros((ROWS, 2 * HEAD), F32)
    for slot in range(8):
        total = total + jnp.dot(
            normed[slot], weights[slot * 512 : (slot + 1) * 512, :], preferred_element_type=F32
        )
    query = total[:, 0:HEAD].astype(BF16)
    for dest in range(NX):
        own = total[dest * SEQ : (dest + 1) * SEQ, HEAD : 2 * HEAD]
        send[dest, 0:ROWS, :] = query
        send[dest, ROWS : ROWS + HALF, :] = side_by_side(own[0:HALF], own[HALF:SEQ], 0, 0)


def own_part(got, first):
    a, b = got[first, ROWS : ROWS + HALF, :], got[first + 1, ROWS : ROWS + HALF, :]
    return jnp.concatenate([side_by_side(a, b, 0, 0), side_by_side(a, b, HALF, HALF)], axis=0)


def queries(got, group):
    rows = pl.ds(pl.multiple_of(group * SEQ, SEQ), SEQ)
    return jnp.concatenate([got[head, rows, :] for head in range(RATIO)], axis=0)


def scores_of(keys, query):
    return (
        lax.dot_general(keys, query, (((1,), (1,)), ((), ())), preferred_element_type=F32) * SCALE
    )


def own_scores(got, group):
    scores = scores_of(own_part(got, 0), queries(got, group))
    key_at = lax.broadcasted_iota(jnp.int32, (SEQ, COLS), 0)
    row_at = lax.broadcasted_iota(jnp.int32, (SEQ, COLS), 1) % SEQ
    return jnp.where(row_at >= key_at, scores, LOW)


def unit_scores(code, got, docs):
    entry, bits = code // 16, code % 16
    group, owner = entry // NZ, entry % NZ
    keys = docs[pl.ds(owner * 2, 2), :, 0:HEAD].reshape(2 * SEQ, HEAD)
    scores = scores_of(keys, queries(got, group))
    second = (lax.broadcasted_iota(jnp.int32, (1, COLS), 1) % SEQ) // HALF
    kept = []
    for local in range(2):
        use_a, use_b = (bits // (4**local)) % 2, (bits // (2 * 4**local)) % 2
        keep = jnp.where(second == 0, use_a, use_b)
        kept.append(jnp.where(keep > 0, scores[local * SEQ : (local + 1) * SEQ], LOW))
    return group, owner, jnp.concatenate(kept, axis=0)


def stats_kernel(where, units, got, docs, send, stats):
    x = where[0]
    scores = own_scores(got, x)
    top = jnp.max(scores, axis=0, keepdims=True)
    stats[0:4, :] = jnp.full((4, COLS), LOW, F32)
    stats[4:8, :] = jnp.zeros((4, COLS), F32)
    stats[pl.ds(x, 1), :] = top
    stats[pl.ds(x + 4, 1), :] = jnp.sum(jnp.exp(scores - top), axis=0, keepdims=True)

    def unit(i, carry):
        group, owner, scores = unit_scores(units[i + 1], got, docs)
        before = stats[pl.ds(group, 1), :]
        top = jnp.maximum(before, jnp.max(scores, axis=0, keepdims=True))
        part = jnp.sum(jnp.exp(scores - top), axis=0, keepdims=True)
        stats[pl.ds(group, 1), :] = top
        stats[pl.ds(group + 4, 1), :] = stats[pl.ds(group + 4, 1), :] * jnp.exp(before - top) + part
        return carry

    lax.fori_loop(0, units[0], unit, 0)
    for dest in range(NX):
        send[dest] = stats[...]


def values_kernel(where, units, got, docs, all_stats, send, total):
    x = where[0]
    tops = [all_stats[src, 0:4, :] for src in range(NX)]
    top = jnp.maximum(jnp.maximum(tops[0], tops[1]), jnp.maximum(tops[2], tops[3]))
    sums = jnp.zeros((4, COLS), F32)
    for src in range(NX):
        sums = sums + all_stats[src, 4:8, :] * jnp.exp(tops[src] - top)
    total[0:4, :] = top
    total[4:8, :] = sums
    send[...] = jnp.zeros(send.shape, F32)

    def add(group, scores, values):
        expo = jnp.exp(scores - total[pl.ds(group, 1), :])
        probs = (expo / total[pl.ds(group + 4, 1), :]).astype(BF16)
        out = lax.dot_general(values, probs, (((0,), (0,)), ((), ())), preferred_element_type=F32)
        send[pl.ds(group, 1)] = send[pl.ds(group, 1)] + out[None]

    add(x, own_scores(got, x), own_part(got, 2))

    def unit(i, carry):
        group, owner, scores = unit_scores(units[i + 1], got, docs)
        values = docs[pl.ds(owner * 2, 2), :, HEAD : 2 * HEAD].reshape(2 * SEQ, HEAD)
        add(group, scores, values)
        return carry

    lax.fori_loop(0, units[0], unit, 0)


def finish_kernel(got, out):
    for head in range(RATIO):
        cols = slice(head * SEQ, (head + 1) * SEQ)
        total = (got[0, :, cols] + got[1, :, cols]) + (got[2, :, cols] + got[3, :, cols])
        out[:, cols] = total.T.astype(BF16)


def exchange(array, axes):
    return lax.all_to_all(array, axes, 0, 0, tiled=True)


def spread(array, axes, count):
    return exchange(jnp.broadcast_to(array[None], (count, *array.shape)), axes)


def shards(tokens, norm_gain, wq, wk, wv, doc_cache, doc_lists, doc_place, block_use):
    shape = jax.ShapeDtypeStruct
    z_axes = ("zh", "zl")
    docs = lax.all_gather(doc_cache, z_axes, axis=0, tiled=True)
    x, zh, zl = lax.axis_index("x"), lax.axis_index("zh"), lax.axis_index("zl")
    y, core = lax.axis_index("y"), lax.axis_index("core")
    where = jnp.stack([x, zh * 4 + zl, zl, core, y]).astype(jnp.int32)

    def from_z(array, step):
        return lax.ppermute(array, z_axes, [((i + step) % NZ, i) for i in range(NZ)])

    def from_y(array, step):
        return lax.ppermute(array, "y", [((i + step) % 4, i) for i in range(4)])

    flags = jnp.pad(block_use.astype(BF16), ((0, 14), (0, HEAD - PICKS)))
    packed = call(
        pack_kernel, shape((NX, 112, HEAD), BF16), (wq, wk, wv, flags), [VMEM] * 4
    )
    by_x = exchange(packed, "x")
    part = by_x[:, 0:96]
    near = jnp.concatenate([part, from_z(part, 4), from_z(part, 8), from_z(part, 12)])

    tokens, _ = lax.optimization_barrier((tokens, by_x))
    mine = spread(tokens, ("x", "y"), 16)
    ahead = from_z(near, 1)
    behind = from_z(near, -1)
    mine, _, _ = lax.optimization_barrier((mine, ahead, behind))
    other = lax.ppermute(mine, "core", [(0, 1), (1, 0)])
    gain = norm_gain.astype(F32).reshape(8, 1, 512)
    normed = call(
        norm_kernel,
        shape((8, ROWS, 512), BF16),
        (where, mine, other, gain),
        [SMEM, VMEM, VMEM, VMEM],
        flops=ROWS * 4096 * 8,
        moved=8 << 20,
    )
    use = by_x[:, 96:98, 0:PICKS].astype(jnp.int32).reshape(8, PICKS)
    units = call(
        route_kernel,
        shape((UNITS,), jnp.int32),
        (where, doc_lists, doc_place, use),
        [SMEM] * 4,
        out_specs=SMEM,
        scratch=[pltpu.SMEM((NX * NZ,), jnp.int32)],
    )

    far = from_z(ahead, 1)
    send = call(
        project_kernel,
        shape((NX, ROWS + HALF, HEAD), BF16),
        (where, normed, near, ahead, far, behind),
        [SMEM] + [VMEM] * 5,
        scratch=[pltpu.VMEM((4096, 2 * HEAD), BF16)],
        flops=2 * ROWS * 4096 * 256,
        moved=8 << 20,
    )
    got = exchange(send, "x")
    stats = call(
        stats_kernel,
        shape((NX, 8, COLS), F32),
        (where, units, got, docs),
        [SMEM, SMEM, VMEM, VMEM],
        scratch=[pltpu.VMEM((8, COLS), F32)],
    )
    all_stats = exchange(stats, "x")
    partial = call(
        values_kernel,
        shape((NX, HEAD, COLS), F32),
        (where, units, got, docs, all_stats),
        [SMEM, SMEM, VMEM, VMEM, VMEM],
        scratch=[pltpu.VMEM((8, COLS), F32)],
    )
    returned = exchange(partial, "x")
    return call(finish_kernel, shape((SEQ, COLS), BF16), (returned,), [VMEM])


def solution(mesh):
    fine = Mesh(mesh.devices.reshape(4, 4, 4, 4, 2), ("x", "zh", "zl", "y", "core"))
    pairs, tensor = ("x", "zh", "zl"), ("y", "core")
    placed = (
        P(pairs, tensor),
        P(),
        P(pairs, tensor),
        P(pairs, tensor),
        P(pairs, tensor),
        P(pairs, None, tensor),
        P(),
        P(),
        P(pairs, None),
    )
    return jax.shard_map(
        shards, mesh=fine, in_specs=placed, out_specs=P(pairs, tensor), check_vma=False
    )
```

```python
import jax
import jax.numpy as jnp
from jax import lax
from jax.experimental import pallas as pl
from jax.experimental.pallas import tpu as pltpu
from jax.sharding import Mesh
from jax.sharding import PartitionSpec as P

F32 = jnp.float32
BF16 = jnp.bfloat16
HEAD = 128
HALF = 64
SEQ = 128
RATIO = 4
NX = 4
NZ = 16
PICKS = 16
ROWS = NX * SEQ
COLS = RATIO * SEQ
SCALE = HEAD ** (-0.5)
LOW = -1e30
UNITS = 128

VMEM = pl.BlockSpec(memory_space=pltpu.VMEM)
SMEM = pl.BlockSpec(memory_space=pltpu.SMEM)
PARAMS = pltpu.CompilerParams(vmem_limit_bytes=24 * 1024 * 1024)


def call(kernel, outs, args, specs, out_specs=None, scratch=(), flops=0, moved=0):
    return pl.pallas_call(
        kernel,
        out_shape=outs,
        in_specs=specs,
        out_specs=VMEM if out_specs is None else out_specs,
        scratch_shapes=list(scratch),
        compiler_params=PARAMS,
        cost_estimate=pl.CostEstimate(flops=flops, bytes_accessed=moved, transcendentals=0),
    )(*args)


def side_by_side(left, right, left_at, right_at):
    left, right = left.astype(F32), right.astype(F32)
    lane = lax.broadcasted_iota(jnp.int32, left.shape, 1)
    left = pltpu.roll(left, HALF, 1) if left_at else left
    right = right if right_at else pltpu.roll(right, HALF, 1)
    return jnp.where(lane < HALF, left, right).astype(BF16)


def pack_kernel(wq, wk, wv, use, out):
    for part in range(NX):
        src = wk if part < 2 else wv
        at = HALF * (part % 2)
        out[part, 0:64, :] = wq[:, part * HEAD : (part + 1) * HEAD]
        out[part, 64:96, :] = side_by_side(src[0:32, :], src[32:64, :], at, at)
        out[part, 96:128, :] = use[...]


def norm_kernel(where, mine, other, gain, out):
    core = where[3]
    for row in range(NX):
        rows = pl.ds(pl.multiple_of(lax.rem(where[0] + row, NX) * SEQ, SEQ), SEQ)
        total = jnp.zeros((SEQ, HEAD), F32)
        for src in (mine, other):
            for y in range(4):
                for c in range(4):
                    feats = src[row, y, :, c * HEAD : (c + 1) * HEAD].astype(F32)
                    total = total + feats * feats
        power = jnp.sum(total, axis=-1, keepdims=True) * (1.0 / 4096.0)
        factor = lax.rsqrt(power + 1e-05)
        for src, flip in ((mine, 0), (other, 1)):
            side = core if flip == 0 else 1 - core
            for y in range(4):
                slot = 2 * y + side
                feats = src[row, y].astype(F32)
                out[slot, rows, :] = (feats * factor * gain[slot]).astype(BF16)


def route_kernel(where, lists, place, use, units, table):
    x, z = where[0], where[1]

    def clear(i, carry):
        table[i] = 0
        return carry

    lax.fori_loop(0, NX * NZ, clear, 0)

    def fill(i, carry):
        row, pick = i // PICKS, i % PICKS
        at = place[lists[row * NZ + z, pick]]
        owner, local = at // 2, at % 2
        bits = use[row * 2, pick] + 2 * use[row * 2 + 1, pick]
        entry = row * NZ + owner % NZ
        mine = jnp.where(owner // NZ == x, 1, 0)
        table[entry] = table[entry] + mine * bits * jnp.where(local == 1, 4, 1)
        return carry

    lax.fori_loop(0, NX * PICKS, fill, 0)

    def compact(i, count):
        bits = table[i]
        units[count + 1] = i * 16 + bits
        return count + jnp.where(bits > 0, 1, 0)

    units[0] = lax.fori_loop(0, NX * NZ, compact, 0)


def project_kernel(where, normed, mine, up, down, send, weights):
    parity = where[1] % 2
    for i in range(8):
        for b in range(8):
            x = b % 4
            if b < 4:
                block, z = mine[i, x], 2 * i + parity
            else:
                block, z = (up[i, x] if i < 4 else down[i - 4, x]), 2 * i + 1 - parity
            base = pl.multiple_of(x * 1024 + z * HALF, HALF)
            packed = block[64:96, :]
            weights[pl.ds(base, 64), 0:HEAD] = block[0:64, :]
            weights[pl.ds(base, 32), HEAD : 2 * HEAD] = packed
            weights[pl.ds(pl.multiple_of(base + 32, 32), 32), HEAD : 2 * HEAD] = pltpu.roll(
                packed.astype(F32), HALF, 1
            ).astype(BF16)
    total = jnp.zeros((ROWS, 2 * HEAD), F32)
    for slot in range(8):
        total = total + jnp.dot(
            normed[slot], weights[slot * 512 : (slot + 1) * 512, :], preferred_element_type=F32
        )
    query = total[:, 0:HEAD].astype(BF16)
    for dest in range(NX):
        own = total[dest * SEQ : (dest + 1) * SEQ, HEAD : 2 * HEAD]
        send[dest, 0:ROWS, :] = query
        send[dest, ROWS : ROWS + HALF, :] = side_by_side(own[0:HALF], own[HALF:SEQ], 0, 0)


def own_part(got, first):
    a, b = got[first, ROWS : ROWS + HALF, :], got[first + 1, ROWS : ROWS + HALF, :]
    return jnp.concatenate([side_by_side(a, b, 0, 0), side_by_side(a, b, HALF, HALF)], axis=0)


def queries(got, group):
    rows = pl.ds(pl.multiple_of(group * SEQ, SEQ), SEQ)
    return jnp.concatenate([got[head, rows, :] for head in range(RATIO)], axis=0)


def scores_of(keys, query):
    return (
        lax.dot_general(keys, query, (((1,), (1,)), ((), ())), preferred_element_type=F32) * SCALE
    )


def own_scores(got, group):
    scores = scores_of(own_part(got, 0), queries(got, group))
    key_at = lax.broadcasted_iota(jnp.int32, (SEQ, COLS), 0)
    row_at = lax.broadcasted_iota(jnp.int32, (SEQ, COLS), 1) % SEQ
    return jnp.where(row_at >= key_at, scores, LOW)


def documents(docs, owner, z, part):
    cols, rows = slice(part * HEAD, (part + 1) * HEAD), pl.ds((owner // 4) * 2, 2)
    step = lax.rem(owner - z + NZ, 4)
    near, ahead, far, behind = (ref[rows, :, cols].reshape(2 * SEQ, HEAD) for ref in docs)
    return jnp.where(step < 2, jnp.where(step == 0, near, ahead), jnp.where(step == 2, far, behind))


def unit_scores(code, got, docs, z):
    entry, bits = code // 16, code % 16
    group, owner = entry // NZ, entry % NZ
    keys = documents(docs, owner, z, 0)
    scores = scores_of(keys, queries(got, group))
    second = (lax.broadcasted_iota(jnp.int32, (1, COLS), 1) % SEQ) // HALF
    kept = []
    for local in range(2):
        use_a, use_b = (bits // (4**local)) % 2, (bits // (2 * 4**local)) % 2
        keep = jnp.where(second == 0, use_a, use_b)
        kept.append(jnp.where(keep > 0, scores[local * SEQ : (local + 1) * SEQ], LOW))
    return group, owner, jnp.concatenate(kept, axis=0)


def stats_kernel(where, units, got, near, ahead, far, behind, send, stats):
    docs = (near, ahead, far, behind)
    x = where[0]
    scores = own_scores(got, x)
    top = jnp.max(scores, axis=0, keepdims=True)
    stats[0:4, :] = jnp.full((4, COLS), LOW, F32)
    stats[4:8, :] = jnp.zeros((4, COLS), F32)
    stats[pl.ds(x, 1), :] = top
    stats[pl.ds(x + 4, 1), :] = jnp.sum(jnp.exp(scores - top), axis=0, keepdims=True)

    def unit(i, carry):
        group, owner, scores = unit_scores(units[i + 1], got, docs, where[1])
        before = stats[pl.ds(group, 1), :]
        top = jnp.maximum(before, jnp.max(scores, axis=0, keepdims=True))
        part = jnp.sum(jnp.exp(scores - top), axis=0, keepdims=True)
        stats[pl.ds(group, 1), :] = top
        stats[pl.ds(group + 4, 1), :] = stats[pl.ds(group + 4, 1), :] * jnp.exp(before - top) + part
        return carry

    lax.fori_loop(0, units[0], unit, 0)
    for dest in range(NX):
        send[dest] = stats[...]


def values_kernel(where, units, got, near, ahead, far, behind, all_stats, send, total):
    docs = (near, ahead, far, behind)
    x = where[0]
    tops = [all_stats[src, 0:4, :] for src in range(NX)]
    top = jnp.maximum(jnp.maximum(tops[0], tops[1]), jnp.maximum(tops[2], tops[3]))
    sums = jnp.zeros((4, COLS), F32)
    for src in range(NX):
        sums = sums + all_stats[src, 4:8, :] * jnp.exp(tops[src] - top)
    total[0:4, :] = top
    total[4:8, :] = sums
    send[...] = jnp.zeros(send.shape, F32)

    def add(group, scores, values):
        expo = jnp.exp(scores - total[pl.ds(group, 1), :])
        probs = (expo / total[pl.ds(group + 4, 1), :]).astype(BF16)
        out = lax.dot_general(values, probs, (((0,), (0,)), ((), ())), preferred_element_type=F32)
        send[pl.ds(group, 1)] = send[pl.ds(group, 1)] + out[None]

    add(x, own_scores(got, x), own_part(got, 2))

    def unit(i, carry):
        group, owner, scores = unit_scores(units[i + 1], got, docs, where[1])
        values = documents(docs, owner, where[1], 1)
        add(group, scores, values)
        return carry

    lax.fori_loop(0, units[0], unit, 0)


def finish_kernel(got, out):
    for head in range(RATIO):
        cols = slice(head * SEQ, (head + 1) * SEQ)
        total = (got[0, :, cols] + got[1, :, cols]) + (got[2, :, cols] + got[3, :, cols])
        out[:, cols] = total.T.astype(BF16)


def exchange(array, axes):
    return lax.all_to_all(array, axes, 0, 0, tiled=True)


def spread(array, axes, count):
    return exchange(jnp.broadcast_to(array[None], (count, *array.shape)), axes)


def shards(tokens, norm_gain, wq, wk, wv, doc_cache, doc_lists, doc_place, block_use):
    shape = jax.ShapeDtypeStruct
    z_axes = ("zh", "zm", "zp")
    x, zh = lax.axis_index("x"), lax.axis_index("zh")
    zl = lax.axis_index("zm") * 2 + lax.axis_index("zp")
    y, core = lax.axis_index("y"), lax.axis_index("core")
    where = jnp.stack([x, zh * 4 + zl, zl, core, y]).astype(jnp.int32)

    def from_z(array, step):
        return lax.ppermute(array, z_axes, [((i + step) % NZ, i) for i in range(NZ)])

    def from_x(array, step):
        return lax.ppermute(array, "x", [((i + step) % NX, i) for i in range(NX)])

    flags = jnp.pad(block_use.astype(BF16), ((0, 30), (0, HEAD - PICKS)))
    packed = call(
        pack_kernel, shape((NX, 128, HEAD), BF16), (wq, wk, wv, flags), [VMEM] * 4
    )
    by_x = exchange(packed, "x")
    w_mine = lax.all_gather(by_x, ("zh", "zm"))

    tokens, doc_cache, _ = lax.optimization_barrier((tokens, doc_cache, by_x))
    near = spread(doc_cache, "zh", 4).reshape(8, SEQ, 2 * HEAD)
    ahead = from_z(near, 1)
    behind = from_z(near, -1)

    by_y = lax.all_gather(tokens, "y")
    mine = jnp.concatenate([by_y, from_x(by_y, 1), from_x(by_y, 2), from_x(by_y, 3)])
    mine = mine.reshape(4, 4, SEQ, 512)
    mine, ahead, behind, w_mine = lax.optimization_barrier((mine, ahead, behind, w_mine))
    w_up = from_z(w_mine[0:4, :, 0:96], 1)
    w_down = from_z(w_mine[4:8, :, 0:96], -1)
    far = from_z(ahead, 1)
    docs = (near, ahead, far, behind)
    other = lax.ppermute(mine, "core", [(0, 1), (1, 0)])
    gain = norm_gain.astype(F32).reshape(8, 1, 512)
    normed = call(
        norm_kernel,
        shape((8, ROWS, 512), BF16),
        (where, mine, other, gain),
        [SMEM, VMEM, VMEM, VMEM],
        flops=ROWS * 4096 * 8,
        moved=8 << 20,
    )
    use = by_x[:, 96:98, 0:PICKS].astype(jnp.int32).reshape(8, PICKS)
    units = call(
        route_kernel,
        shape((UNITS,), jnp.int32),
        (where, doc_lists, doc_place, use),
        [SMEM] * 4,
        out_specs=SMEM,
        scratch=[pltpu.SMEM((NX * NZ,), jnp.int32)],
    )

    send = call(
        project_kernel,
        shape((NX, ROWS + HALF, HEAD), BF16),
        (where, normed, w_mine, w_up, w_down),
        [SMEM] + [VMEM] * 4,
        scratch=[pltpu.VMEM((4096, 2 * HEAD), BF16)],
        flops=2 * ROWS * 4096 * 256,
        moved=8 << 20,
    )
    got = exchange(send, "x")
    stats = call(
        stats_kernel,
        shape((NX, 8, COLS), F32),
        (where, units, got, *docs),
        [SMEM, SMEM] + [VMEM] * 5,
        scratch=[pltpu.VMEM((8, COLS), F32)],
    )
    all_stats = exchange(stats, "x")
    partial = call(
        values_kernel,
        shape((NX, HEAD, COLS), F32),
        (where, units, got, *docs, all_stats),
        [SMEM, SMEM] + [VMEM] * 6,
        scratch=[pltpu.VMEM((8, COLS), F32)],
    )
    returned = exchange(partial, "x")
    return call(finish_kernel, shape((SEQ, COLS), BF16), (returned,), [VMEM])


def solution(mesh):
    fine = Mesh(mesh.devices.reshape(4, 4, 2, 2, 4, 2), ("x", "zh", "zm", "zp", "y", "core"))
    pairs, tensor = ("x", "zh", "zm", "zp"), ("y", "core")
    placed = (
        P(pairs, tensor),
        P(),
        P(pairs, tensor),
        P(pairs, tensor),
        P(pairs, tensor),
        P(pairs, None, tensor),
        P(),
        P(),
        P(pairs, None),
    )
    return jax.shard_map(
        shards, mesh=fine, in_specs=placed, out_specs=P(pairs, tensor), check_vma=False
    )
```

```python
import math

import jax
import jax.numpy as jnp
from jax import lax
from jax.experimental import pallas as pl
from jax.experimental.pallas import tpu as pltpu
from jax.sharding import Mesh
from jax.sharding import PartitionSpec as P

F32 = jnp.float32
BF16 = jnp.bfloat16
HEAD = 128
HALF = 64
SEQ = 128
RATIO = 4
NX = 4
NZ = 16
PICKS = 16
ROWS = NX * SEQ
COLS = RATIO * SEQ
RATE = HEAD ** (-0.5) * math.log2(math.e)
LOW = -1e30
UNITS = 128

VMEM = pl.BlockSpec(memory_space=pltpu.VMEM)
SMEM = pl.BlockSpec(memory_space=pltpu.SMEM)
ANY = pl.BlockSpec(memory_space=pl.ANY)
PARAMS = pltpu.CompilerParams(vmem_limit_bytes=24 * 1024 * 1024)


def call(kernel, outs, args, specs, out_specs=None, scratch=(), flops=0, moved=0):
    return pl.pallas_call(
        kernel,
        out_shape=outs,
        in_specs=specs,
        out_specs=VMEM if out_specs is None else out_specs,
        scratch_shapes=list(scratch),
        compiler_params=PARAMS,
        cost_estimate=pl.CostEstimate(flops=flops, bytes_accessed=moved, transcendentals=0),
    )(*args)


def side_by_side(left, right, left_at, right_at):
    left, right = left.astype(F32), right.astype(F32)
    lane = lax.broadcasted_iota(jnp.int32, left.shape, 1)
    left = pltpu.roll(left, HALF, 1) if left_at else left
    right = right if right_at else pltpu.roll(right, HALF, 1)
    return jnp.where(lane < HALF, left, right).astype(BF16)


def pack_kernel(*refs):
    sources, (out, tagged), copies, done = refs[:5], refs[5:7], refs[7:12], refs[12]
    moves = [
        pltpu.make_async_copy(src, dst, done.at[i])
        for i, (src, dst) in enumerate(zip(sources, copies))
    ]
    for move in moves:
        move.start()
    for move in moves:
        move.wait()
    wq, wk, wv, tokens, flags = copies
    for part in range(NX):
        src = wk if part < 2 else wv
        at = HALF * (part % 2)
        packed = side_by_side(src[0:32, :], src[32:64, :], at, at)
        for copy in range(4):
            out[part, copy, 0:64, :] = wq[:, part * HEAD : (part + 1) * HEAD]
            out[part, copy, 64:96, :] = packed
    tagged[0:SEQ, :] = tokens[...]
    tagged[SEQ : SEQ + 16, :] = flags[...]


def norm_kernel(where, mine, other, gain, out):
    core = where[3]
    for row in range(NX):
        rows = pl.ds(pl.multiple_of(lax.rem(where[0] + row, NX) * SEQ, SEQ), SEQ)
        total = jnp.zeros((SEQ, HEAD), F32)
        for src in (mine, other):
            for y in range(4):
                for c in range(4):
                    feats = src[row, y, 0:SEQ, c * HEAD : (c + 1) * HEAD].astype(F32)
                    total = total + feats * feats
        power = jnp.sum(total, axis=-1, keepdims=True) * (1.0 / 4096.0)
        factor = lax.rsqrt(power + 1e-05)
        for src, side in ((mine, core), (other, 1 - core)):
            for y in range(4):
                slot = 2 * y + side
                feats = src[row, y, 0:SEQ, :].astype(F32)
                out[slot, rows, :] = (feats * factor * gain[slot]).astype(BF16)


def route_kernel(where, lists, place, use, units, table):
    x, z = where[0], where[1]

    def clear(i, carry):
        table[i] = 0
        return carry

    lax.fori_loop(0, NX * NZ, clear, 0)

    def fill(i, carry):
        row, pick = i // PICKS, i % PICKS
        at = place[lists[row * NZ + z, pick]]
        owner, local = at // 2, at % 2
        step = lax.rem(row - x + NX, NX) * 2
        bits = use[step, pick] + 2 * use[step + 1, pick]
        entry = row * NZ + owner % NZ
        mine = jnp.where(owner // NZ == x, 1, 0)
        table[entry] = table[entry] + mine * bits * jnp.where(local == 1, 4, 1)
        return carry

    lax.fori_loop(0, NX * PICKS, fill, 0)

    def compact(i, count):
        bits = table[i]
        units[count + 1] = i * 16 + bits
        return count + jnp.where(bits > 0, 1, 0)

    count = lax.fori_loop(0, NX * NZ, compact, 0)
    units[0] = count
    units[count + 1] = 0


def project_kernel(where, normed, near, ahead, far, behind, send, weights):
    lane_part = where[2]
    for step, blocks in enumerate((near, ahead, far, behind)):
        row = lax.rem(lane_part + step, 4) * HALF
        for b in range(16):
            block = blocks[b]
            base = pl.multiple_of(b * 256 + row, HALF)
            packed = block[64:96, :]
            weights[pl.ds(base, 64), 0:HEAD] = block[0:64, :]
            weights[pl.ds(base, 32), HEAD : 2 * HEAD] = packed
            weights[pl.ds(pl.multiple_of(base + 32, 32), 32), HEAD : 2 * HEAD] = pltpu.roll(
                packed.astype(F32), HALF, 1
            ).astype(BF16)
    total = jnp.zeros((ROWS, 2 * HEAD), F32)
    for slot in range(8):
        total = total + jnp.dot(
            normed[slot], weights[slot * 512 : (slot + 1) * 512, :], preferred_element_type=F32
        )
    query = total[:, 0:HEAD].astype(BF16)
    for dest in range(NX):
        own = total[dest * SEQ : (dest + 1) * SEQ, HEAD : 2 * HEAD]
        send[dest, 0:ROWS, :] = query
        send[dest, ROWS : ROWS + HALF, :] = side_by_side(own[0:HALF], own[HALF:SEQ], 0, 0)


def own_part(got, first):
    a, b = got[first, ROWS : ROWS + HALF, :], got[first + 1, ROWS : ROWS + HALF, :]
    return jnp.concatenate([side_by_side(a, b, 0, 0), side_by_side(a, b, HALF, HALF)], axis=0)


def queries(got, group):
    rows = pl.ds(pl.multiple_of(group * SEQ, SEQ), SEQ)
    return jnp.concatenate([got[head, rows, :] for head in range(RATIO)], axis=0)


def scores_of(keys, query):
    return lax.dot_general(keys, query, (((1,), (1,)), ((), ())), preferred_element_type=F32)


def own_scores(got, group):
    scores = scores_of(own_part(got, 0), queries(got, group))
    key_at = lax.broadcasted_iota(jnp.int32, (SEQ, COLS), 0)
    row_at = lax.broadcasted_iota(jnp.int32, (SEQ, COLS), 1) % SEQ
    return jnp.where(row_at >= key_at, scores, LOW)


def unit_scores(code, got, docs):
    entry, bits = code // 16, code % 16
    group, owner = entry // NZ, entry % NZ
    keys = docs[pl.ds(owner * 2, 2), :, 0:HEAD].reshape(2 * SEQ, HEAD)
    scores = scores_of(keys, queries(got, group))
    second = (lax.broadcasted_iota(jnp.int32, (1, COLS), 1) % SEQ) // HALF
    parts = []
    for local in range(2):
        use_a, use_b = (bits // (4**local)) % 2, (bits // (2 * 4**local)) % 2
        keep = jnp.where(second == 0, use_a, use_b) > 0
        parts.append((scores[local * SEQ : (local + 1) * SEQ], keep))
    return group, owner, parts


def weigh(scores, shift):
    return jnp.exp2((scores - shift) * RATE)


def stats_kernel(where, units, got, docs, send, stats):
    x = where[0]
    scores = own_scores(got, x)
    top = jnp.max(scores, axis=0, keepdims=True)
    stats[0:4, :] = jnp.full((4, COLS), LOW, F32)
    stats[4:8, :] = jnp.zeros((4, COLS), F32)
    stats[pl.ds(x, 1), :] = top
    stats[pl.ds(x + 4, 1), :] = jnp.sum(weigh(scores, top), axis=0, keepdims=True)

    def unit(code):
        group, _, parts = unit_scores(code, got, docs)
        tops = [jnp.where(keep, jnp.max(s, axis=0, keepdims=True), LOW) for s, keep in parts]
        top = jnp.maximum(tops[0], tops[1])
        sums = [
            jnp.sum(weigh(s, jnp.where(keep, top, -LOW)), axis=0, keepdims=True)
            for s, keep in parts
        ]
        return group, top, sums[0] + sums[1]

    def pair(i, carry):
        for group, top, part in [unit(units[2 * i + 1]), unit(units[2 * i + 2])]:
            before = stats[pl.ds(group, 1), :]
            new = jnp.maximum(before, top)
            old = stats[pl.ds(group + 4, 1), :] * weigh(before, new)
            stats[pl.ds(group, 1), :] = new
            stats[pl.ds(group + 4, 1), :] = old + part * weigh(top, new)
        return carry

    lax.fori_loop(0, (units[0] + 1) // 2, pair, 0)
    for dest in range(NX):
        send[dest] = stats[...]


def values_kernel(where, units, got, docs, all_stats, send, total):
    x = where[0]
    tops = [all_stats[src, 0:4, :] for src in range(NX)]
    top = jnp.maximum(jnp.maximum(tops[0], tops[1]), jnp.maximum(tops[2], tops[3]))
    sums = jnp.zeros((4, COLS), F32)
    for src in range(NX):
        sums = sums + all_stats[src, 4:8, :] * weigh(tops[src], top)
    total[0:4, :] = top
    total[4:8, :] = 1.0 / sums
    send[...] = jnp.zeros(send.shape, F32)

    def apply(values, probs):
        return lax.dot_general(values, probs, (((0,), (0,)), ((), ())), preferred_element_type=F32)

    own = weigh(own_scores(got, x), total[pl.ds(x, 1), :]) * total[pl.ds(x + 4, 1), :]
    send[pl.ds(x, 1)] = apply(own_part(got, 2), own.astype(BF16))[None]

    def unit(code):
        group, owner, parts = unit_scores(code, got, docs)
        top, inverse = total[pl.ds(group, 1), :], total[pl.ds(group + 4, 1), :]
        probs = [
            (weigh(s, jnp.where(keep, top, -LOW)) * inverse).astype(BF16) for s, keep in parts
        ]
        values = docs[pl.ds(owner * 2, 2), :, HEAD : 2 * HEAD].reshape(2 * SEQ, HEAD)
        return group, apply(values, jnp.concatenate(probs, axis=0))

    def pair(i, carry):
        for group, out in [unit(units[2 * i + 1]), unit(units[2 * i + 2])]:
            send[pl.ds(group, 1)] = send[pl.ds(group, 1)] + out[None]
        return carry

    lax.fori_loop(0, (units[0] + 1) // 2, pair, 0)


def finish_kernel(got, out):
    for head in range(RATIO):
        cols = slice(head * SEQ, (head + 1) * SEQ)
        total = (got[0, :, cols] + got[1, :, cols]) + (got[2, :, cols] + got[3, :, cols])
        out[:, cols] = total.T.astype(BF16)


def exchange(array, axes):
    return lax.all_to_all(array, axes, 0, 0, tiled=True)


def shards(tokens, norm_gain, wq, wk, wv, doc_cache, doc_lists, doc_place, block_use):
    shape = jax.ShapeDtypeStruct
    z_axes = ("zh", "zl")
    docs = lax.all_gather(doc_cache, z_axes, axis=0, tiled=True)
    x, zh, zl = lax.axis_index("x"), lax.axis_index("zh"), lax.axis_index("zl")
    where = jnp.stack([x, zh * 4 + zl, zl, lax.axis_index("core")]).astype(jnp.int32)

    flags = jnp.pad(block_use.astype(BF16), ((0, 14), (0, 512 - PICKS)))
    sources = (wq, wk, wv, tokens, flags)
    parts, tagged = call(
        pack_kernel,
        [shape((4, 4, 96, HEAD), BF16), shape((SEQ + 16, 512), BF16)],
        sources,
        [ANY] * 5,
        out_specs=[VMEM] * 2,
        scratch=[pltpu.VMEM(a.shape, BF16) for a in sources] + [pltpu.SemaphoreType.DMA((5,))],
    )
    near = exchange(parts.reshape(16, 96, HEAD), ("x", "zh"))

    def from_z(array, step):
        return lax.ppermute(array, z_axes, [((i + step) % NZ, i) for i in range(NZ)])

    def from_x(array, step):
        return lax.ppermute(array, "x", [((i + step) % NX, i) for i in range(NX)])

    by_y = lax.all_gather(tagged, "y")
    mine = jnp.concatenate([by_y, from_x(by_y, 1), from_x(by_y, 2), from_x(by_y, 3)])
    mine = mine.reshape(NX, 4, SEQ + 16, 512)
    ahead = from_z(near, 1)
    behind = from_z(near, -1)
    mine, ahead, behind = lax.optimization_barrier((mine, ahead, behind))
    other = lax.ppermute(mine, "core", [(0, 1), (1, 0)])
    gain = norm_gain.astype(F32).reshape(8, 1, 512)
    normed = call(
        norm_kernel,
        shape((8, ROWS, 512), BF16),
        (where, mine, other, gain),
        [SMEM, VMEM, VMEM, VMEM],
        flops=ROWS * 4096 * 8,
        moved=8 << 20,
    )
    use = mine[:, 0, SEQ : SEQ + 2, 0:PICKS].astype(jnp.int32).reshape(8, PICKS)
    units = call(
        route_kernel,
        shape((UNITS,), jnp.int32),
        (where, doc_lists, doc_place, use),
        [SMEM] * 4,
        out_specs=SMEM,
        scratch=[pltpu.SMEM((NX * NZ,), jnp.int32)],
    )

    far = from_z(ahead, 1)
    send = call(
        project_kernel,
        shape((NX, ROWS + HALF, HEAD), BF16),
        (where, normed, near, ahead, far, behind),
        [SMEM] + [VMEM] * 5,
        scratch=[pltpu.VMEM((4096, 2 * HEAD), BF16)],
        flops=2 * ROWS * 4096 * 256,
        moved=8 << 20,
    )
    got = exchange(send, "x")
    stats = call(
        stats_kernel,
        shape((NX, 8, COLS), F32),
        (where, units, got, docs),
        [SMEM, SMEM, VMEM, VMEM],
        scratch=[pltpu.VMEM((8, COLS), F32)],
    )
    all_stats = exchange(stats, "x")
    partial = call(
        values_kernel,
        shape((NX, HEAD, COLS), F32),
        (where, units, got, docs, all_stats),
        [SMEM, SMEM, VMEM, VMEM, VMEM],
        scratch=[pltpu.VMEM((8, COLS), F32)],
    )
    returned = exchange(partial, "x")
    return call(finish_kernel, shape((SEQ, COLS), BF16), (returned,), [VMEM])


def solution(mesh):
    fine = Mesh(mesh.devices.reshape(4, 4, 4, 4, 2), ("x", "zh", "zl", "y", "core"))
    pairs, tensor = ("x", "zh", "zl"), ("y", "core")
    placed = (
        P(pairs, tensor),
        P(),
        P(pairs, tensor),
        P(pairs, tensor),
        P(pairs, tensor),
        P(pairs, None, tensor),
        P(),
        P(),
        P(pairs, None),
    )
    return jax.shard_map(
        shards, mesh=fine, in_specs=placed, out_specs=P(pairs, tensor), check_vma=False
    )
```

```python
import math

import jax
import jax.numpy as jnp
from jax import lax
from jax.experimental import pallas as pl
from jax.experimental.pallas import tpu as pltpu
from jax.sharding import Mesh
from jax.sharding import PartitionSpec as P

F32 = jnp.float32
BF16 = jnp.bfloat16
HEAD = 128
HALF = 64
SEQ = 128
RATIO = 4
NX = 4
NZ = 16
PICKS = 16
ROWS = NX * SEQ
COLS = RATIO * SEQ
RATE = HEAD ** (-0.5) * math.log2(math.e)
LOW = -1e30
UNITS = 128

VMEM = pl.BlockSpec(memory_space=pltpu.VMEM)
SMEM = pl.BlockSpec(memory_space=pltpu.SMEM)
ANY = pl.BlockSpec(memory_space=pl.ANY)


def call(kernel, outs, args, specs, out_specs=None, scratch=(), flops=0, moved=0, limit=24):
    return pl.pallas_call(
        kernel,
        out_shape=outs,
        in_specs=specs,
        out_specs=VMEM if out_specs is None else out_specs,
        scratch_shapes=list(scratch),
        compiler_params=pltpu.CompilerParams(vmem_limit_bytes=limit * 1024 * 1024),
        cost_estimate=pl.CostEstimate(flops=flops, bytes_accessed=moved, transcendentals=0),
    )(*args)


def side_by_side(left, right, left_at, right_at):
    left, right = left.astype(F32), right.astype(F32)
    lane = lax.broadcasted_iota(jnp.int32, left.shape, 1)
    left = pltpu.roll(left, HALF, 1) if left_at else left
    right = right if right_at else pltpu.roll(right, HALF, 1)
    return jnp.where(lane < HALF, left, right).astype(BF16)


def pack_kernel(*refs):
    sources, use, (out, tagged), copies, flags, done = refs[:4], refs[4], refs[5:7], refs[7:11], refs[11], refs[12]
    moves = [
        pltpu.make_async_copy(src, dst, done.at[i])
        for i, (src, dst) in enumerate(zip(sources, copies))
    ]
    for move in moves:
        move.start()
    flags[...] = jnp.zeros(flags.shape, jnp.int32)
    flags[0:2, 0:PICKS] = use[...]
    tagged[SEQ : SEQ + 16, :] = flags[...].astype(F32).astype(BF16)
    for move in moves:
        move.wait()
    wq, wk, wv, tokens = copies
    tagged[0:SEQ, :] = tokens[...]
    for part in range(NX):
        src = wk if part < 2 else wv
        at = HALF * (part % 2)
        packed = side_by_side(src[0:32, :], src[32:64, :], at, at)
        for copy in range(4):
            out[part, copy, 0:64, :] = wq[:, part * HEAD : (part + 1) * HEAD]
            out[part, copy, 64:96, :] = packed


def norm_kernel(mine, other, gain, out):
    core = lax.axis_index("core")
    for row in range(NX):
        rows = pl.ds(pl.multiple_of(lax.rem(lax.axis_index("x") + row, NX) * SEQ, SEQ), SEQ)
        total = jnp.zeros((SEQ, HEAD), F32)
        for src in (mine, other):
            for y in range(4):
                for c in range(4):
                    feats = src[row, y, 0:SEQ, c * HEAD : (c + 1) * HEAD].astype(F32)
                    total = total + feats * feats
        power = jnp.sum(total, axis=-1, keepdims=True) * (1.0 / 4096.0)
        factor = lax.rsqrt(power + 1e-05)
        for src, side in ((mine, core), (other, 1 - core)):
            for y in range(4):
                slot = 2 * y + side
                feats = src[row, y, 0:SEQ, :].astype(F32)
                out[slot, rows, :] = (feats * factor * gain[slot]).astype(BF16)


def route_kernel(lists, place, use, units, table):
    x, z = lax.axis_index("x"), lax.axis_index("zh") * 4 + lax.axis_index("zl")

    def clear(i, carry):
        table[i] = 0
        return carry

    lax.fori_loop(0, NX * NZ, clear, 0)

    def fill(i, carry):
        row, pick = i // PICKS, i % PICKS
        at = place[lists[row * NZ + z, pick]]
        owner, local = at // 2, at % 2
        step = lax.rem(row - x + NX, NX) * 2
        bits = use[step, pick] + 2 * use[step + 1, pick]
        entry = row * NZ + owner % NZ
        mine = jnp.where(owner // NZ == x, 1, 0)
        table[entry] = table[entry] + mine * bits * jnp.where(local == 1, 4, 1)
        return carry

    lax.fori_loop(0, NX * PICKS, fill, 0)

    def compact(i, count):
        bits = table[i]
        units[count + 1] = i * 16 + bits
        return count + jnp.where(bits > 0, 1, 0)

    count = lax.fori_loop(0, NX * NZ, compact, 0)
    units[0] = count
    units[count + 1] = 0


def project_kernel(normed, near, ahead, far_a, far_b, behind, send, weights):
    for step, blocks in enumerate((near, ahead, (far_a, far_b), behind)):
        row = lax.rem(lax.axis_index("zl") + step, 4) * HALF
        for b in range(16):
            block = blocks[b // 8][b % 8] if step == 2 else blocks[b]
            base = pl.multiple_of(b * 256 + row, HALF)
            packed = block[64:96, :]
            weights[pl.ds(base, 64), 0:HEAD] = block[0:64, :]
            weights[pl.ds(base, 32), HEAD : 2 * HEAD] = packed
            weights[pl.ds(pl.multiple_of(base + 32, 32), 32), HEAD : 2 * HEAD] = pltpu.roll(
                packed.astype(F32), HALF, 1
            ).astype(BF16)
    total = jnp.zeros((ROWS, 2 * HEAD), F32)
    for slot in range(8):
        total = total + jnp.dot(
            normed[slot], weights[slot * 512 : (slot + 1) * 512, :], preferred_element_type=F32
        )
    query = total[:, 0:HEAD].astype(BF16)
    for dest in range(NX):
        own = total[dest * SEQ : (dest + 1) * SEQ, HEAD : 2 * HEAD]
        send[dest, 0:ROWS, :] = query
        send[dest, ROWS : ROWS + HALF, :] = side_by_side(own[0:HALF], own[HALF:SEQ], 0, 0)


def own_part(got, first):
    a, b = got[first, ROWS : ROWS + HALF, :], got[first + 1, ROWS : ROWS + HALF, :]
    return jnp.concatenate([side_by_side(a, b, 0, 0), side_by_side(a, b, HALF, HALF)], axis=0)


def queries(got, group):
    rows = pl.ds(pl.multiple_of(group * SEQ, SEQ), SEQ)
    return jnp.concatenate([got[head, rows, :] for head in range(RATIO)], axis=0)


def scores_of(keys, query):
    return lax.dot_general(keys, query, (((1,), (1,)), ((), ())), preferred_element_type=F32)


def own_scores(got, group):
    scores = scores_of(own_part(got, 0), queries(got, group))
    key_at = lax.broadcasted_iota(jnp.int32, (SEQ, COLS), 0)
    row_at = lax.broadcasted_iota(jnp.int32, (SEQ, COLS), 1) % SEQ
    return jnp.where(row_at >= key_at, scores, LOW)


def unit_scores(code, got, docs):
    entry, bits = code // 16, code % 16
    group, owner = entry // NZ, entry % NZ
    keys = docs[pl.ds(owner * 2, 2), :, 0:HEAD].reshape(2 * SEQ, HEAD)
    scores = scores_of(keys, queries(got, group))
    second = (lax.broadcasted_iota(jnp.int32, (1, COLS), 1) % SEQ) // HALF
    parts = []
    for local in range(2):
        use_a, use_b = (bits // (4**local)) % 2, (bits // (2 * 4**local)) % 2
        keep = jnp.where(second == 0, use_a, use_b) > 0
        parts.append((scores[local * SEQ : (local + 1) * SEQ], keep))
    return group, owner, parts


def weigh(scores, shift):
    return jnp.exp2((scores - shift) * RATE)


def stats_kernel(units, got, far_docs, send, stats, docs, done):
    fetch = pltpu.make_async_copy(far_docs, docs, done)
    fetch.start()
    x = lax.axis_index("x")
    scores = own_scores(got, x)
    top = jnp.max(scores, axis=0, keepdims=True)
    stats[0:4, :] = jnp.full((4, COLS), LOW, F32)
    stats[4:8, :] = jnp.zeros((4, COLS), F32)
    stats[pl.ds(x, 1), :] = top
    stats[pl.ds(x + 4, 1), :] = jnp.sum(weigh(scores, top), axis=0, keepdims=True)

    def unit(code):
        group, _, parts = unit_scores(code, got, docs)
        tops = [jnp.where(keep, jnp.max(s, axis=0, keepdims=True), LOW) for s, keep in parts]
        top = jnp.maximum(tops[0], tops[1])
        sums = [
            jnp.sum(weigh(s, jnp.where(keep, top, -LOW)), axis=0, keepdims=True)
            for s, keep in parts
        ]
        return group, top, sums[0] + sums[1]

    def pair(i, carry):
        for group, top, part in [unit(units[2 * i + 1]), unit(units[2 * i + 2])]:
            before = stats[pl.ds(group, 1), :]
            new = jnp.maximum(before, top)
            old = stats[pl.ds(group + 4, 1), :] * weigh(before, new)
            stats[pl.ds(group, 1), :] = new
            stats[pl.ds(group + 4, 1), :] = old + part * weigh(top, new)
        return carry

    fetch.wait()
    lax.fori_loop(0, (units[0] + 1) // 2, pair, 0)
    for dest in range(NX):
        send[dest] = stats[...]


def values_kernel(units, got, far_docs, all_stats, send, total, docs, done):
    fetch = pltpu.make_async_copy(far_docs, docs, done)
    fetch.start()
    x = lax.axis_index("x")
    tops = [all_stats[src, 0:4, :] for src in range(NX)]
    top = jnp.maximum(jnp.maximum(tops[0], tops[1]), jnp.maximum(tops[2], tops[3]))
    sums = jnp.zeros((4, COLS), F32)
    for src in range(NX):
        sums = sums + all_stats[src, 4:8, :] * weigh(tops[src], top)
    total[0:4, :] = top
    total[4:8, :] = 1.0 / sums
    send[...] = jnp.zeros(send.shape, F32)

    def apply(values, probs):
        return lax.dot_general(values, probs, (((0,), (0,)), ((), ())), preferred_element_type=F32)

    own = weigh(own_scores(got, x), total[pl.ds(x, 1), :]) * total[pl.ds(x + 4, 1), :]
    send[pl.ds(x, 1)] = apply(own_part(got, 2), own.astype(BF16))[None]

    def unit(code):
        group, owner, parts = unit_scores(code, got, docs)
        top, inverse = total[pl.ds(group, 1), :], total[pl.ds(group + 4, 1), :]
        probs = [
            (weigh(s, jnp.where(keep, top, -LOW)) * inverse).astype(BF16) for s, keep in parts
        ]
        values = docs[pl.ds(owner * 2, 2), :, HEAD : 2 * HEAD].reshape(2 * SEQ, HEAD)
        return group, apply(values, jnp.concatenate(probs, axis=0))

    def pair(i, carry):
        for group, out in [unit(units[2 * i + 1]), unit(units[2 * i + 2])]:
            send[pl.ds(group, 1)] = send[pl.ds(group, 1)] + out[None]
        return carry

    fetch.wait()
    lax.fori_loop(0, (units[0] + 1) // 2, pair, 0)


def finish_kernel(got, out):
    for head in range(RATIO):
        cols = slice(head * SEQ, (head + 1) * SEQ)
        total = (got[0, :, cols] + got[1, :, cols]) + (got[2, :, cols] + got[3, :, cols])
        out[:, cols] = total.T.astype(BF16)


def exchange(array, axes):
    return lax.all_to_all(array, axes, 0, 0, tiled=True)


def shards(tokens, norm_gain, wq, wk, wv, doc_cache, doc_lists, doc_place, block_use):
    shape = jax.ShapeDtypeStruct
    z_axes = ("zh", "zl")
    docs = lax.all_gather(doc_cache, z_axes, axis=0, tiled=True)

    sources = (wq, wk, wv, tokens)
    parts, tagged = call(
        pack_kernel,
        [shape((4, 4, 96, HEAD), BF16), shape((SEQ + 16, 512), BF16)],
        (*sources, block_use),
        [ANY] * 4 + [VMEM],
        out_specs=[VMEM] * 2,
        scratch=[pltpu.VMEM(a.shape, BF16) for a in sources]
        + [pltpu.VMEM((16, 512), jnp.int32), pltpu.SemaphoreType.DMA((4,))],
        limit=62,
    )
    near = exchange(parts.reshape(16, 96, HEAD), ("x", "zh"))

    def from_z(array, step):
        return lax.ppermute(array, z_axes, [((i + step) % NZ, i) for i in range(NZ)])

    def from_x(array, step):
        return lax.ppermute(array, "x", [((i + step) % NX, i) for i in range(NX)])

    by_y = lax.all_gather(tagged, "y")
    mine = jnp.concatenate([by_y, from_x(by_y, 1), from_x(by_y, 2), from_x(by_y, 3)])
    mine = mine.reshape(NX, 4, SEQ + 16, 512)
    ahead = from_z(near, 1)
    behind = from_z(near, -1)
    far_a = from_z(near[0:8], 2)
    far_b = from_z(near[8:16], -2)
    mine, ahead, behind, far_a, far_b = lax.optimization_barrier((mine, ahead, behind, far_a, far_b))
    other = lax.ppermute(mine, "core", [(0, 1), (1, 0)])
    gain = norm_gain.astype(F32).reshape(8, 1, 512)
    normed = call(
        norm_kernel,
        shape((8, ROWS, 512), BF16),
        (mine, other, gain),
        [VMEM] * 3,
        flops=ROWS * 4096 * 8,
        moved=8 << 20,
    )
    use = mine[:, 0, SEQ : SEQ + 2, 0:PICKS].astype(jnp.int32).reshape(8, PICKS)
    units = call(
        route_kernel,
        shape((UNITS,), jnp.int32),
        (doc_lists, doc_place, use),
        [SMEM] * 3,
        out_specs=SMEM,
        scratch=[pltpu.SMEM((NX * NZ,), jnp.int32)],
    )

    send = call(
        project_kernel,
        shape((NX, ROWS + HALF, HEAD), BF16),
        (normed, near, ahead, far_a, far_b, behind),
        [VMEM] * 6,
        scratch=[pltpu.VMEM((4096, 2 * HEAD), BF16)],
        flops=2 * ROWS * 4096 * 256,
        moved=8 << 20,
    )
    got = exchange(send, "x")
    scratch = [
        pltpu.VMEM((8, COLS), F32),
        pltpu.VMEM((2 * NZ, SEQ, 2 * HEAD), BF16),
        pltpu.SemaphoreType.DMA,
    ]
    stats = call(
        stats_kernel,
        shape((NX, 8, COLS), F32),
        (units, got, docs),
        [SMEM, VMEM, ANY],
        scratch=scratch,
        limit=52,
    )
    all_stats = exchange(stats, "x")
    partial = call(
        values_kernel,
        shape((NX, HEAD, COLS), F32),
        (units, got, docs, all_stats),
        [SMEM, VMEM, ANY, VMEM],
        scratch=scratch,
        limit=52,
    )
    returned = exchange(partial, "x")
    return call(finish_kernel, shape((SEQ, COLS), BF16), (returned,), [VMEM])


def solution(mesh):
    fine = Mesh(mesh.devices.reshape(4, 4, 4, 4, 2), ("x", "zh", "zl", "y", "core"))
    pairs, tensor = ("x", "zh", "zl"), ("y", "core")
    placed = (
        P(pairs, tensor),
        P(),
        P(pairs, tensor),
        P(pairs, tensor),
        P(pairs, tensor),
        P(pairs, None, tensor),
        P(),
        P(),
        P(pairs, None),
    )
    return jax.shard_map(
        shards, mesh=fine, in_specs=placed, out_specs=P(pairs, tensor), check_vma=False
    )
```

```python
import math

import jax
import jax.numpy as jnp
from jax import lax
from jax.experimental import pallas as pl
from jax.experimental.pallas import tpu as pltpu
from jax.sharding import Mesh
from jax.sharding import PartitionSpec as P

F32 = jnp.float32
BF16 = jnp.bfloat16
HEAD = 128
HALF = 64
SEQ = 128
RATIO = 4
NX = 4
NZ = 16
PICKS = 16
ROWS = NX * SEQ
COLS = RATIO * SEQ
RATE = HEAD ** (-0.5) * math.log2(math.e)
LOW = -1e30
UNITS = 128

VMEM = pl.BlockSpec(memory_space=pltpu.VMEM)
SMEM = pl.BlockSpec(memory_space=pltpu.SMEM)
ANY = pl.BlockSpec(memory_space=pl.ANY)


def call(kernel, outs, args, specs, out_specs=None, scratch=(), flops=0, moved=0, limit=24):
    return pl.pallas_call(
        kernel,
        out_shape=outs,
        in_specs=specs,
        out_specs=VMEM if out_specs is None else out_specs,
        scratch_shapes=list(scratch),
        compiler_params=pltpu.CompilerParams(vmem_limit_bytes=limit * 1024 * 1024),
        cost_estimate=pl.CostEstimate(flops=flops, bytes_accessed=moved, transcendentals=0),
    )(*args)


def side_by_side(left, right, left_at, right_at):
    left, right = left.astype(F32), right.astype(F32)
    lane = lax.broadcasted_iota(jnp.int32, left.shape, 1)
    left = pltpu.roll(left, HALF, 1) if left_at else left
    right = right if right_at else pltpu.roll(right, HALF, 1)
    return jnp.where(lane < HALF, left, right).astype(BF16)


def pack_kernel(*refs):
    sources, use, (out, tagged), copies, flags, done = refs[:4], refs[4], refs[5:7], refs[7:11], refs[11], refs[12]
    moves = [
        pltpu.make_async_copy(src, dst, done.at[i])
        for i, (src, dst) in enumerate(zip(sources, copies))
    ]
    for move in moves:
        move.start()
    flags[...] = jnp.zeros(flags.shape, jnp.int32)
    flags[0:2, 0:PICKS] = use[...]
    tagged[SEQ : SEQ + 16, :] = flags[...].astype(F32).astype(BF16)
    for move in moves:
        move.wait()
    wq, wk, wv, tokens = copies
    tagged[0:SEQ, :] = tokens[...]
    for part in range(NX):
        src = wk if part < 2 else wv
        at = HALF * (part % 2)
        packed = side_by_side(src[0:32, :], src[32:64, :], at, at)
        for copy in range(4):
            out[part, copy, 0:64, :] = wq[:, part * HEAD : (part + 1) * HEAD]
            out[part, copy, 64:96, :] = packed


def norm_kernel(mine, other, gain, out):
    core = lax.axis_index("core")
    for row in range(NX):
        rows = pl.ds(pl.multiple_of(lax.rem(lax.axis_index("x") + row, NX) * SEQ, SEQ), SEQ)
        total = jnp.zeros((SEQ, HEAD), F32)
        for src in (mine, other):
            for y in range(4):
                for c in range(4):
                    feats = src[row, y, 0:SEQ, c * HEAD : (c + 1) * HEAD].astype(F32)
                    total = total + feats * feats
        power = jnp.sum(total, axis=-1, keepdims=True) * (1.0 / 4096.0)
        factor = lax.rsqrt(power + 1e-05)
        for src, side in ((mine, core), (other, 1 - core)):
            for y in range(4):
                slot = 2 * y + side
                feats = src[row, y, 0:SEQ, :].astype(F32)
                out[slot, rows, :] = (feats * factor * gain[slot]).astype(BF16)


def route_kernel(lists, place, use, units, table):
    x, z = lax.axis_index("x"), lax.axis_index("zh") * 4 + lax.axis_index("zl")

    def clear(i, carry):
        table[i] = 0
        return carry

    lax.fori_loop(0, NX * NZ, clear, 0)

    def fill(i, carry):
        row, pick = i // PICKS, i % PICKS
        at = place[lists[row * NZ + z, pick]]
        owner, local = at // 2, at % 2
        step = lax.rem(row - x + NX, NX) * 2
        bits = use[step, pick] + 2 * use[step + 1, pick]
        entry = row * NZ + owner % NZ
        mine = jnp.where(owner // NZ == x, 1, 0)
        table[entry] = table[entry] + mine * bits * jnp.where(local == 1, 4, 1)
        return carry

    lax.fori_loop(0, NX * PICKS, fill, 0)

    def compact(i, count):
        bits = table[i]
        units[count + 1] = i * 16 + bits
        return count + jnp.where(bits > 0, 1, 0)

    count = lax.fori_loop(0, NX * NZ, compact, 0)
    units[0] = count
    units[count + 1] = 0


def project_kernel(normed, near, ahead, far, behind, *rest):
    sends, weights, owns = rest[:NX], rest[NX], rest[NX + 1]
    for step, blocks in enumerate((near, ahead, far, behind)):
        row = lax.rem(lax.axis_index("zl") + step, 4) * HALF
        for b in range(16):
            block = blocks[b]
            base = pl.multiple_of(b * 256 + row, HALF)
            packed = block[64:96, :]
            weights[pl.ds(base, 64), 0:HEAD] = block[0:64, :]
            weights[pl.ds(base, 32), HEAD : 2 * HEAD] = packed
            weights[pl.ds(pl.multiple_of(base + 32, 32), 32), HEAD : 2 * HEAD] = pltpu.roll(
                packed.astype(F32), HALF, 1
            ).astype(BF16)
    total = jnp.zeros((ROWS, 2 * HEAD), F32)
    for slot in range(8):
        total = total + jnp.dot(
            normed[slot], weights[slot * 512 : (slot + 1) * 512, :], preferred_element_type=F32
        )
    query = total[:, 0:HEAD].astype(BF16)
    owns[...] = total[:, HEAD : 2 * HEAD]
    for step, send in enumerate(sends):
        dest = lax.rem(lax.axis_index("x") + step, NX)
        own = owns[pl.ds(pl.multiple_of(dest * SEQ, SEQ), SEQ), :]
        send[0:ROWS, :] = query
        send[ROWS : ROWS + HALF, :] = side_by_side(own[0:HALF], own[HALF:SEQ], 0, 0)


def own_part(got, first):
    a, b = got[first, ROWS : ROWS + HALF, :], got[first + 1, ROWS : ROWS + HALF, :]
    return jnp.concatenate([side_by_side(a, b, 0, 0), side_by_side(a, b, HALF, HALF)], axis=0)


def queries(got, group):
    rows = pl.ds(pl.multiple_of(group * SEQ, SEQ), SEQ)
    return jnp.concatenate([got[head, rows, :] for head in range(RATIO)], axis=0)


def scores_of(keys, query):
    return lax.dot_general(keys, query, (((1,), (1,)), ((), ())), preferred_element_type=F32)


def own_scores(got, group):
    scores = scores_of(own_part(got, 0), queries(got, group))
    key_at = lax.broadcasted_iota(jnp.int32, (SEQ, COLS), 0)
    row_at = lax.broadcasted_iota(jnp.int32, (SEQ, COLS), 1) % SEQ
    return jnp.where(row_at >= key_at, scores, LOW)


def unit_scores(code, got, docs):
    entry, bits = code // 16, code % 16
    group, owner = entry // NZ, entry % NZ
    keys = docs[pl.ds(owner * 2, 2), :, 0:HEAD].reshape(2 * SEQ, HEAD)
    scores = scores_of(keys, queries(got, group))
    second = (lax.broadcasted_iota(jnp.int32, (1, COLS), 1) % SEQ) // HALF
    parts = []
    for local in range(2):
        use_a, use_b = (bits // (4**local)) % 2, (bits // (2 * 4**local)) % 2
        keep = jnp.where(second == 0, use_a, use_b) > 0
        parts.append((scores[local * SEQ : (local + 1) * SEQ], keep))
    return group, owner, parts


def weigh(scores, shift):
    return jnp.exp2((scores - shift) * RATE)


def in_order(pieces, got):
    for step, piece in enumerate(pieces):
        got[lax.rem(lax.axis_index("x") - step + NX, NX)] = piece[...]


def stats_kernel(units, own, one, two, three, far_docs, send, stats, docs, got, done):
    fetch = pltpu.make_async_copy(far_docs, docs, done)
    fetch.start()
    in_order((own, one, two, three), got)
    x = lax.axis_index("x")
    scores = own_scores(got, x)
    top = jnp.max(scores, axis=0, keepdims=True)
    stats[0:4, :] = jnp.full((4, COLS), LOW, F32)
    stats[4:8, :] = jnp.zeros((4, COLS), F32)
    stats[pl.ds(x, 1), :] = top
    stats[pl.ds(x + 4, 1), :] = jnp.sum(weigh(scores, top), axis=0, keepdims=True)

    def unit(code):
        group, _, parts = unit_scores(code, got, docs)
        tops = [jnp.where(keep, jnp.max(s, axis=0, keepdims=True), LOW) for s, keep in parts]
        top = jnp.maximum(tops[0], tops[1])
        sums = [
            jnp.sum(weigh(s, jnp.where(keep, top, -LOW)), axis=0, keepdims=True)
            for s, keep in parts
        ]
        return group, top, sums[0] + sums[1]

    def pair(i, carry):
        for group, top, part in [unit(units[2 * i + 1]), unit(units[2 * i + 2])]:
            before = stats[pl.ds(group, 1), :]
            new = jnp.maximum(before, top)
            old = stats[pl.ds(group + 4, 1), :] * weigh(before, new)
            stats[pl.ds(group, 1), :] = new
            stats[pl.ds(group + 4, 1), :] = old + part * weigh(top, new)
        return carry

    fetch.wait()
    lax.fori_loop(0, (units[0] + 1) // 2, pair, 0)
    for dest in range(NX):
        send[dest] = stats[...]


def values_kernel(units, own, one, two, three, far_docs, all_stats, send, total, docs, got, done):
    fetch = pltpu.make_async_copy(far_docs, docs, done)
    fetch.start()
    in_order((own, one, two, three), got)
    x = lax.axis_index("x")
    tops = [all_stats[src, 0:4, :] for src in range(NX)]
    top = jnp.maximum(jnp.maximum(tops[0], tops[1]), jnp.maximum(tops[2], tops[3]))
    sums = jnp.zeros((4, COLS), F32)
    for src in range(NX):
        sums = sums + all_stats[src, 4:8, :] * weigh(tops[src], top)
    total[0:4, :] = top
    total[4:8, :] = 1.0 / sums
    send[...] = jnp.zeros(send.shape, F32)

    def apply(values, probs):
        return lax.dot_general(values, probs, (((0,), (0,)), ((), ())), preferred_element_type=F32)

    own = weigh(own_scores(got, x), total[pl.ds(x, 1), :]) * total[pl.ds(x + 4, 1), :]
    send[pl.ds(x, 1)] = apply(own_part(got, 2), own.astype(BF16))[None]

    def unit(code):
        group, owner, parts = unit_scores(code, got, docs)
        top, inverse = total[pl.ds(group, 1), :], total[pl.ds(group + 4, 1), :]
        probs = [
            (weigh(s, jnp.where(keep, top, -LOW)) * inverse).astype(BF16) for s, keep in parts
        ]
        values = docs[pl.ds(owner * 2, 2), :, HEAD : 2 * HEAD].reshape(2 * SEQ, HEAD)
        return group, apply(values, jnp.concatenate(probs, axis=0))

    def pair(i, carry):
        for group, out in [unit(units[2 * i + 1]), unit(units[2 * i + 2])]:
            send[pl.ds(group, 1)] = send[pl.ds(group, 1)] + out[None]
        return carry

    fetch.wait()
    lax.fori_loop(0, (units[0] + 1) // 2, pair, 0)


def finish_kernel(got, out):
    for head in range(RATIO):
        cols = slice(head * SEQ, (head + 1) * SEQ)
        total = (got[0, :, cols] + got[1, :, cols]) + (got[2, :, cols] + got[3, :, cols])
        out[:, cols] = total.T.astype(BF16)


def exchange(array, axes):
    return lax.all_to_all(array, axes, 0, 0, tiled=True)


def shards(tokens, norm_gain, wq, wk, wv, doc_cache, doc_lists, doc_place, block_use):
    shape = jax.ShapeDtypeStruct
    z_axes = ("zh", "zl")
    docs = lax.all_gather(doc_cache, z_axes, axis=0, tiled=True)

    sources = (wq, wk, wv, tokens)
    parts, tagged = call(
        pack_kernel,
        [shape((4, 4, 96, HEAD), BF16), shape((SEQ + 16, 512), BF16)],
        (*sources, block_use),
        [ANY] * 4 + [VMEM],
        out_specs=[VMEM] * 2,
        scratch=[pltpu.VMEM(a.shape, BF16) for a in sources]
        + [pltpu.VMEM((16, 512), jnp.int32), pltpu.SemaphoreType.DMA((4,))],
        limit=62,
    )
    near = exchange(parts.reshape(16, 96, HEAD), ("x", "zh"))

    def from_z(array, step):
        return lax.ppermute(array, z_axes, [((i + step) % NZ, i) for i in range(NZ)])

    def from_x(array, step):
        return lax.ppermute(array, "x", [((i + step) % NX, i) for i in range(NX)])

    by_y = lax.all_gather(tagged, "y")
    mine = jnp.concatenate([by_y, from_x(by_y, 1), from_x(by_y, 2), from_x(by_y, 3)])
    mine = mine.reshape(NX, 4, SEQ + 16, 512)
    ahead = from_z(near, 1)
    behind = from_z(near, -1)
    far = lax.ppermute(near, z_axes, [((i + 2 - 4 * (i % 2)) % NZ, i) for i in range(NZ)])
    mine, ahead, far, behind = lax.optimization_barrier((mine, ahead, far, behind))
    other = lax.ppermute(mine, "core", [(0, 1), (1, 0)])
    gain = norm_gain.astype(F32).reshape(8, 1, 512)
    normed = call(
        norm_kernel,
        shape((8, ROWS, 512), BF16),
        (mine, other, gain),
        [VMEM] * 3,
        flops=ROWS * 4096 * 8,
        moved=8 << 20,
    )
    use = mine[:, 0, SEQ : SEQ + 2, 0:PICKS].astype(jnp.int32).reshape(8, PICKS)
    units = call(
        route_kernel,
        shape((UNITS,), jnp.int32),
        (doc_lists, doc_place, use),
        [SMEM] * 3,
        out_specs=SMEM,
        scratch=[pltpu.SMEM((NX * NZ,), jnp.int32)],
    )

    sends = call(
        project_kernel,
        [shape((ROWS + HALF, HEAD), BF16)] * NX,
        (normed, near, ahead, far, behind),
        [VMEM] * 5,
        out_specs=[VMEM] * NX,
        scratch=[pltpu.VMEM((4096, 2 * HEAD), BF16), pltpu.VMEM((ROWS, HEAD), F32)],
        flops=2 * ROWS * 4096 * 256,
        moved=8 << 20,
    )
    got = [
        lax.ppermute(sends[k], "x", [(i, (i + k) % NX) for i in range(NX)]) if k else sends[0]
        for k in range(NX)
    ]
    scratch = [
        pltpu.VMEM((8, COLS), F32),
        pltpu.VMEM((2 * NZ, SEQ, 2 * HEAD), BF16),
        pltpu.VMEM((NX, ROWS + HALF, HEAD), BF16),
        pltpu.SemaphoreType.DMA,
    ]
    stats = call(
        stats_kernel,
        shape((NX, 8, COLS), F32),
        (units, *got, docs),
        [SMEM] + [VMEM] * 4 + [ANY],
        scratch=scratch,
        limit=52,
    )
    all_stats = exchange(stats, "x")
    partial = call(
        values_kernel,
        shape((NX, HEAD, COLS), F32),
        (units, *got, docs, all_stats),
        [SMEM] + [VMEM] * 4 + [ANY, VMEM],
        scratch=scratch,
        limit=52,
    )
    returned = exchange(partial, "x")
    return call(finish_kernel, shape((SEQ, COLS), BF16), (returned,), [VMEM])


def solution(mesh):
    fine = Mesh(mesh.devices.reshape(4, 4, 4, 4, 2), ("x", "zh", "zl", "y", "core"))
    pairs, tensor = ("x", "zh", "zl"), ("y", "core")
    placed = (
        P(pairs, tensor),
        P(),
        P(pairs, tensor),
        P(pairs, tensor),
        P(pairs, tensor),
        P(pairs, None, tensor),
        P(),
        P(),
        P(pairs, None),
    )
    return jax.shard_map(
        shards, mesh=fine, in_specs=placed, out_specs=P(pairs, tensor), check_vma=False
    )
```

```python
import math

import jax
import jax.numpy as jnp
from jax import lax
from jax.experimental import pallas as pl
from jax.experimental.pallas import tpu as pltpu
from jax.sharding import Mesh
from jax.sharding import PartitionSpec as P

F32 = jnp.float32
BF16 = jnp.bfloat16
HEAD = 128
HALF = 64
SEQ = 128
RATIO = 4
NX = 4
NZ = 16
PICKS = 16
ROWS = NX * SEQ
COLS = RATIO * SEQ
RATE = HEAD ** (-0.5) * math.log2(math.e)
LOW = -1e30
UNITS = 128

VMEM = pl.BlockSpec(memory_space=pltpu.VMEM)
SMEM = pl.BlockSpec(memory_space=pltpu.SMEM)
ANY = pl.BlockSpec(memory_space=pl.ANY)


def call(kernel, outs, args, specs, out_specs=None, scratch=(), flops=0, moved=0, limit=24):
    return pl.pallas_call(
        kernel,
        out_shape=outs,
        in_specs=specs,
        out_specs=VMEM if out_specs is None else out_specs,
        scratch_shapes=list(scratch),
        compiler_params=pltpu.CompilerParams(vmem_limit_bytes=limit * 1024 * 1024),
        cost_estimate=pl.CostEstimate(flops=flops, bytes_accessed=moved, transcendentals=0),
    )(*args)


def side_by_side(left, right, left_at, right_at):
    left, right = left.astype(F32), right.astype(F32)
    lane = lax.broadcasted_iota(jnp.int32, left.shape, 1)
    left = pltpu.roll(left, HALF, 1) if left_at else left
    right = right if right_at else pltpu.roll(right, HALF, 1)
    return jnp.where(lane < HALF, left, right).astype(BF16)


def pack_kernel(*refs):
    sources, use, (out, tagged), copies, flags, done = refs[:4], refs[4], refs[5:7], refs[7:11], refs[11], refs[12]
    moves = [
        pltpu.make_async_copy(src, dst, done.at[i])
        for i, (src, dst) in enumerate(zip(sources, copies))
    ]
    for move in moves:
        move.start()
    flags[...] = jnp.zeros(flags.shape, jnp.int32)
    flags[0:2, 0:PICKS] = use[...]
    tagged[SEQ : SEQ + 16, :] = flags[...].astype(F32).astype(BF16)
    for move in moves:
        move.wait()
    wq, wk, wv, tokens = copies
    tagged[0:SEQ, :] = tokens[...]
    for part in range(NX):
        src = wk if part < 2 else wv
        at = HALF * (part % 2)
        packed = side_by_side(src[0:32, :], src[32:64, :], at, at)
        for copy in range(4):
            out[part, copy, 0:64, :] = wq[:, part * HEAD : (part + 1) * HEAD]
            out[part, copy, 64:96, :] = packed


def norm_kernel(mine, other, gain, out):
    core = lax.axis_index("core")
    for row in range(NX):
        rows = pl.ds(pl.multiple_of(lax.rem(lax.axis_index("x") + row, NX) * SEQ, SEQ), SEQ)
        total = jnp.zeros((SEQ, HEAD), F32)
        for src in (mine, other):
            for y in range(4):
                for c in range(4):
                    feats = src[row, y, 0:SEQ, c * HEAD : (c + 1) * HEAD].astype(F32)
                    total = total + feats * feats
        power = jnp.sum(total, axis=-1, keepdims=True) * (1.0 / 4096.0)
        factor = lax.rsqrt(power + 1e-05)
        for src, side in ((mine, core), (other, 1 - core)):
            for y in range(4):
                slot = 2 * y + side
                feats = src[row, y, 0:SEQ, :].astype(F32)
                out[slot, rows, :] = (feats * factor * gain[slot]).astype(BF16)


def route_kernel(lists, place, use, units, table):
    x, z = lax.axis_index("x"), lax.axis_index("zh") * 4 + lax.axis_index("zl")

    def clear(i, carry):
        table[i] = 0
        return carry

    lax.fori_loop(0, NX * NZ, clear, 0)

    def fill(i, carry):
        row, pick = i // PICKS, i % PICKS
        at = place[lists[row * NZ + z, pick]]
        owner, local = at // 2, at % 2
        step = lax.rem(row - x + NX, NX) * 2
        bits = use[step, pick] + 2 * use[step + 1, pick]
        entry = row * NZ + owner % NZ
        mine = jnp.where(owner // NZ == x, 1, 0)
        table[entry] = table[entry] + mine * bits * jnp.where(local == 1, 4, 1)
        return carry

    lax.fori_loop(0, NX * PICKS, fill, 0)

    def compact(i, count):
        bits = table[i]
        units[count + 1] = i * 16 + bits
        return count + jnp.where(bits > 0, 1, 0)

    count = lax.fori_loop(0, NX * NZ, compact, 0)
    units[0] = count
    for step in range(1, 4):
        units[count + step] = 0


def project_kernel(normed, near, ahead, far, behind, *rest):
    sends, weights, owns = rest[:NX], rest[NX], rest[NX + 1]
    for step, blocks in enumerate((near, ahead, far, behind)):
        row = lax.rem(lax.axis_index("zl") + step, 4) * HALF
        for b in range(16):
            block = blocks[b]
            base = pl.multiple_of(b * 256 + row, HALF)
            packed = block[64:96, :]
            weights[pl.ds(base, 64), 0:HEAD] = block[0:64, :]
            weights[pl.ds(base, 32), HEAD : 2 * HEAD] = packed
            weights[pl.ds(pl.multiple_of(base + 32, 32), 32), HEAD : 2 * HEAD] = pltpu.roll(
                packed.astype(F32), HALF, 1
            ).astype(BF16)
    total = jnp.zeros((ROWS, 2 * HEAD), F32)
    for slot in range(8):
        total = total + jnp.dot(
            normed[slot], weights[slot * 512 : (slot + 1) * 512, :], preferred_element_type=F32
        )
    query = total[:, 0:HEAD].astype(BF16)
    owns[...] = total[:, HEAD : 2 * HEAD]
    for step, send in enumerate(sends):
        dest = lax.rem(lax.axis_index("x") + step, NX)
        own = owns[pl.ds(pl.multiple_of(dest * SEQ, SEQ), SEQ), :]
        send[0:ROWS, :] = query
        send[ROWS : ROWS + HALF, :] = side_by_side(own[0:HALF], own[HALF:SEQ], 0, 0)


def own_part(got, first):
    a, b = got[first, ROWS : ROWS + HALF, :], got[first + 1, ROWS : ROWS + HALF, :]
    return jnp.concatenate([side_by_side(a, b, 0, 0), side_by_side(a, b, HALF, HALF)], axis=0)


def queries(got, group):
    rows = pl.ds(pl.multiple_of(group * SEQ, SEQ), SEQ)
    return jnp.concatenate([got[head, rows, :] for head in range(RATIO)], axis=0)


def scores_of(keys, query):
    return lax.dot_general(keys, query, (((1,), (1,)), ((), ())), preferred_element_type=F32)


def own_scores(got, group):
    scores = scores_of(own_part(got, 0), queries(got, group))
    key_at = lax.broadcasted_iota(jnp.int32, (SEQ, COLS), 0)
    row_at = lax.broadcasted_iota(jnp.int32, (SEQ, COLS), 1) % SEQ
    return jnp.where(row_at >= key_at, scores, LOW)


def unit_scores(code, got, docs):
    entry, bits = code // 16, code % 16
    group, owner = entry // NZ, entry % NZ
    keys = docs[pl.ds(owner * 2, 2), :, 0:HEAD].reshape(2 * SEQ, HEAD)
    scores = scores_of(keys, queries(got, group))
    second = (lax.broadcasted_iota(jnp.int32, (1, COLS), 1) % SEQ) // HALF
    parts = []
    for local in range(2):
        use_a, use_b = (bits // (4**local)) % 2, (bits // (2 * 4**local)) % 2
        keep = jnp.where(second == 0, use_a, use_b) > 0
        parts.append((scores[local * SEQ : (local + 1) * SEQ], keep))
    return group, owner, parts


def weigh(scores, shift):
    return jnp.exp2((scores - shift) * RATE)


def in_order(pieces, got):
    for step, piece in enumerate(pieces):
        got[lax.rem(lax.axis_index("x") - step + NX, NX)] = piece[...]


def stats_kernel(units, own, one, two, three, far_docs, send, stats, docs, got, done):
    fetch = pltpu.make_async_copy(far_docs.at[:, :, 0:HEAD], docs, done)
    fetch.start()
    in_order((own, one, two, three), got)
    x = lax.axis_index("x")
    scores = own_scores(got, x)
    top = jnp.max(scores, axis=0, keepdims=True)
    stats[0:4, :] = jnp.full((4, COLS), LOW, F32)
    stats[4:8, :] = jnp.zeros((4, COLS), F32)
    stats[pl.ds(x, 1), :] = top
    stats[pl.ds(x + 4, 1), :] = jnp.sum(weigh(scores, top), axis=0, keepdims=True)

    def unit(code):
        group, _, parts = unit_scores(code, got, docs)
        tops = [jnp.where(keep, jnp.max(s, axis=0, keepdims=True), LOW) for s, keep in parts]
        top = jnp.maximum(tops[0], tops[1])
        sums = [
            jnp.sum(weigh(s, jnp.where(keep, top, -LOW)), axis=0, keepdims=True)
            for s, keep in parts
        ]
        return group, top, sums[0] + sums[1]

    def pair(i, carry):
        for group, top, part in [unit(units[4 * i + j]) for j in range(1, 5)]:
            before = stats[pl.ds(group, 1), :]
            new = jnp.maximum(before, top)
            old = stats[pl.ds(group + 4, 1), :] * weigh(before, new)
            stats[pl.ds(group, 1), :] = new
            stats[pl.ds(group + 4, 1), :] = old + part * weigh(top, new)
        return carry

    fetch.wait()
    lax.fori_loop(0, (units[0] + 3) // 4, pair, 0)
    for dest in range(NX):
        send[dest] = stats[...]


def values_kernel(units, own, one, two, three, docs, all_stats, send, total, got):
    in_order((own, one, two, three), got)
    x = lax.axis_index("x")
    tops = [all_stats[src, 0:4, :] for src in range(NX)]
    top = jnp.maximum(jnp.maximum(tops[0], tops[1]), jnp.maximum(tops[2], tops[3]))
    sums = jnp.zeros((4, COLS), F32)
    for src in range(NX):
        sums = sums + all_stats[src, 4:8, :] * weigh(tops[src], top)
    total[0:4, :] = top
    total[4:8, :] = top * RATE + jnp.log2(sums)
    send[...] = jnp.zeros(send.shape, F32)

    def apply(values, probs):
        return lax.dot_general(values, probs, (((0,), (0,)), ((), ())), preferred_element_type=F32)

    own = jnp.exp2(own_scores(got, x) * RATE - total[pl.ds(x + 4, 1), :])
    send[pl.ds(x, 1)] = apply(own_part(got, 2), own.astype(BF16))[None]

    def unit(code):
        group, owner, parts = unit_scores(code, got, docs)
        shift = total[pl.ds(group + 4, 1), :]
        probs = [
            jnp.exp2(s * RATE - jnp.where(keep, shift, -LOW)).astype(BF16) for s, keep in parts
        ]
        values = docs[pl.ds(owner * 2, 2), :, HEAD : 2 * HEAD].reshape(2 * SEQ, HEAD)
        return group, apply(values, jnp.concatenate(probs, axis=0))

    def pair(i, carry):
        for group, out in [unit(units[4 * i + j]) for j in range(1, 5)]:
            send[pl.ds(group, 1)] = send[pl.ds(group, 1)] + out[None]
        return carry

    lax.fori_loop(0, (units[0] + 3) // 4, pair, 0)


def finish_kernel(got, out):
    for head in range(RATIO):
        cols = slice(head * SEQ, (head + 1) * SEQ)
        total = (got[0, :, cols] + got[1, :, cols]) + (got[2, :, cols] + got[3, :, cols])
        out[:, cols] = total.T.astype(BF16)


def exchange(array, axes):
    return lax.all_to_all(array, axes, 0, 0, tiled=True)


def shards(tokens, norm_gain, wq, wk, wv, doc_cache, doc_lists, doc_place, block_use):
    shape = jax.ShapeDtypeStruct
    z_axes = ("zh", "zl")
    docs = lax.all_gather(doc_cache, z_axes, axis=0, tiled=True)

    sources = (wq, wk, wv, tokens)
    parts, tagged = call(
        pack_kernel,
        [shape((4, 4, 96, HEAD), BF16), shape((SEQ + 16, 512), BF16)],
        (*sources, block_use),
        [ANY] * 4 + [VMEM],
        out_specs=[VMEM] * 2,
        scratch=[pltpu.VMEM(a.shape, BF16) for a in sources]
        + [pltpu.VMEM((16, 512), jnp.int32), pltpu.SemaphoreType.DMA((4,))],
        limit=62,
    )
    near = exchange(parts.reshape(16, 96, HEAD), ("x", "zh"))

    def from_z(array, step):
        return lax.ppermute(array, z_axes, [((i + step) % NZ, i) for i in range(NZ)])

    def from_x(array, step):
        return lax.ppermute(array, "x", [((i + step) % NX, i) for i in range(NX)])

    by_y = lax.all_gather(tagged, "y")
    mine = jnp.concatenate([by_y, from_x(by_y, 1), from_x(by_y, 2), from_x(by_y, 3)])
    mine = mine.reshape(NX, 4, SEQ + 16, 512)
    ahead = from_z(near, 1)
    behind = from_z(near, -1)
    far = lax.ppermute(near, z_axes, [((i + 2 - 4 * (i % 2)) % NZ, i) for i in range(NZ)])
    mine, ahead, far, behind = lax.optimization_barrier((mine, ahead, far, behind))
    other = lax.ppermute(mine, "core", [(0, 1), (1, 0)])
    gain = norm_gain.astype(F32).reshape(8, 1, 512)
    normed = call(
        norm_kernel,
        shape((8, ROWS, 512), BF16),
        (mine, other, gain),
        [VMEM] * 3,
        flops=ROWS * 4096 * 8,
        moved=8 << 20,
    )
    use = mine[:, 0, SEQ : SEQ + 2, 0:PICKS].astype(jnp.int32).reshape(8, PICKS)
    units = call(
        route_kernel,
        shape((UNITS,), jnp.int32),
        (doc_lists, doc_place, use),
        [SMEM] * 3,
        out_specs=SMEM,
        scratch=[pltpu.SMEM((NX * NZ,), jnp.int32)],
    )

    sends = call(
        project_kernel,
        [shape((ROWS + HALF, HEAD), BF16)] * NX,
        (normed, near, ahead, far, behind),
        [VMEM] * 5,
        out_specs=[VMEM] * NX,
        scratch=[pltpu.VMEM((4096, 2 * HEAD), BF16), pltpu.VMEM((ROWS, HEAD), F32)],
        flops=2 * ROWS * 4096 * 256,
        moved=8 << 20,
    )
    got = [
        lax.ppermute(sends[k], "x", [(i, (i + k) % NX) for i in range(NX)]) if k else sends[0]
        for k in range(NX)
    ]
    scratch = [
        pltpu.VMEM((8, COLS), F32),
        pltpu.VMEM((2 * NZ, SEQ, HEAD), BF16),
        pltpu.VMEM((NX, ROWS + HALF, HEAD), BF16),
        pltpu.SemaphoreType.DMA,
    ]
    stats = call(
        stats_kernel,
        shape((NX, 8, COLS), F32),
        (units, *got, docs),
        [SMEM] + [VMEM] * 4 + [ANY],
        scratch=scratch,
        limit=52,
    )
    all_stats = exchange(stats, "x")
    partial = call(
        values_kernel,
        shape((NX, HEAD, COLS), F32),
        (units, *got, docs, all_stats),
        [SMEM] + [VMEM] * 6,
        scratch=[scratch[0], scratch[2]],
    )
    returned = exchange(partial, "x")
    return call(finish_kernel, shape((SEQ, COLS), BF16), (returned,), [VMEM])


def solution(mesh):
    fine = Mesh(mesh.devices.reshape(4, 4, 4, 4, 2), ("x", "zh", "zl", "y", "core"))
    pairs, tensor = ("x", "zh", "zl"), ("y", "core")
    placed = (
        P(pairs, tensor),
        P(),
        P(pairs, tensor),
        P(pairs, tensor),
        P(pairs, tensor),
        P(pairs, None, tensor),
        P(),
        P(),
        P(pairs, None),
    )
    return jax.shard_map(
        shards, mesh=fine, in_specs=placed, out_specs=P(pairs, tensor), check_vma=False
    )
```

```python
import math

import jax
import jax.numpy as jnp
from jax import lax
from jax.experimental import pallas as pl
from jax.experimental.pallas import tpu as pltpu
from jax.sharding import Mesh
from jax.sharding import PartitionSpec as P

F32 = jnp.float32
BF16 = jnp.bfloat16
HEAD = 128
HALF = 64
SEQ = 128
RATIO = 4
NX = 4
NZ = 16
PICKS = 16
ROWS = NX * SEQ
COLS = RATIO * SEQ
RATE = HEAD ** (-0.5) * math.log2(math.e)
LOW = -1e30
UNITS = 128

VMEM = pl.BlockSpec(memory_space=pltpu.VMEM)
SMEM = pl.BlockSpec(memory_space=pltpu.SMEM)
ANY = pl.BlockSpec(memory_space=pl.ANY)


def call(kernel, outs, args, specs, out_specs=None, scratch=(), flops=0, moved=0, limit=24):
    return pl.pallas_call(
        kernel,
        out_shape=outs,
        in_specs=specs,
        out_specs=VMEM if out_specs is None else out_specs,
        scratch_shapes=list(scratch),
        compiler_params=pltpu.CompilerParams(vmem_limit_bytes=limit * 1024 * 1024),
        cost_estimate=pl.CostEstimate(flops=flops, bytes_accessed=moved, transcendentals=0),
    )(*args)


def side_by_side(left, right, left_at, right_at):
    left, right = left.astype(F32), right.astype(F32)
    lane = lax.broadcasted_iota(jnp.int32, left.shape, 1)
    left = pltpu.roll(left, HALF, 1) if left_at else left
    right = right if right_at else pltpu.roll(right, HALF, 1)
    return jnp.where(lane < HALF, left, right).astype(BF16)


def pack_kernel(*refs):
    sources, use, (out, tagged), copies, flags, done = refs[:4], refs[4], refs[5:7], refs[7:11], refs[11], refs[12]
    moves = [
        pltpu.make_async_copy(src, dst, done.at[i])
        for i, (src, dst) in enumerate(zip(sources, copies))
    ]
    for move in moves:
        move.start()
    flags[...] = jnp.zeros(flags.shape, jnp.int32)
    flags[0:2, 0:PICKS] = use[...]
    tagged[SEQ : SEQ + 16, :] = flags[...].astype(F32).astype(BF16)
    for move in moves:
        move.wait()
    wq, wk, wv, tokens = copies
    tagged[0:SEQ, :] = tokens[...]
    for part in range(NX):
        src = wk if part < 2 else wv
        at = HALF * (part % 2)
        packed = side_by_side(src[0:32, :], src[32:64, :], at, at)
        for copy in range(4):
            out[part, copy, 0:64, :] = wq[:, part * HEAD : (part + 1) * HEAD]
            out[part, copy, 64:96, :] = packed


def norm_kernel(mine, other, gain, out):
    core = lax.axis_index("core")
    for row in range(NX):
        rows = pl.ds(pl.multiple_of(lax.rem(lax.axis_index("x") + row, NX) * SEQ, SEQ), SEQ)
        total = jnp.zeros((SEQ, HEAD), F32)
        for src in (mine, other):
            for y in range(4):
                for c in range(4):
                    feats = src[row, y, 0:SEQ, c * HEAD : (c + 1) * HEAD].astype(F32)
                    total = total + feats * feats
        power = jnp.sum(total, axis=-1, keepdims=True) * (1.0 / 4096.0)
        factor = lax.rsqrt(power + 1e-05)
        for src, side in ((mine, core), (other, 1 - core)):
            for y in range(4):
                slot = 2 * y + side
                feats = src[row, y, 0:SEQ, :].astype(F32)
                out[slot, rows, :] = (feats * factor * gain[slot]).astype(BF16)


def route_kernel(lists, place, use, units, table):
    x, z = lax.axis_index("x"), lax.axis_index("zh") * 4 + lax.axis_index("zl")

    def clear(i, carry):
        table[i] = 0
        return carry

    lax.fori_loop(0, NX * NZ, clear, 0)

    def fill(i, carry):
        row, pick = i // PICKS, i % PICKS
        at = place[lists[row * NZ + z, pick]]
        owner, local = at // 2, at % 2
        step = lax.rem(row - x + NX, NX) * 2
        bits = use[step, pick] + 2 * use[step + 1, pick]
        entry = row * NZ + owner % NZ
        mine = jnp.where(owner // NZ == x, 1, 0)
        table[entry] = table[entry] + mine * bits * jnp.where(local == 1, 4, 1)
        return carry

    lax.fori_loop(0, NX * PICKS, fill, 0)

    def compact(i, count):
        bits = table[i]
        units[count + 1] = i * 16 + bits
        return count + jnp.where(bits > 0, 1, 0)

    count = lax.fori_loop(0, NX * NZ, compact, 0)
    units[0] = count
    for step in range(1, 4):
        units[count + step] = 0


def project_kernel(normed, near, ahead, far, behind, *rest):
    sends, weights, owns = rest[:NX], rest[NX], rest[NX + 1]
    for step, blocks in enumerate((near, ahead, far, behind)):
        row = lax.rem(lax.axis_index("zl") + step, 4) * HALF
        for b in range(16):
            block = blocks[b]
            base = pl.multiple_of(b * 256 + row, HALF)
            packed = block[64:96, :]
            weights[pl.ds(base, 64), 0:HEAD] = block[0:64, :]
            weights[pl.ds(base, 32), HEAD : 2 * HEAD] = packed
            weights[pl.ds(pl.multiple_of(base + 32, 32), 32), HEAD : 2 * HEAD] = pltpu.roll(
                packed.astype(F32), HALF, 1
            ).astype(BF16)
    total = jnp.zeros((ROWS, 2 * HEAD), F32)
    for slot in range(8):
        total = total + jnp.dot(
            normed[slot], weights[slot * 512 : (slot + 1) * 512, :], preferred_element_type=F32
        )
    query = total[:, 0:HEAD].astype(BF16)
    owns[...] = total[:, HEAD : 2 * HEAD]
    for step, send in enumerate(sends):
        dest = lax.rem(lax.axis_index("x") + step, NX)
        own = owns[pl.ds(pl.multiple_of(dest * SEQ, SEQ), SEQ), :]
        send[0:ROWS, :] = query
        send[ROWS : ROWS + HALF, :] = side_by_side(own[0:HALF], own[HALF:SEQ], 0, 0)


def own_part(got, first):
    a, b = got[first, ROWS : ROWS + HALF, :], got[first + 1, ROWS : ROWS + HALF, :]
    return jnp.concatenate([side_by_side(a, b, 0, 0), side_by_side(a, b, HALF, HALF)], axis=0)


def queries(got, group):
    rows = pl.ds(pl.multiple_of(group * SEQ, SEQ), SEQ)
    return jnp.concatenate([got[head, rows, :] for head in range(RATIO)], axis=0)


def scores_of(keys, query):
    return lax.dot_general(keys, query, (((1,), (1,)), ((), ())), preferred_element_type=F32)


def own_scores(got, group):
    scores = scores_of(own_part(got, 0), queries(got, group))
    key_at = lax.broadcasted_iota(jnp.int32, (SEQ, COLS), 0)
    row_at = lax.broadcasted_iota(jnp.int32, (SEQ, COLS), 1) % SEQ
    return jnp.where(row_at >= key_at, scores, LOW)


def unit_scores(code, got, docs):
    entry, bits = code // 16, code % 16
    group, owner = entry // NZ, entry % NZ
    keys = docs[pl.ds(owner * 2, 2), :, 0:HEAD].reshape(2 * SEQ, HEAD)
    scores = scores_of(keys, queries(got, group))
    second = (lax.broadcasted_iota(jnp.int32, (1, COLS), 1) % SEQ) // HALF
    parts = []
    for local in range(2):
        use_a, use_b = (bits // (4**local)) % 2, (bits // (2 * 4**local)) % 2
        keep = jnp.where(second == 0, use_a, use_b) > 0
        parts.append((scores[local * SEQ : (local + 1) * SEQ], keep))
    return group, owner, parts


def weigh(scores, shift):
    return jnp.exp2((scores - shift) * RATE)


def in_order(pieces, got):
    for step, piece in enumerate(pieces):
        got[lax.rem(lax.axis_index("x") - step + NX, NX)] = piece[...]


def stats_kernel(units, own, one, two, three, far_docs, send, stats, docs, got, done):
    fetch = pltpu.make_async_copy(far_docs.at[:, :, 0:HEAD], docs, done)
    fetch.start()
    in_order((own, one, two, three), got)
    x = lax.axis_index("x")
    scores = own_scores(got, x)
    top = jnp.max(scores, axis=0, keepdims=True)
    stats[0:4, :] = jnp.full((4, COLS), LOW, F32)
    stats[4:8, :] = jnp.zeros((4, COLS), F32)
    stats[pl.ds(x, 1), :] = top
    stats[pl.ds(x + 4, 1), :] = jnp.sum(weigh(scores, top), axis=0, keepdims=True)

    def unit(code):
        group, _, parts = unit_scores(code, got, docs)
        tops = [jnp.where(keep, jnp.max(s, axis=0, keepdims=True), LOW) for s, keep in parts]
        top = jnp.maximum(tops[0], tops[1])
        sums = [
            jnp.sum(weigh(s, jnp.where(keep, top, -LOW)), axis=0, keepdims=True)
            for s, keep in parts
        ]
        return group, top, sums[0] + sums[1]

    def pair(i, carry):
        for group, top, part in [unit(units[4 * i + j]) for j in range(1, 5)]:
            before = stats[pl.ds(group, 1), :]
            new = jnp.maximum(before, top)
            old = stats[pl.ds(group + 4, 1), :] * weigh(before, new)
            stats[pl.ds(group, 1), :] = new
            stats[pl.ds(group + 4, 1), :] = old + part * weigh(top, new)
        return carry

    fetch.wait()
    lax.fori_loop(0, (units[0] + 3) // 4, pair, 0)
    for dest in range(NX):
        send[dest] = stats[...]


def values_kernel(units, own, one, two, three, docs, all_stats, send, total, got):
    in_order((own, one, two, three), got)
    x = lax.axis_index("x")
    tops = [all_stats[src, 0:4, :] for src in range(NX)]
    top = jnp.maximum(jnp.maximum(tops[0], tops[1]), jnp.maximum(tops[2], tops[3]))
    sums = jnp.zeros((4, COLS), F32)
    for src in range(NX):
        sums = sums + all_stats[src, 4:8, :] * weigh(tops[src], top)
    total[0:4, :] = top
    total[4:8, :] = top * RATE + jnp.log2(sums)
    send[...] = jnp.zeros(send.shape, F32)

    def apply(values, probs):
        return lax.dot_general(values, probs, (((0,), (0,)), ((), ())), preferred_element_type=F32)

    own = jnp.exp2(own_scores(got, x) * RATE - total[pl.ds(x + 4, 1), :])
    send[pl.ds(x, 1)] = apply(own_part(got, 2), own.astype(BF16))[None]

    def unit(code):
        group, owner, parts = unit_scores(code, got, docs)
        shift = total[pl.ds(group + 4, 1), :]
        probs = [
            jnp.exp2(s * RATE - jnp.where(keep, shift, -LOW)).astype(BF16) for s, keep in parts
        ]
        values = docs[pl.ds(owner * 2, 2), :, HEAD : 2 * HEAD].reshape(2 * SEQ, HEAD)
        return group, apply(values, jnp.concatenate(probs, axis=0))

    def pair(i, carry):
        for group, out in [unit(units[4 * i + j]) for j in range(1, 5)]:
            send[pl.ds(group, 1)] = send[pl.ds(group, 1)] + out[None]
        return carry

    lax.fori_loop(0, (units[0] + 3) // 4, pair, 0)


def finish_kernel(got, out):
    for head in range(RATIO):
        cols = slice(head * SEQ, (head + 1) * SEQ)
        total = (got[0, :, cols] + got[1, :, cols]) + (got[2, :, cols] + got[3, :, cols])
        out[:, cols] = total.T.astype(BF16)


def exchange(array, axes):
    return lax.all_to_all(array, axes, 0, 0, tiled=True)


def shards(tokens, norm_gain, wq, wk, wv, doc_cache, doc_lists, doc_place, block_use):
    shape = jax.ShapeDtypeStruct
    z_axes = ("zh", "zl")
    docs = lax.all_gather(doc_cache, z_axes, axis=0, tiled=True)

    sources = (wq, wk, wv, tokens)
    parts, tagged = call(
        pack_kernel,
        [shape((4, 4, 96, HEAD), BF16), shape((SEQ + 16, 512), BF16)],
        (*sources, block_use),
        [ANY] * 4 + [VMEM],
        out_specs=[VMEM] * 2,
        scratch=[pltpu.VMEM(a.shape, BF16) for a in sources]
        + [pltpu.VMEM((16, 512), jnp.int32), pltpu.SemaphoreType.DMA((4,))],
        limit=62,
    )
    near = exchange(parts.reshape(16, 96, HEAD), ("x", "zh"))

    def from_z(array, step):
        return lax.ppermute(array, z_axes, [((i + step) % NZ, i) for i in range(NZ)])

    def from_x(array, step):
        return lax.ppermute(array, "x", [((i + step) % NX, i) for i in range(NX)])

    by_y = lax.all_gather(tagged, "y")
    mine = jnp.concatenate([by_y, from_x(by_y, 1), from_x(by_y, 2), from_x(by_y, 3)])
    mine = mine.reshape(NX, 4, SEQ + 16, 512)
    ahead = from_z(near, 1)
    behind = from_z(near, -1)
    far = from_z(ahead, 1)
    mine, ahead, far, behind = lax.optimization_barrier((mine, ahead, far, behind))
    other = lax.ppermute(mine, "core", [(0, 1), (1, 0)])
    use = mine[:, 0, SEQ : SEQ + 2, 0:PICKS].astype(jnp.int32).reshape(8, PICKS)
    units = call(
        route_kernel,
        shape((UNITS,), jnp.int32),
        (doc_lists, doc_place, use),
        [SMEM] * 3,
        out_specs=SMEM,
        scratch=[pltpu.SMEM((NX * NZ,), jnp.int32)],
    )
    other, units = lax.optimization_barrier((other, units))
    gain = norm_gain.astype(F32).reshape(8, 1, 512)
    normed = call(
        norm_kernel,
        shape((8, ROWS, 512), BF16),
        (mine, other, gain),
        [VMEM] * 3,
        flops=ROWS * 4096 * 8,
        moved=8 << 20,
    )
    sends = call(
        project_kernel,
        [shape((ROWS + HALF, HEAD), BF16)] * NX,
        (normed, near, ahead, far, behind),
        [VMEM] * 5,
        out_specs=[VMEM] * NX,
        scratch=[pltpu.VMEM((4096, 2 * HEAD), BF16), pltpu.VMEM((ROWS, HEAD), F32)],
        flops=2 * ROWS * 4096 * 256,
        moved=8 << 20,
    )
    got = [
        lax.ppermute(sends[k], "x", [(i, (i + k) % NX) for i in range(NX)]) if k else sends[0]
        for k in range(NX)
    ]
    scratch = [
        pltpu.VMEM((8, COLS), F32),
        pltpu.VMEM((2 * NZ, SEQ, HEAD), BF16),
        pltpu.VMEM((NX, ROWS + HALF, HEAD), BF16),
        pltpu.SemaphoreType.DMA,
    ]
    stats = call(
        stats_kernel,
        shape((NX, 8, COLS), F32),
        (units, *got, docs),
        [SMEM] + [VMEM] * 4 + [ANY],
        scratch=scratch,
        limit=52,
    )
    all_stats = exchange(stats, "x")
    partial = call(
        values_kernel,
        shape((NX, HEAD, COLS), F32),
        (units, *got, docs, all_stats),
        [SMEM] + [VMEM] * 6,
        scratch=[scratch[0], scratch[2]],
    )
    returned = exchange(partial, "x")
    return call(finish_kernel, shape((SEQ, COLS), BF16), (returned,), [VMEM])


def solution(mesh):
    fine = Mesh(mesh.devices.reshape(4, 4, 4, 4, 2), ("x", "zh", "zl", "y", "core"))
    pairs, tensor = ("x", "zh", "zl"), ("y", "core")
    placed = (
        P(pairs, tensor),
        P(),
        P(pairs, tensor),
        P(pairs, tensor),
        P(pairs, tensor),
        P(pairs, None, tensor),
        P(),
        P(),
        P(pairs, None),
    )
    return jax.shard_map(
        shards, mesh=fine, in_specs=placed, out_specs=P(pairs, tensor), check_vma=False
    )
```

```python
import math

import jax
import jax.numpy as jnp
from jax import lax
from jax.experimental import pallas as pl
from jax.experimental.pallas import tpu as pltpu
from jax.sharding import Mesh
from jax.sharding import PartitionSpec as P

F32 = jnp.float32
BF16 = jnp.bfloat16
HEAD = 128
HALF = 64
SEQ = 128
RATIO = 4
NX = 4
NZ = 16
PICKS = 16
ROWS = NX * SEQ
COLS = RATIO * SEQ
RATE = HEAD ** (-0.5) * math.log2(math.e)
LOW = -1e30
UNITS = 128

VMEM = pl.BlockSpec(memory_space=pltpu.VMEM)
SMEM = pl.BlockSpec(memory_space=pltpu.SMEM)
ANY = pl.BlockSpec(memory_space=pl.ANY)


def call(kernel, outs, args, specs, out_specs=None, scratch=(), flops=0, moved=0, limit=24):
    return pl.pallas_call(
        kernel,
        out_shape=outs,
        in_specs=specs,
        out_specs=VMEM if out_specs is None else out_specs,
        scratch_shapes=list(scratch),
        compiler_params=pltpu.CompilerParams(vmem_limit_bytes=limit * 1024 * 1024),
        cost_estimate=pl.CostEstimate(flops=flops, bytes_accessed=moved, transcendentals=0),
    )(*args)


def side_by_side(left, right, left_at, right_at):
    left, right = left.astype(F32), right.astype(F32)
    lane = lax.broadcasted_iota(jnp.int32, left.shape, 1)
    left = pltpu.roll(left, HALF, 1) if left_at else left
    right = right if right_at else pltpu.roll(right, HALF, 1)
    return jnp.where(lane < HALF, left, right).astype(BF16)


def pack_kernel(*refs):
    sources, out, copies, done = refs[:3], refs[3], refs[4:7], refs[7]
    moves = [
        pltpu.make_async_copy(src, dst, done.at[i])
        for i, (src, dst) in enumerate(zip(sources, copies))
    ]
    for move in moves:
        move.start()
    for move in moves:
        move.wait()
    wq, wk, wv = copies
    for part in range(NX):
        src = wk if part < 2 else wv
        at = HALF * (part % 2)
        packed = side_by_side(src[0:32, :], src[32:64, :], at, at)
        for copy in range(4):
            out[part, copy, 0:64, :] = wq[:, part * HEAD : (part + 1) * HEAD]
            out[part, copy, 64:96, :] = packed


def tag_kernel(tokens, use, out, flags):
    flags[...] = jnp.zeros(flags.shape, jnp.int32)
    flags[0:2, 0:PICKS] = use[...]
    out[0:SEQ, :] = tokens[...]
    out[SEQ : SEQ + 16, :] = flags[...].astype(F32).astype(BF16)


def norm_kernel(mine, other, gain, out):
    core = lax.axis_index("core")
    for row in range(NX):
        rows = pl.ds(pl.multiple_of(lax.rem(lax.axis_index("x") + row, NX) * SEQ, SEQ), SEQ)
        total = jnp.zeros((SEQ, HEAD), F32)
        for src in (mine, other):
            for y in range(4):
                for c in range(4):
                    feats = src[row, y, 0:SEQ, c * HEAD : (c + 1) * HEAD].astype(F32)
                    total = total + feats * feats
        power = jnp.sum(total, axis=-1, keepdims=True) * (1.0 / 4096.0)
        factor = lax.rsqrt(power + 1e-05)
        for src, side in ((mine, core), (other, 1 - core)):
            for y in range(4):
                slot = 2 * y + side
                feats = src[row, y, 0:SEQ, :].astype(F32)
                out[slot, rows, :] = (feats * factor * gain[slot]).astype(BF16)


def route_kernel(lists, place, use, units, table):
    x, z = lax.axis_index("x"), lax.axis_index("zh") * 4 + lax.axis_index("zl")

    def clear(i, carry):
        table[i] = 0
        return carry

    lax.fori_loop(0, NX * NZ, clear, 0)

    def fill(i, carry):
        row, pick = i // PICKS, i % PICKS
        at = place[lists[row * NZ + z, pick]]
        owner, local = at // 2, at % 2
        step = lax.rem(row - x + NX, NX) * 2
        bits = use[step, pick] + 2 * use[step + 1, pick]
        entry = row * NZ + owner % NZ
        mine = jnp.where(owner // NZ == x, 1, 0)
        table[entry] = table[entry] + mine * bits * jnp.where(local == 1, 4, 1)
        return carry

    lax.fori_loop(0, NX * PICKS, fill, 0)

    def compact(i, count):
        bits = table[i]
        units[count + 1] = i * 16 + bits
        return count + jnp.where(bits > 0, 1, 0)

    count = lax.fori_loop(0, NX * NZ, compact, 0)
    units[0] = count
    for step in range(1, 4):
        units[count + step] = 0


def project_kernel(normed, near, ahead, far, behind, *rest):
    sends, weights, owns = rest[:NX], rest[NX], rest[NX + 1]
    for step, blocks in enumerate((near, ahead, far, behind)):
        row = lax.rem(lax.axis_index("zl") + step, 4) * HALF
        for b in range(16):
            block = blocks[b]
            base = pl.multiple_of(b * 256 + row, HALF)
            packed = block[64:96, :]
            weights[pl.ds(base, 64), 0:HEAD] = block[0:64, :]
            weights[pl.ds(base, 32), HEAD : 2 * HEAD] = packed
            weights[pl.ds(pl.multiple_of(base + 32, 32), 32), HEAD : 2 * HEAD] = pltpu.roll(
                packed.astype(F32), HALF, 1
            ).astype(BF16)
    total = jnp.zeros((ROWS, 2 * HEAD), F32)
    for slot in range(8):
        total = total + jnp.dot(
            normed[slot], weights[slot * 512 : (slot + 1) * 512, :], preferred_element_type=F32
        )
    query = total[:, 0:HEAD].astype(BF16)
    owns[...] = total[:, HEAD : 2 * HEAD]
    for step, send in enumerate(sends):
        dest = lax.rem(lax.axis_index("x") + step, NX)
        own = owns[pl.ds(pl.multiple_of(dest * SEQ, SEQ), SEQ), :]
        send[0:ROWS, :] = query
        send[ROWS : ROWS + HALF, :] = side_by_side(own[0:HALF], own[HALF:SEQ], 0, 0)


def own_part(got, first):
    a, b = got[first, ROWS : ROWS + HALF, :], got[first + 1, ROWS : ROWS + HALF, :]
    return jnp.concatenate([side_by_side(a, b, 0, 0), side_by_side(a, b, HALF, HALF)], axis=0)


def queries(got, group):
    rows = pl.ds(pl.multiple_of(group * SEQ, SEQ), SEQ)
    return jnp.concatenate([got[head, rows, :] for head in range(RATIO)], axis=0)


def scores_of(keys, query):
    return lax.dot_general(keys, query, (((1,), (1,)), ((), ())), preferred_element_type=F32)


def own_scores(got, group):
    scores = scores_of(own_part(got, 0), queries(got, group))
    key_at = lax.broadcasted_iota(jnp.int32, (SEQ, COLS), 0)
    row_at = lax.broadcasted_iota(jnp.int32, (SEQ, COLS), 1) % SEQ
    return jnp.where(row_at >= key_at, scores, LOW)


def unit_scores(code, got, docs):
    entry, bits = code // 16, code % 16
    group, owner = entry // NZ, entry % NZ
    keys = docs[pl.ds(owner * 2, 2), :, 0:HEAD].reshape(2 * SEQ, HEAD)
    scores = scores_of(keys, queries(got, group))
    second = (lax.broadcasted_iota(jnp.int32, (1, COLS), 1) % SEQ) // HALF
    parts = []
    for local in range(2):
        use_a, use_b = (bits // (4**local)) % 2, (bits // (2 * 4**local)) % 2
        keep = jnp.where(second == 0, use_a, use_b) > 0
        parts.append((scores[local * SEQ : (local + 1) * SEQ], keep))
    return group, owner, parts


def in_steps(units, unit, merge):
    def steps(width, first):
        def step(i, carry):
            for result in [unit(units[first + width * i + j]) for j in range(1, width + 1)]:
                merge(*result)
            return carry

        return step

    eights = units[0] // 8
    lax.fori_loop(0, eights, steps(8, 0), 0)
    lax.fori_loop(0, (units[0] - 8 * eights + 3) // 4, steps(4, 8 * eights), 0)


def weigh(scores, shift):
    return jnp.exp2((scores - shift) * RATE)


def in_order(pieces, got):
    for step, piece in enumerate(pieces):
        got[lax.rem(lax.axis_index("x") - step + NX, NX)] = piece[...]


def stats_kernel(units, own, one, two, three, far_docs, send, stats, docs, got, done):
    fetch = pltpu.make_async_copy(far_docs.at[:, :, 0:HEAD], docs, done)
    fetch.start()
    in_order((own, one, two, three), got)
    x = lax.axis_index("x")
    scores = own_scores(got, x)
    top = jnp.max(scores, axis=0, keepdims=True)
    stats[0:4, :] = jnp.full((4, COLS), LOW, F32)
    stats[4:8, :] = jnp.zeros((4, COLS), F32)
    stats[pl.ds(x, 1), :] = top
    stats[pl.ds(x + 4, 1), :] = jnp.sum(weigh(scores, top), axis=0, keepdims=True)

    def unit(code):
        group, _, parts = unit_scores(code, got, docs)
        tops = [jnp.where(keep, jnp.max(s, axis=0, keepdims=True), LOW) for s, keep in parts]
        top = jnp.maximum(tops[0], tops[1])
        sums = [
            jnp.sum(weigh(s, jnp.where(keep, top, -LOW)), axis=0, keepdims=True)
            for s, keep in parts
        ]
        return group, top, sums[0] + sums[1]

    def merge(group, top, part):
        before = stats[pl.ds(group, 1), :]
        new = jnp.maximum(before, top)
        old = stats[pl.ds(group + 4, 1), :] * weigh(before, new)
        stats[pl.ds(group, 1), :] = new
        stats[pl.ds(group + 4, 1), :] = old + part * weigh(top, new)

    fetch.wait()
    in_steps(units, unit, merge)
    for dest in range(NX):
        send[dest] = stats[...]


def values_kernel(units, own, one, two, three, docs, all_stats, send, total, got):
    in_order((own, one, two, three), got)
    x = lax.axis_index("x")
    tops = [all_stats[src, 0:4, :] for src in range(NX)]
    top = jnp.maximum(jnp.maximum(tops[0], tops[1]), jnp.maximum(tops[2], tops[3]))
    sums = jnp.zeros((4, COLS), F32)
    for src in range(NX):
        sums = sums + all_stats[src, 4:8, :] * weigh(tops[src], top)
    total[0:4, :] = top
    total[4:8, :] = top * RATE + jnp.log2(sums)
    send[...] = jnp.zeros(send.shape, F32)

    def apply(values, probs):
        return lax.dot_general(values, probs, (((0,), (0,)), ((), ())), preferred_element_type=F32)

    own = jnp.exp2(own_scores(got, x) * RATE - total[pl.ds(x + 4, 1), :])
    send[pl.ds(x, 1)] = apply(own_part(got, 2), own.astype(BF16))[None]

    def unit(code):
        group, owner, parts = unit_scores(code, got, docs)
        shift = total[pl.ds(group + 4, 1), :]
        probs = [
            jnp.exp2(s * RATE - jnp.where(keep, shift, -LOW)).astype(BF16) for s, keep in parts
        ]
        values = docs[pl.ds(owner * 2, 2), :, HEAD : 2 * HEAD].reshape(2 * SEQ, HEAD)
        return group, apply(values, jnp.concatenate(probs, axis=0))

    def merge(group, out):
        send[pl.ds(group, 1)] = send[pl.ds(group, 1)] + out[None]

    in_steps(units, unit, merge)


def finish_kernel(got, out):
    for head in range(RATIO):
        cols = slice(head * SEQ, (head + 1) * SEQ)
        total = (got[0, :, cols] + got[1, :, cols]) + (got[2, :, cols] + got[3, :, cols])
        out[:, cols] = total.T.astype(BF16)


def exchange(array, axes):
    return lax.all_to_all(array, axes, 0, 0, tiled=True)


def shards(tokens, norm_gain, wq, wk, wv, doc_cache, doc_lists, doc_place, block_use):
    shape = jax.ShapeDtypeStruct
    z_axes = ("zh", "zl")
    docs = lax.all_gather(doc_cache, z_axes, axis=0, tiled=True)

    sources = (wq, wk, wv)
    parts = call(
        pack_kernel,
        shape((4, 4, 96, HEAD), BF16),
        sources,
        [ANY] * 3,
        scratch=[pltpu.VMEM(a.shape, BF16) for a in sources] + [pltpu.SemaphoreType.DMA((3,))],
        limit=62,
    )
    tagged = call(
        tag_kernel,
        shape((SEQ + 16, 512), BF16),
        (tokens, block_use),
        [VMEM] * 2,
        scratch=[pltpu.VMEM((16, 512), jnp.int32)],
        flops=0,
        limit=62,
    )
    near = exchange(parts.reshape(16, 96, HEAD), ("x", "zh"))

    def from_z(array, step):
        return lax.ppermute(array, z_axes, [((i + step) % NZ, i) for i in range(NZ)])

    def from_x(array, step):
        return lax.ppermute(array, "x", [((i + step) % NX, i) for i in range(NX)])

    by_y = lax.all_gather(tagged, "y")
    mine = jnp.concatenate([by_y, from_x(by_y, 1), from_x(by_y, 2), from_x(by_y, 3)])
    mine = mine.reshape(NX, 4, SEQ + 16, 512)
    ahead = from_z(near, 1)
    behind = from_z(near, -1)
    far = lax.ppermute(near, z_axes, [((i + 2 - 4 * (i % 2)) % NZ, i) for i in range(NZ)])
    mine, ahead, far, behind = lax.optimization_barrier((mine, ahead, far, behind))
    other = lax.ppermute(mine, "core", [(0, 1), (1, 0)])
    gain = norm_gain.astype(F32).reshape(8, 1, 512)
    normed = call(
        norm_kernel,
        shape((8, ROWS, 512), BF16),
        (mine, other, gain),
        [VMEM] * 3,
        flops=ROWS * 4096 * 8,
        moved=8 << 20,
    )
    use = mine[:, 0, SEQ : SEQ + 2, 0:PICKS].astype(jnp.int32).reshape(8, PICKS)
    units = call(
        route_kernel,
        shape((UNITS,), jnp.int32),
        (doc_lists, doc_place, use),
        [SMEM] * 3,
        out_specs=SMEM,
        scratch=[pltpu.SMEM((NX * NZ,), jnp.int32)],
    )

    sends = call(
        project_kernel,
        [shape((ROWS + HALF, HEAD), BF16)] * NX,
        (normed, near, ahead, far, behind),
        [VMEM] * 5,
        out_specs=[VMEM] * NX,
        scratch=[pltpu.VMEM((4096, 2 * HEAD), BF16), pltpu.VMEM((ROWS, HEAD), F32)],
        flops=2 * ROWS * 4096 * 256,
        moved=8 << 20,
    )
    got = [
        lax.ppermute(sends[k], "x", [(i, (i + k) % NX) for i in range(NX)]) if k else sends[0]
        for k in range(NX)
    ]
    scratch = [
        pltpu.VMEM((8, COLS), F32),
        pltpu.VMEM((2 * NZ, SEQ, HEAD), BF16),
        pltpu.VMEM((NX, ROWS + HALF, HEAD), BF16),
        pltpu.SemaphoreType.DMA,
    ]
    stats = call(
        stats_kernel,
        shape((NX, 8, COLS), F32),
        (units, *got, docs),
        [SMEM] + [VMEM] * 4 + [ANY],
        scratch=scratch,
        limit=52,
    )
    all_stats = exchange(stats, "x")
    partial = call(
        values_kernel,
        shape((NX, HEAD, COLS), F32),
        (units, *got, docs, all_stats),
        [SMEM] + [VMEM] * 6,
        scratch=[scratch[0], scratch[2]],
    )
    returned = exchange(partial, "x")
    return call(finish_kernel, shape((SEQ, COLS), BF16), (returned,), [VMEM])


def solution(mesh):
    fine = Mesh(mesh.devices.reshape(4, 4, 4, 4, 2), ("x", "zh", "zl", "y", "core"))
    pairs, tensor = ("x", "zh", "zl"), ("y", "core")
    placed = (
        P(pairs, tensor),
        P(),
        P(pairs, tensor),
        P(pairs, tensor),
        P(pairs, tensor),
        P(pairs, None, tensor),
        P(),
        P(),
        P(pairs, None),
    )
    return jax.shard_map(
        shards, mesh=fine, in_specs=placed, out_specs=P(pairs, tensor), check_vma=False
    )
```

```python
import math

import jax
import jax.numpy as jnp
from jax import lax
from jax.experimental import pallas as pl
from jax.experimental.pallas import tpu as pltpu
from jax.sharding import Mesh
from jax.sharding import PartitionSpec as P

F32 = jnp.float32
BF16 = jnp.bfloat16
HEAD = 128
HALF = 64
SEQ = 128
RATIO = 4
NX = 4
NZ = 16
PICKS = 16
ROWS = NX * SEQ
COLS = RATIO * SEQ
RATE = HEAD ** (-0.5) * math.log2(math.e)
LOW = -1e30
UNITS = 128

VMEM = pl.BlockSpec(memory_space=pltpu.VMEM)
SMEM = pl.BlockSpec(memory_space=pltpu.SMEM)
ANY = pl.BlockSpec(memory_space=pl.ANY)


def call(kernel, outs, args, specs, out_specs=None, scratch=(), flops=0, moved=0, limit=24):
    return pl.pallas_call(
        kernel,
        out_shape=outs,
        in_specs=specs,
        out_specs=VMEM if out_specs is None else out_specs,
        scratch_shapes=list(scratch),
        compiler_params=pltpu.CompilerParams(vmem_limit_bytes=limit * 1024 * 1024),
        cost_estimate=pl.CostEstimate(flops=flops, bytes_accessed=moved, transcendentals=0),
    )(*args)


def side_by_side(left, right, left_at, right_at):
    left, right = left.astype(F32), right.astype(F32)
    lane = lax.broadcasted_iota(jnp.int32, left.shape, 1)
    left = pltpu.roll(left, HALF, 1) if left_at else left
    right = right if right_at else pltpu.roll(right, HALF, 1)
    return jnp.where(lane < HALF, left, right).astype(BF16)


def pack_kernel(*refs):
    sources, out, copies, done = refs[:3], refs[3], refs[4:7], refs[7]
    moves = [
        pltpu.make_async_copy(src, dst, done.at[i])
        for i, (src, dst) in enumerate(zip(sources, copies))
    ]
    for move in moves:
        move.start()
    for move in moves:
        move.wait()
    wq, wk, wv = copies
    for part in range(NX):
        src = wk if part < 2 else wv
        at = HALF * (part % 2)
        packed = side_by_side(src[0:32, :], src[32:64, :], at, at)
        for copy in range(4):
            out[part, copy, 0:64, :] = wq[:, part * HEAD : (part + 1) * HEAD]
            out[part, copy, 64:96, :] = packed


def tag_kernel(tokens, use, out, flags):
    flags[...] = jnp.zeros(flags.shape, jnp.int32)
    flags[0:2, 0:PICKS] = use[...]
    out[0:SEQ, :] = tokens[...]
    out[SEQ : SEQ + 16, :] = flags[...].astype(F32).astype(BF16)


def norm_kernel(mine, other, gain, out):
    core = lax.axis_index("core")
    for row in range(NX):
        rows = pl.ds(pl.multiple_of(lax.rem(lax.axis_index("x") + row, NX) * SEQ, SEQ), SEQ)
        total = jnp.zeros((SEQ, HEAD), F32)
        for src in (mine, other):
            for y in range(4):
                for c in range(4):
                    feats = src[row, y, 0:SEQ, c * HEAD : (c + 1) * HEAD].astype(F32)
                    total = total + feats * feats
        power = jnp.sum(total, axis=-1, keepdims=True) * (1.0 / 4096.0)
        factor = lax.rsqrt(power + 1e-05)
        for src, side in ((mine, core), (other, 1 - core)):
            for y in range(4):
                slot = 2 * y + side
                feats = src[row, y, 0:SEQ, :].astype(F32)
                out[slot, rows, :] = (feats * factor * gain[slot]).astype(BF16)


def route_kernel(lists, place, use, units, table):
    x, z = lax.axis_index("x"), lax.axis_index("zh") * 4 + lax.axis_index("zl")

    def clear(i, carry):
        table[i] = 0
        return carry

    lax.fori_loop(0, NX * NZ, clear, 0)

    def fill(i, carry):
        row, pick = i // PICKS, i % PICKS
        at = place[lists[row * NZ + z, pick]]
        owner, local = at // 2, at % 2
        step = lax.rem(row - x + NX, NX) * 2
        bits = use[step, pick] + 2 * use[step + 1, pick]
        entry = row * NZ + owner % NZ
        mine = jnp.where(owner // NZ == x, 1, 0)
        table[entry] = table[entry] + mine * bits * jnp.where(local == 1, 4, 1)
        return carry

    lax.fori_loop(0, NX * PICKS, fill, 0)

    def compact(i, count):
        bits = table[i]
        units[count + 1] = i * 16 + bits
        return count + jnp.where(bits > 0, 1, 0)

    count = lax.fori_loop(0, NX * NZ, compact, 0)
    units[0] = count
    for step in range(1, 4):
        units[count + step] = 0


def project_kernel(normed, near, ahead, far, behind, *rest):
    sends, weights, owns = rest[:NX], rest[NX], rest[NX + 1]
    for step, blocks in enumerate((near, ahead, far, behind)):
        row = lax.rem(lax.axis_index("zl") + step, 4) * HALF
        for b in range(16):
            block = blocks[b]
            base = pl.multiple_of(b * 256 + row, HALF)
            packed = block[64:96, :]
            weights[pl.ds(base, 64), 0:HEAD] = block[0:64, :]
            weights[pl.ds(base, 32), HEAD : 2 * HEAD] = packed
            weights[pl.ds(pl.multiple_of(base + 32, 32), 32), HEAD : 2 * HEAD] = pltpu.roll(
                packed.astype(F32), HALF, 1
            ).astype(BF16)
    total = jnp.zeros((ROWS, 2 * HEAD), F32)
    for slot in range(8):
        total = total + jnp.dot(
            normed[slot], weights[slot * 512 : (slot + 1) * 512, :], preferred_element_type=F32
        )
    query = total[:, 0:HEAD].astype(BF16)
    owns[...] = total[:, HEAD : 2 * HEAD]
    for step, send in enumerate(sends):
        dest = lax.rem(lax.axis_index("x") + step, NX)
        own = owns[pl.ds(pl.multiple_of(dest * SEQ, SEQ), SEQ), :]
        send[0:ROWS, :] = query
        send[ROWS : ROWS + HALF, :] = side_by_side(own[0:HALF], own[HALF:SEQ], 0, 0)


def own_part(got, first):
    a, b = got[first, ROWS : ROWS + HALF, :], got[first + 1, ROWS : ROWS + HALF, :]
    return jnp.concatenate([side_by_side(a, b, 0, 0), side_by_side(a, b, HALF, HALF)], axis=0)


def queries(got, group):
    rows = pl.ds(pl.multiple_of(group * SEQ, SEQ), SEQ)
    return jnp.concatenate([got[head, rows, :] for head in range(RATIO)], axis=0)


def scores_of(keys, query):
    return lax.dot_general(keys, query, (((1,), (1,)), ((), ())), preferred_element_type=F32)


def own_scores(got, group):
    scores = scores_of(own_part(got, 0), queries(got, group))
    key_at = lax.broadcasted_iota(jnp.int32, (SEQ, COLS), 0)
    row_at = lax.broadcasted_iota(jnp.int32, (SEQ, COLS), 1) % SEQ
    return jnp.where(row_at >= key_at, scores, LOW)


def unit_scores(code, got, docs):
    entry, bits = code // 16, code % 16
    group, owner = entry // NZ, entry % NZ
    keys = docs[pl.ds(owner * 2, 2), :, 0:HEAD].reshape(2 * SEQ, HEAD)
    scores = scores_of(keys, queries(got, group))
    second = (lax.broadcasted_iota(jnp.int32, (1, COLS), 1) % SEQ) // HALF
    parts = []
    for local in range(2):
        use_a, use_b = (bits // (4**local)) % 2, (bits // (2 * 4**local)) % 2
        keep = jnp.where(second == 0, use_a, use_b) > 0
        parts.append((scores[local * SEQ : (local + 1) * SEQ], keep))
    return group, owner, parts


def in_steps(units, unit, merge):
    def steps(width, first):
        def step(i, carry):
            for result in [unit(units[first + width * i + j]) for j in range(1, width + 1)]:
                merge(*result)
            return carry

        return step

    eights = units[0] // 8
    lax.fori_loop(0, eights, steps(8, 0), 0)
    lax.fori_loop(0, (units[0] - 8 * eights + 3) // 4, steps(4, 8 * eights), 0)


def weigh(scores, shift):
    return jnp.exp2((scores - shift) * RATE)


def in_order(pieces, got):
    for step, piece in enumerate(pieces):
        got[lax.rem(lax.axis_index("x") - step + NX, NX)] = piece[...]


def stats_kernel(units, own, one, two, three, far_docs, send, stats, docs, got, done):
    fetch = pltpu.make_async_copy(far_docs.at[:, :, 0:HEAD], docs, done)
    fetch.start()
    in_order((own, one, two, three), got)
    x = lax.axis_index("x")
    scores = own_scores(got, x)
    top = jnp.max(scores, axis=0, keepdims=True)
    stats[0:4, :] = jnp.full((4, COLS), LOW, F32)
    stats[4:8, :] = jnp.zeros((4, COLS), F32)
    stats[pl.ds(x, 1), :] = top
    stats[pl.ds(x + 4, 1), :] = jnp.sum(weigh(scores, top), axis=0, keepdims=True)

    def unit(code):
        group, _, parts = unit_scores(code, got, docs)
        tops = [jnp.where(keep, jnp.max(s, axis=0, keepdims=True), LOW) for s, keep in parts]
        top = jnp.maximum(tops[0], tops[1])
        sums = [
            jnp.sum(weigh(s, jnp.where(keep, top, -LOW)), axis=0, keepdims=True)
            for s, keep in parts
        ]
        return group, top, sums[0] + sums[1]

    def merge(group, top, part):
        before = stats[pl.ds(group, 1), :]
        new = jnp.maximum(before, top)
        old = stats[pl.ds(group + 4, 1), :] * weigh(before, new)
        stats[pl.ds(group, 1), :] = new
        stats[pl.ds(group + 4, 1), :] = old + part * weigh(top, new)

    fetch.wait()
    in_steps(units, unit, merge)
    for dest in range(NX):
        send[dest] = stats[...]


def values_kernel(units, own, one, two, three, docs, all_stats, send, total, got):
    in_order((own, one, two, three), got)
    x = lax.axis_index("x")
    tops = [all_stats[src, 0:4, :] for src in range(NX)]
    top = jnp.maximum(jnp.maximum(tops[0], tops[1]), jnp.maximum(tops[2], tops[3]))
    sums = jnp.zeros((4, COLS), F32)
    for src in range(NX):
        sums = sums + all_stats[src, 4:8, :] * weigh(tops[src], top)
    total[0:4, :] = top
    total[4:8, :] = top * RATE + jnp.log2(sums)
    send[...] = jnp.zeros(send.shape, F32)

    def apply(values, probs):
        return lax.dot_general(values, probs, (((0,), (0,)), ((), ())), preferred_element_type=F32)

    own = jnp.exp2(own_scores(got, x) * RATE - total[pl.ds(x + 4, 1), :])
    send[pl.ds(x, 1)] = apply(own_part(got, 2), own.astype(BF16))[None]

    def unit(code):
        group, owner, parts = unit_scores(code, got, docs)
        shift = total[pl.ds(group + 4, 1), :]
        probs = [
            jnp.exp2(s * RATE - jnp.where(keep, shift, -LOW)).astype(BF16) for s, keep in parts
        ]
        values = docs[pl.ds(owner * 2, 2), :, HEAD : 2 * HEAD].reshape(2 * SEQ, HEAD)
        return group, apply(values, jnp.concatenate(probs, axis=0))

    def merge(group, out):
        send[pl.ds(group, 1)] = send[pl.ds(group, 1)] + out[None]

    in_steps(units, unit, merge)


def finish_kernel(got, out):
    for head in range(RATIO):
        cols = slice(head * SEQ, (head + 1) * SEQ)
        total = (got[0, :, cols] + got[1, :, cols]) + (got[2, :, cols] + got[3, :, cols])
        out[:, cols] = total.T.astype(BF16)


def exchange(array, axes):
    return lax.all_to_all(array, axes, 0, 0, tiled=True)


def shards(tokens, norm_gain, wq, wk, wv, doc_cache, doc_lists, doc_place, block_use):
    shape = jax.ShapeDtypeStruct
    z_axes = ("zh", "zl")
    docs = lax.all_gather(doc_cache, z_axes, axis=0, tiled=True)

    sources = (wq, wk, wv)
    parts = call(
        pack_kernel,
        shape((4, 4, 96, HEAD), BF16),
        sources,
        [ANY] * 3,
        scratch=[pltpu.VMEM(a.shape, BF16) for a in sources] + [pltpu.SemaphoreType.DMA((3,))],
        limit=62,
    )
    tagged = call(
        tag_kernel,
        shape((SEQ + 16, 512), BF16),
        (tokens, block_use),
        [VMEM] * 2,
        scratch=[pltpu.VMEM((16, 512), jnp.int32)],
        flops=0,
        limit=62,
    )
    near = exchange(parts.reshape(16, 96, HEAD), ("x", "zh"))

    def from_z(array, step):
        return lax.ppermute(array, z_axes, [((i + step) % NZ, i) for i in range(NZ)])

    def from_x(array, step):
        return lax.ppermute(array, "x", [((i + step) % NX, i) for i in range(NX)])

    by_y = lax.all_gather(tagged, "y")
    mine = jnp.concatenate([by_y, from_x(by_y, 1), from_x(by_y, 2), from_x(by_y, 3)])
    mine = mine.reshape(NX, 4, SEQ + 16, 512)
    ahead = from_z(near, 1)
    behind = from_z(near, -1)
    far = lax.ppermute(near, z_axes, [((i + 2 - 4 * (i % 2)) % NZ, i) for i in range(NZ)])
    use = mine[:, 0, SEQ : SEQ + 2, 0:PICKS].astype(jnp.int32).reshape(8, PICKS)
    units = call(
        route_kernel,
        shape((UNITS,), jnp.int32),
        (doc_lists, doc_place, use),
        [SMEM] * 3,
        out_specs=SMEM,
        scratch=[pltpu.SMEM((NX * NZ,), jnp.int32)],
    )
    mine, units, ahead, far, behind = lax.optimization_barrier((mine, units, ahead, far, behind))
    other = lax.ppermute(mine, "core", [(0, 1), (1, 0)])
    gain = norm_gain.astype(F32).reshape(8, 1, 512)
    normed = call(
        norm_kernel,
        shape((8, ROWS, 512), BF16),
        (mine, other, gain),
        [VMEM] * 3,
        flops=ROWS * 4096 * 8,
        moved=8 << 20,
    )
    sends = call(
        project_kernel,
        [shape((ROWS + HALF, HEAD), BF16)] * NX,
        (normed, near, ahead, far, behind),
        [VMEM] * 5,
        out_specs=[VMEM] * NX,
        scratch=[pltpu.VMEM((4096, 2 * HEAD), BF16), pltpu.VMEM((ROWS, HEAD), F32)],
        flops=2 * ROWS * 4096 * 256,
        moved=8 << 20,
    )
    got = {
        k: lax.ppermute(sends[k], "x", [(i, (i + k) % NX) for i in range(NX)]) for k in (2, 1, 3)
    }
    got = [sends[0], got[1], got[2], got[3]]
    scratch = [
        pltpu.VMEM((8, COLS), F32),
        pltpu.VMEM((2 * NZ, SEQ, HEAD), BF16),
        pltpu.VMEM((NX, ROWS + HALF, HEAD), BF16),
        pltpu.SemaphoreType.DMA,
    ]
    stats = call(
        stats_kernel,
        shape((NX, 8, COLS), F32),
        (units, *got, docs),
        [SMEM] + [VMEM] * 4 + [ANY],
        scratch=scratch,
        limit=52,
    )
    all_stats = exchange(stats, "x")
    partial = call(
        values_kernel,
        shape((NX, HEAD, COLS), F32),
        (units, *got, docs, all_stats),
        [SMEM] + [VMEM] * 6,
        scratch=[scratch[0], scratch[2]],
    )
    returned = exchange(partial, "x")
    return call(finish_kernel, shape((SEQ, COLS), BF16), (returned,), [VMEM])


def solution(mesh):
    fine = Mesh(mesh.devices.reshape(4, 4, 4, 4, 2), ("x", "zh", "zl", "y", "core"))
    pairs, tensor = ("x", "zh", "zl"), ("y", "core")
    placed = (
        P(pairs, tensor),
        P(),
        P(pairs, tensor),
        P(pairs, tensor),
        P(pairs, tensor),
        P(pairs, None, tensor),
        P(),
        P(),
        P(pairs, None),
    )
    return jax.shard_map(
        shards, mesh=fine, in_specs=placed, out_specs=P(pairs, tensor), check_vma=False
    )
```

```python
import math

import jax
import jax.numpy as jnp
from jax import lax
from jax.experimental import pallas as pl
from jax.experimental.pallas import tpu as pltpu
from jax.sharding import Mesh
from jax.sharding import PartitionSpec as P

F32 = jnp.float32
BF16 = jnp.bfloat16
HEAD = 128
HALF = 64
SEQ = 128
RATIO = 4
NX = 4
NZ = 16
PICKS = 16
ROWS = NX * SEQ
COLS = RATIO * SEQ
RATE = HEAD ** (-0.5) * math.log2(math.e)
LOW = -1e30
UNITS = 128

VMEM = pl.BlockSpec(memory_space=pltpu.VMEM)
SMEM = pl.BlockSpec(memory_space=pltpu.SMEM)
ANY = pl.BlockSpec(memory_space=pl.ANY)


def call(kernel, outs, args, specs, out_specs=None, scratch=(), flops=0, moved=0, limit=24):
    return pl.pallas_call(
        kernel,
        out_shape=outs,
        in_specs=specs,
        out_specs=VMEM if out_specs is None else out_specs,
        scratch_shapes=list(scratch),
        compiler_params=pltpu.CompilerParams(vmem_limit_bytes=limit * 1024 * 1024),
        cost_estimate=pl.CostEstimate(flops=flops, bytes_accessed=moved, transcendentals=0),
    )(*args)


def side_by_side(left, right, left_at, right_at):
    left, right = left.astype(F32), right.astype(F32)
    lane = lax.broadcasted_iota(jnp.int32, left.shape, 1)
    left = pltpu.roll(left, HALF, 1) if left_at else left
    right = right if right_at else pltpu.roll(right, HALF, 1)
    return jnp.where(lane < HALF, left, right).astype(BF16)


def pack_kernel(*refs):
    sources, out, copies, done = refs[:3], refs[3], refs[4:7], refs[7]
    moves = [
        pltpu.make_async_copy(src, dst, done.at[i])
        for i, (src, dst) in enumerate(zip(sources, copies))
    ]
    for move in moves:
        move.start()
    for move in moves:
        move.wait()
    wq, wk, wv = copies
    for part in range(NX):
        src = wk if part < 2 else wv
        at = HALF * (part % 2)
        packed = side_by_side(src[0:32, :], src[32:64, :], at, at)
        for copy in range(4):
            out[part, copy, 0:64, :] = wq[:, part * HEAD : (part + 1) * HEAD]
            out[part, copy, 64:96, :] = packed


def tag_kernel(tokens, use, out, flags):
    flags[...] = jnp.zeros(flags.shape, jnp.int32)
    flags[0:2, 0:PICKS] = use[...]
    out[0:SEQ, :] = tokens[...]
    out[SEQ : SEQ + 16, :] = flags[...].astype(F32).astype(BF16)


def norm_kernel(mine, other, gain, out):
    core = lax.axis_index("core")
    for row in range(NX):
        rows = pl.ds(pl.multiple_of(lax.rem(lax.axis_index("x") + row, NX) * SEQ, SEQ), SEQ)
        total = jnp.zeros((SEQ, HEAD), F32)
        for src in (mine, other):
            for y in range(4):
                for c in range(4):
                    feats = src[row, y, 0:SEQ, c * HEAD : (c + 1) * HEAD].astype(F32)
                    total = total + feats * feats
        power = jnp.sum(total, axis=-1, keepdims=True) * (1.0 / 4096.0)
        factor = lax.rsqrt(power + 1e-05)
        for src, side in ((mine, core), (other, 1 - core)):
            for y in range(4):
                slot = 2 * y + side
                feats = src[row, y, 0:SEQ, :].astype(F32)
                out[slot, rows, :] = (feats * factor * gain[slot]).astype(BF16)


def route_kernel(lists, place, use, units, table):
    x, z = lax.axis_index("x"), lax.axis_index("zh") * 4 + lax.axis_index("zl")

    def clear(i, carry):
        table[i] = 0
        return carry

    lax.fori_loop(0, NX * NZ, clear, 0)

    def fill(i, carry):
        row, pick = i // PICKS, i % PICKS
        at = place[lists[row * NZ + z, pick]]
        owner, local = at // 2, at % 2
        step = lax.rem(row - x + NX, NX) * 2
        bits = use[step, pick] + 2 * use[step + 1, pick]
        entry = row * NZ + owner % NZ
        mine = jnp.where(owner // NZ == x, 1, 0)
        table[entry] = table[entry] + mine * bits * jnp.where(local == 1, 4, 1)
        return carry

    lax.fori_loop(0, NX * PICKS, fill, 0)

    def compact(i, count):
        bits = table[i]
        units[count + 1] = i * 16 + bits
        return count + jnp.where(bits > 0, 1, 0)

    count = lax.fori_loop(0, NX * NZ, compact, 0)
    units[0] = count
    for step in range(1, 4):
        units[count + step] = 0


def project_kernel(normed, near, ahead, far, behind, *rest):
    sends, weights, owns = rest[:NX], rest[NX], rest[NX + 1]
    for step, blocks in enumerate((near, ahead, far, behind)):
        row = lax.rem(lax.axis_index("zl") + step, 4) * HALF
        for b in range(16):
            block = blocks[b]
            base = pl.multiple_of(b * 256 + row, HALF)
            packed = block[64:96, :]
            weights[pl.ds(base, 64), 0:HEAD] = block[0:64, :]
            weights[pl.ds(base, 32), HEAD : 2 * HEAD] = packed
            weights[pl.ds(pl.multiple_of(base + 32, 32), 32), HEAD : 2 * HEAD] = pltpu.roll(
                packed.astype(F32), HALF, 1
            ).astype(BF16)
    total = jnp.zeros((ROWS, 2 * HEAD), F32)
    for slot in range(8):
        total = total + jnp.dot(
            normed[slot], weights[slot * 512 : (slot + 1) * 512, :], preferred_element_type=F32
        )
    query = total[:, 0:HEAD].astype(BF16)
    owns[...] = total[:, HEAD : 2 * HEAD]
    for step, send in enumerate(sends):
        dest = lax.rem(lax.axis_index("x") + step, NX)
        own = owns[pl.ds(pl.multiple_of(dest * SEQ, SEQ), SEQ), :]
        send[0:ROWS, :] = query
        send[ROWS : ROWS + HALF, :] = side_by_side(own[0:HALF], own[HALF:SEQ], 0, 0)


def own_part(got, first):
    a, b = got[first, ROWS : ROWS + HALF, :], got[first + 1, ROWS : ROWS + HALF, :]
    return jnp.concatenate([side_by_side(a, b, 0, 0), side_by_side(a, b, HALF, HALF)], axis=0)


def queries(got, group):
    rows = pl.ds(pl.multiple_of(group * SEQ, SEQ), SEQ)
    return jnp.concatenate([got[head, rows, :] for head in range(RATIO)], axis=0)


def scores_of(keys, query):
    return lax.dot_general(keys, query, (((1,), (1,)), ((), ())), preferred_element_type=F32)


def own_scores(got, group):
    scores = scores_of(own_part(got, 0), queries(got, group))
    key_at = lax.broadcasted_iota(jnp.int32, (SEQ, COLS), 0)
    row_at = lax.broadcasted_iota(jnp.int32, (SEQ, COLS), 1) % SEQ
    return jnp.where(row_at >= key_at, scores, LOW)


def unit_scores(code, got, docs):
    entry, bits = code // 16, code % 16
    group, owner = entry // NZ, entry % NZ
    keys = docs[pl.ds(owner * 2, 2), :, 0:HEAD].reshape(2 * SEQ, HEAD)
    scores = scores_of(keys, queries(got, group))
    second = (lax.broadcasted_iota(jnp.int32, (1, COLS), 1) % SEQ) // HALF
    parts = []
    for local in range(2):
        use_a, use_b = (bits // (4**local)) % 2, (bits // (2 * 4**local)) % 2
        keep = jnp.where(second == 0, use_a, use_b) > 0
        parts.append((scores[local * SEQ : (local + 1) * SEQ], keep))
    return group, owner, parts


def in_steps(units, unit, merge):
    def steps(width, first):
        def step(i, carry):
            for result in [unit(units[first + width * i + j]) for j in range(1, width + 1)]:
                merge(*result)
            return carry

        return step

    eights = units[0] // 8
    lax.fori_loop(0, eights, steps(8, 0), 0)
    lax.fori_loop(0, (units[0] - 8 * eights + 3) // 4, steps(4, 8 * eights), 0)


def weigh(scores, shift):
    return jnp.exp2((scores - shift) * RATE)


def in_order(pieces, got):
    for step, piece in enumerate(pieces):
        got[lax.rem(lax.axis_index("x") - step + NX, NX)] = piece[...]


def stats_kernel(units, own, one, two, three, far_docs, send, stats, docs, got, done):
    fetch = pltpu.make_async_copy(far_docs.at[:, :, 0:HEAD], docs, done)
    fetch.start()
    in_order((own, one, two, three), got)
    x = lax.axis_index("x")
    scores = own_scores(got, x)
    top = jnp.max(scores, axis=0, keepdims=True)
    stats[0:4, :] = jnp.full((4, COLS), LOW, F32)
    stats[4:8, :] = jnp.zeros((4, COLS), F32)
    stats[pl.ds(x, 1), :] = top
    stats[pl.ds(x + 4, 1), :] = jnp.sum(weigh(scores, top), axis=0, keepdims=True)

    def unit(code):
        group, _, parts = unit_scores(code, got, docs)
        tops = [jnp.where(keep, jnp.max(s, axis=0, keepdims=True), LOW) for s, keep in parts]
        top = jnp.maximum(tops[0], tops[1])
        sums = [
            jnp.sum(weigh(s, jnp.where(keep, top, -LOW)), axis=0, keepdims=True)
            for s, keep in parts
        ]
        return group, top, sums[0] + sums[1]

    def merge(group, top, part):
        before = stats[pl.ds(group, 1), :]
        new = jnp.maximum(before, top)
        old = stats[pl.ds(group + 4, 1), :] * weigh(before, new)
        stats[pl.ds(group, 1), :] = new
        stats[pl.ds(group + 4, 1), :] = old + part * weigh(top, new)

    fetch.wait()
    in_steps(units, unit, merge)
    for dest in range(NX):
        send[dest] = stats[...]


def values_kernel(units, own, one, two, three, docs, all_stats, send, total, got):
    in_order((own, one, two, three), got)
    x = lax.axis_index("x")
    tops = [all_stats[src, 0:4, :] for src in range(NX)]
    top = jnp.maximum(jnp.maximum(tops[0], tops[1]), jnp.maximum(tops[2], tops[3]))
    sums = jnp.zeros((4, COLS), F32)
    for src in range(NX):
        sums = sums + all_stats[src, 4:8, :] * weigh(tops[src], top)
    total[0:4, :] = top
    total[4:8, :] = top * RATE + jnp.log2(sums)
    send[...] = jnp.zeros(send.shape, F32)

    def apply(values, probs):
        return lax.dot_general(values, probs, (((0,), (0,)), ((), ())), preferred_element_type=F32)

    own = jnp.exp2(own_scores(got, x) * RATE - total[pl.ds(x + 4, 1), :])
    send[pl.ds(x, 1)] = apply(own_part(got, 2), own.astype(BF16))[None]

    def unit(code):
        group, owner, parts = unit_scores(code, got, docs)
        shift = total[pl.ds(group + 4, 1), :]
        probs = [
            jnp.exp2(s * RATE - jnp.where(keep, shift, -LOW)).astype(BF16) for s, keep in parts
        ]
        values = docs[pl.ds(owner * 2, 2), :, HEAD : 2 * HEAD].reshape(2 * SEQ, HEAD)
        return group, apply(values, jnp.concatenate(probs, axis=0))

    def merge(group, out):
        send[pl.ds(group, 1)] = send[pl.ds(group, 1)] + out[None]

    in_steps(units, unit, merge)


def finish_kernel(got, out):
    for head in range(RATIO):
        cols = slice(head * SEQ, (head + 1) * SEQ)
        total = (got[0, :, cols] + got[1, :, cols]) + (got[2, :, cols] + got[3, :, cols])
        out[:, cols] = total.T.astype(BF16)


def exchange(array, axes):
    return lax.all_to_all(array, axes, 0, 0, tiled=True)


def shards(tokens, norm_gain, wq, wk, wv, doc_cache, doc_lists, doc_place, block_use):
    shape = jax.ShapeDtypeStruct
    z_axes = ("zh", "zl")
    docs = lax.all_gather(doc_cache, z_axes, axis=0, tiled=True)

    sources = (wq, wk, wv)
    parts = call(
        pack_kernel,
        shape((4, 4, 96, HEAD), BF16),
        sources,
        [ANY] * 3,
        scratch=[pltpu.VMEM(a.shape, BF16) for a in sources] + [pltpu.SemaphoreType.DMA((3,))],
        limit=62,
    )
    tagged = call(
        tag_kernel,
        shape((SEQ + 16, 512), BF16),
        (tokens, block_use),
        [VMEM] * 2,
        scratch=[pltpu.VMEM((16, 512), jnp.int32)],
        flops=0,
        limit=62,
    )
    near = exchange(parts.reshape(16, 96, HEAD), ("x", "zh"))

    def from_z(array, step):
        return lax.ppermute(array, z_axes, [((i + step) % NZ, i) for i in range(NZ)])

    def from_x(array, step):
        return lax.ppermute(array, "x", [((i + step) % NX, i) for i in range(NX)])

    by_y = lax.all_gather(tagged, "y")
    mine = jnp.concatenate([by_y, from_x(by_y, 1), from_x(by_y, 2), from_x(by_y, 3)])
    mine = mine.reshape(NX, 4, SEQ + 16, 512)
    ahead = from_z(near, 1)
    behind = from_z(near, -1)
    far = from_z(ahead, 1)
    use = mine[:, 0, SEQ : SEQ + 2, 0:PICKS].astype(jnp.int32).reshape(8, PICKS)
    units = call(
        route_kernel,
        shape((UNITS,), jnp.int32),
        (doc_lists, doc_place, use),
        [SMEM] * 3,
        out_specs=SMEM,
        scratch=[pltpu.SMEM((NX * NZ,), jnp.int32)],
    )
    mine, units, ahead, far, behind = lax.optimization_barrier((mine, units, ahead, far, behind))
    other = lax.ppermute(mine, "core", [(0, 1), (1, 0)])
    gain = norm_gain.astype(F32).reshape(8, 1, 512)
    normed = call(
        norm_kernel,
        shape((8, ROWS, 512), BF16),
        (mine, other, gain),
        [VMEM] * 3,
        flops=ROWS * 4096 * 8,
        moved=8 << 20,
    )
    sends = call(
        project_kernel,
        [shape((ROWS + HALF, HEAD), BF16)] * NX,
        (normed, near, ahead, far, behind),
        [VMEM] * 5,
        out_specs=[VMEM] * NX,
        scratch=[pltpu.VMEM((4096, 2 * HEAD), BF16), pltpu.VMEM((ROWS, HEAD), F32)],
        flops=2 * ROWS * 4096 * 256,
        moved=8 << 20,
    )
    got = {
        k: lax.ppermute(sends[k], "x", [(i, (i + k) % NX) for i in range(NX)]) for k in (2, 1, 3)
    }
    got = [sends[0], got[1], got[2], got[3]]
    scratch = [
        pltpu.VMEM((8, COLS), F32),
        pltpu.VMEM((2 * NZ, SEQ, HEAD), BF16),
        pltpu.VMEM((NX, ROWS + HALF, HEAD), BF16),
        pltpu.SemaphoreType.DMA,
    ]
    stats = call(
        stats_kernel,
        shape((NX, 8, COLS), F32),
        (units, *got, docs),
        [SMEM] + [VMEM] * 4 + [ANY],
        scratch=scratch,
        limit=52,
    )
    all_stats = exchange(stats, "x")
    partial = call(
        values_kernel,
        shape((NX, HEAD, COLS), F32),
        (units, *got, docs, all_stats),
        [SMEM] + [VMEM] * 6,
        scratch=[scratch[0], scratch[2]],
    )
    returned = exchange(partial, "x")
    return call(finish_kernel, shape((SEQ, COLS), BF16), (returned,), [VMEM])


def solution(mesh):
    fine = Mesh(mesh.devices.reshape(4, 4, 4, 4, 2), ("x", "zh", "zl", "y", "core"))
    pairs, tensor = ("x", "zh", "zl"), ("y", "core")
    placed = (
        P(pairs, tensor),
        P(),
        P(pairs, tensor),
        P(pairs, tensor),
        P(pairs, tensor),
        P(pairs, None, tensor),
        P(),
        P(),
        P(pairs, None),
    )
    return jax.shard_map(
        shards, mesh=fine, in_specs=placed, out_specs=P(pairs, tensor), check_vma=False
    )
```
